32 devices in a mesh: seq: 16 (over z, y, core), row: 2 (over x).
Axes of the slice: x: 2, y: 2, z: 4, core: 2. Of those that a mesh axis runs over, the one named last changes fastest.
Arguments:
- tokens: bfloat16 [2, 8192, 768], P('row', 'seq'), may hold values from -18 to 18
- cotangent: bfloat16 [2, 8192, 768], P('row', 'seq'), may hold values from -6 to 6
- lengths: int32 [2, 4], P('row'), may hold values from 1 to 7681, 8192 in all within a row
- padding: int32 [2, 8192], P('row', 'seq'), may hold values 0 or 1
- feature_draws: float32 [12, 64, 64], replicated, may hold values from -4 to 4
- rel_bias: float32 [12, 1024], replicated, may hold values from -4 to 4
- w_qkv: bfloat16 [768, 2304], P(('seq', 'row')), may hold values from -0.21875 to 0.21875
- b_qkv: bfloat16 [2304], P(('seq', 'row')), may hold values from -1.5 to 1.5
- w_out: bfloat16 [768, 768], P(('seq', 'row')), may hold values from -1.25 to 1.25
- b_out: bfloat16 [768], P(('seq', 'row')), may hold values from -1.5 to 1.5
- gain_attn: bfloat16 [768], P(('seq', 'row')), may hold values from 0.5 to 1.5
- shift_attn: bfloat16 [768], P(('seq', 'row')), may hold values from -1.5 to 1.5
- w_up: bfloat16 [768, 3072], P(('seq', 'row')), may hold values from -0.21875 to 0.21875
- b_up: bfloat16 [3072], P(('seq', 'row')), may hold values from -1.5 to 1.5
- w_down: bfloat16 [3072, 768], P(('seq', 'row')), may hold values from -0.109375 to 0.109375
- b_down: bfloat16 [768], P(('seq', 'row')), may hold values from -1.5 to 1.5
- gain_ffn: bfloat16 [768], P(('seq', 'row')), may hold values from 0.5 to 1.5
- shift_ffn: bfloat16 [768], P(('seq', 'row')), may hold values from -1.5 to 1.5
Outputs:
- output: bfloat16 [2, 8192, 768], P('row', 'seq')
- grad_tokens: float32 [2, 8192, 768], P('row', 'seq')
- grad_rel_bias: float32 [12, 1024], replicated
- grad_qkv: float32 [768, 2304], P(('seq', 'row'))
- grad_qkv_bias: float32 [2304], P(('seq', 'row'))
- grad_out: float32 [768, 768], P(('seq', 'row'))
- grad_out_bias: float32 [768], P(('seq', 'row'))
- grad_gain_attn: float32 [768], P(('seq', 'row'))
- grad_shift_attn: float32 [768], P(('seq', 'row'))
- grad_up: float32 [768, 3072], P(('seq', 'row'))
- grad_up_bias: float32 [3072], P(('seq', 'row'))
- grad_down: float32 [3072, 768], P(('seq', 'row'))
- grad_down_bias: float32 [768], P(('seq', 'row'))
- gradient_feedforward_gain: float32 [768], P(('seq', 'row'))
- grad_shift_ffn: float32 [768], P(('seq', 'row'))
The draws below stay inside these ranges and needn't reach their ends.
Inputs may be any that keep to these rules, and one draw needn't show every extreme that they name: Each row's lengths sum to 8192, and its longest document has exactly 7681 tokens.
All inputs are finite; a program needn't handle non-finite values. No bound on the sum of `padding` on one device may be relied on, other than what follows from the above.
Results may differ from the reference program's by a relative error of at most 0.017.
Values may be sent and summed in bfloat16 or wider, within the bound.
A program may use at most 192 MiB of HBM per device.

```python
import math
import jax
import jax.numpy as jnp
import numpy as np
from jax import lax

D = 768
HEADS = 12
HEAD_DIM = 64
FEATURES = 64
FF = 3072
WIN = 1024
HALF = 512
TOK_DEV = 512
NDOC = 4
GROUPS = 2
STREAM = 8192
LONG = 7681


def draw_tokens(key, part):
    key = jax.random.fold_in(key, 11)
    key_vals = jax.random.fold_in(key, 0)
    key_pair = jax.random.fold_in(key, 2)
    shape = (GROUPS, STREAM, D)
    base = jnp.clip(jax.random.normal(key_vals, shape, jnp.float32), -6.0, 6.0)
    per_row = STREAM // TOK_DEV
    block_total = per_row * GROUPS
    col_width = D // block_total
    pairing = jax.random.permutation(key_pair, block_total).astype(jnp.int32)
    token_block = (jnp.arange(GROUPS, dtype=jnp.int32)[:, None] * per_row + jnp.arange(STREAM, dtype=jnp.int32)[None, :] // TOK_DEV).astype(jnp.int32)
    target = pairing[token_block]
    col_block = (jnp.arange(D, dtype=jnp.int32) // col_width).astype(jnp.int32)
    factor = jnp.where(col_block[None, None, :] == target[:, :, None], 3.0, 1.0).astype(jnp.float32)
    return (base * factor).astype(jnp.bfloat16)


def draw_feature_draws(key, part):
    key = jax.random.fold_in(key, 23)
    shape = (HEADS, FEATURES, HEAD_DIM)
    return jnp.clip(jax.random.normal(key, shape, jnp.float32), -4.0, 4.0)


def plant(drawn, stream_key, smallest, top_value):
    longest = drawn.shape.index(max(drawn.shape))
    spots = []
    for shift in (0, 1):
        where = [jax.random.randint(jax.random.fold_in(stream_key, axis), (), 0, length) for axis, length in enumerate(drawn.shape)]
        where[longest] = (where[longest] + shift) % drawn.shape[longest]
        spots.append(tuple(where))
    return drawn.at[spots[0]].set(smallest).at[spots[1]].set(top_value)


def block_scale(rng, dims, cuts, least, high):
    def one(position, parts):
        draws = jax.random.uniform(jax.random.fold_in(jax.random.fold_in(rng, 6), position), (parts,), jnp.float32, least / len(cuts), high / len(cuts))
        return jnp.repeat(jnp.exp(draws), dims[position] // parts).reshape((-1,) + (1,) * (len(dims) - position - 1))

    level = one(*cuts[0])
    for cut in cuts[1:]:
        level = level * one(*cut)
    return level


def profile(amount, total, limit, slope):
    portions = [(1 << 20) // math.isqrt(rank ** slope) + 1 for rank in range(2, amount + 1)]
    spare, holding = total - limit - (amount - 1), [1] * (amount - 1)
    while spare > 0:
        candidates = [i for i in range(amount - 1) if holding[i] < limit]
        whole, left = sum([portions[i] for i in candidates]), spare
        for i in candidates:
            addition = min(limit - holding[i], max(1, left * portions[i] // whole), spare)
            holding[i] = holding[i] + addition
            spare = spare - addition
    return np.array([limit] + holding)


def uneven_parts(rng, number_of, total, most, lean):
    if number_of == 2:
        one = jax.random.randint(rng, (), max(1, total - most), min(most, total - 1) + 1)
        return jnp.stack([one, total - one])
    sizes = jnp.asarray(profile(number_of, total, most, lean), jnp.int32)
    pairs = (number_of - 1) // 2
    donor, taker = sizes[1:1 + 2 * pairs:2], sizes[2:2 + 2 * pairs:2]
    margin = jnp.minimum(donor - 1, most - taker)
    passed = jax.random.randint(jax.random.fold_in(rng, 1), (pairs,), 0, 1 << 20) % (margin + 1)
    sizes = sizes.at[1:1 + 2 * pairs:2].set(donor - passed).at[2:2 + 2 * pairs:2].set(taker + passed)
    return sizes[jax.random.permutation(jax.random.fold_in(rng, 2), number_of)]


def normal_values(stream_key, shape, width, reach, shards=(), kind=jnp.bfloat16):
    loudness = block_scale(stream_key, shape, shards, -0.22, 0.18) if shards else 1.0
    array = jax.random.normal(stream_key, shape, jnp.float32) * width * loudness
    return jnp.minimum(jnp.maximum(array, -reach), reach).astype(kind)


def setup_inputs(seed: int = 0) -> dict:
    splits = jax.random.split(jax.random.key(seed), 19)
    tokens = draw_tokens(jax.random.fold_in(splits[18], 71), 0)
    cotangent = normal_values(splits[1], (GROUPS, STREAM, D), 1.0, 6.0, ((0, 2), (1, 16)))
    lengths = jax.vmap(lambda own: uneven_parts(own, NDOC, STREAM, LONG, 0))(jax.random.split(splits[2], GROUPS)).reshape((GROUPS, NDOC)).astype(jnp.int32)
    padding = plant((jax.random.randint(splits[3], (GROUPS, STREAM), 0, 8) < 7).astype(jnp.int32), jax.random.fold_in(splits[3], 1), 0, 1)
    feature_draws = draw_feature_draws(jax.random.fold_in(splits[18], 71), 0)
    rel_bias = normal_values(splits[5], (HEADS, WIN), 1.0, 4.0, (), jnp.float32)
    w_qkv = normal_values(splits[6], (D, 3 * D), D ** -0.5, 0.21875, ((0, 32),))
    b_qkv = normal_values(splits[7], (3 * D,), 0.3, 1.5, ((0, 32),))
    w_out = normal_values(splits[8], (D, D), (D // 32) ** -0.5, 1.25, ((0, 32),))
    b_out = normal_values(splits[9], (D,), 0.3, 1.5, ((0, 32),))
    gain_attn = jnp.clip(1.0 + 0.1 * jax.random.normal(splits[10], (D,), jnp.float32), 0.5, 1.5).astype(jnp.bfloat16)
    shift_attn = normal_values(splits[11], (D,), 0.3, 1.5, ((0, 32),))
    w_up = normal_values(splits[12], (D, FF), D ** -0.5, 0.21875, ((0, 32),))
    b_up = normal_values(splits[13], (FF,), 0.3, 1.5, ((0, 32),))
    w_down = normal_values(splits[14], (FF, D), FF ** -0.5, 0.109375, ((0, 32),))
    b_down = normal_values(splits[15], (D,), 0.3, 1.5, ((0, 32),))
    gain_ffn = jnp.clip(1.0 + 0.1 * jax.random.normal(splits[16], (D,), jnp.float32), 0.5, 1.5).astype(jnp.bfloat16)
    shift_ffn = normal_values(splits[17], (D,), 0.3, 1.5, ((0, 32),))
    return dict(tokens=tokens, cotangent=cotangent, lengths=lengths, padding=padding, feature_draws=feature_draws, rel_bias=rel_bias, w_qkv=w_qkv, b_qkv=b_qkv, w_out=w_out, b_out=b_out, gain_attn=gain_attn, shift_attn=shift_attn, w_up=w_up, b_up=b_up, w_down=w_down, b_down=b_down, gain_ffn=gain_ffn, shift_ffn=shift_ffn)


EPS = 1e-06
EXACT_MATMUL = lax.Precision.HIGHEST

@jax.custom_vjp
def low(v):
    return lax.optimization_barrier(v.astype(jnp.bfloat16)).astype(jnp.float32)

@jax.custom_vjp
def low_back(v):
    return v

def low_keep(v):
    return (low(v), None)

def low_pass(kept, grad):
    return (grad,)

def back_keep(v):
    return (v, None)

def back_low(kept, grad):
    return (low(grad),)
low.defvjp(low_keep, low_pass)
low_back.defvjp(back_keep, back_low)

def layer_norm(values, gain, shift):
    center = values - lax.optimization_barrier(jnp.mean(values, -1, keepdims=True))
    spread = lax.optimization_barrier(jnp.mean(center * center, -1, keepdims=True))
    return center * lax.rsqrt(spread + EPS) * gain + shift

def feature_map(heads_in, random_features):
    scaled_input = heads_in * heads_in.shape[-1] ** (-0.25)
    projected_rows = jnp.einsum('ykb,kib->yki', scaled_input, random_features, precision=EXACT_MATMUL)
    half_square = 0.5 * lax.optimization_barrier(jnp.sum(scaled_input * scaled_input, -1, keepdims=True))
    return jnp.exp(projected_rows - half_square) * random_features.shape[1] ** (-0.5)

def toeplitz(rows_in, q_block):
    head_count, window_len = rows_in.shape
    key_span = q_block + window_len
    padded = jnp.pad(rows_in, ((0, 0), (0, key_span + 1 - window_len)))
    tiled = jnp.broadcast_to(padded[:, None, :], (head_count, q_block, key_span + 1))
    tiled = tiled.reshape(head_count, q_block * (key_span + 1))
    return tiled[:, :q_block * key_span].reshape(head_count, q_block, key_span)

def document_numbers(positions, lengths_row):
    ends = jnp.cumsum(lengths_row).astype(jnp.int32)
    counted = lax.optimization_barrier(jnp.sum((positions[:, None] >= ends[None, :]).astype(jnp.int32), -1)).astype(jnp.int32)
    return jnp.where(positions < 0, -1, counted).astype(jnp.int32)

def band_mask(doc_query, doc_keys, pad_keys, half_win):
    row_count = doc_query.shape[0]
    col_count = doc_keys.shape[0]
    diagonal = jnp.arange(col_count, dtype=jnp.int32)[None, :] == jnp.arange(row_count, dtype=jnp.int32)[:, None] + half_win
    same_doc = doc_query[:, None] == doc_keys[None, :]
    return jnp.where(same_doc & ((pad_keys[None, :] == 1) | diagonal), 1.0, 0.0).astype(jnp.float32)

def reference(tokens, cotangent, lengths, padding, feature_draws, rel_bias, w_qkv, b_qkv, w_out, b_out, gain_attn, shift_attn, w_up, b_up, w_down, b_down, gain_ffn, shift_ffn):
    q_block = min(512, STREAM)
    block_count = STREAM // q_block
    key_span = q_block + WIN
    tail_rows = min(4096, STREAM)
    starts = jnp.arange(block_count, dtype=jnp.int32) * q_block
    positions = jnp.arange(STREAM, dtype=jnp.int32)

    def forward(token_f, rel_f, qkv_w, qkv_b, out_w, out_b, first_norm_gain, shift_one, up_w, up_b, down_w, down_b, gain_two, shift_two):
        coef = toeplitz(jnp.exp(rel_f), q_block)

        def one_row(row_in):
            row_x, row_len, row_pad = row_in
            docs = document_numbers(positions, row_len)
            proj = low_back(jnp.dot(row_x, qkv_w, precision=EXACT_MATMUL) + qkv_b)
            queries = proj[:, :D].reshape(STREAM, HEADS, HEAD_DIM)
            keys_in = proj[:, D:2 * D].reshape(STREAM, HEADS, HEAD_DIM)
            q_feat = low(feature_map(queries, feature_draws))
            k_feat = low(feature_map(keys_in, feature_draws))
            values = low(proj[:, 2 * D:]).reshape(STREAM, HEADS, HEAD_DIM)
            k_ext = jnp.pad(k_feat, ((HALF, HALF), (0, 0), (0, 0)))
            v_ext = jnp.pad(values, ((HALF, HALF), (0, 0), (0, 0)))
            doc_ext = jnp.pad(docs, (HALF, HALF), constant_values=-1)
            pad_ext = jnp.pad(row_pad, (HALF, HALF))

            def attend(start):
                fq_blk = lax.dynamic_slice_in_dim(q_feat, start, q_block, 0)
                keys_w = lax.dynamic_slice_in_dim(k_ext, start, key_span, 0)
                values_w = lax.dynamic_slice_in_dim(v_ext, start, key_span, 0)
                mask = band_mask(lax.dynamic_slice_in_dim(docs, start, q_block, 0), lax.dynamic_slice_in_dim(doc_ext, start, key_span, 0), lax.dynamic_slice_in_dim(pad_ext, start, key_span, 0), HALF)
                score = low_back(jnp.einsum('qhm,khm->hqk', fq_blk, keys_w, precision=EXACT_MATMUL))
                weight = score * coef * mask[None]
                totals = lax.optimization_barrier(jnp.sum(weight, -1))
                weighted = low_back(jnp.einsum('hqk,khd->qhd', low(weight), values_w, precision=EXACT_MATMUL))
                return weighted / totals.T[:, :, None]
            attended = low(lax.map(jax.checkpoint(attend), starts).reshape(STREAM, D))
            branch = low_back(jnp.dot(attended, out_w, precision=EXACT_MATMUL) + out_b)
            hidden = layer_norm(row_x + branch, first_norm_gain, shift_one)

            def tail(hidden_blk):
                inner = low_back(jnp.dot(low(hidden_blk), up_w, precision=EXACT_MATMUL) + up_b)
                active = low(jax.nn.gelu(inner, approximate=False))
                ffn_out = low_back(jnp.dot(active, down_w, precision=EXACT_MATMUL) + down_b)
                return layer_norm(hidden_blk + ffn_out, gain_two, shift_two)
            pieces = hidden.reshape(STREAM // tail_rows, tail_rows, D)
            return lax.map(jax.checkpoint(tail), pieces).reshape(STREAM, D)
        return lax.map(jax.checkpoint(one_row), (token_f, lengths, padding))
    primal, pullback = jax.vjp(forward, tokens.astype(jnp.float32), rel_bias, w_qkv.astype(jnp.float32), b_qkv.astype(jnp.float32), w_out.astype(jnp.float32), b_out.astype(jnp.float32), gain_attn.astype(jnp.float32), shift_attn.astype(jnp.float32), w_up.astype(jnp.float32), b_up.astype(jnp.float32), w_down.astype(jnp.float32), b_down.astype(jnp.float32), gain_ffn.astype(jnp.float32), shift_ffn.astype(jnp.float32))
    grads = pullback(cotangent.astype(jnp.float32))
    return (primal.astype(jnp.bfloat16), grads[0], grads[1], grads[2], grads[3], grads[4], grads[5], grads[6], grads[7], grads[8], grads[9], grads[10], grads[11], grads[12], grads[13])
```

```python
from functools import partial

import functools
import jax
import jax.numpy as jnp
from jax import lax
from jax.experimental import pallas as pl
from jax.experimental.pallas import tpu as pltpu
from jax.sharding import PartitionSpec as P

F32, BF16 = jnp.float32, jnp.bfloat16
NT = (((1,), (1,)), ((), ()))
TN = (((0,), (0,)), ((), ()))
SB = 128

def dot(a, b, dims=None):
    if dims is None:
        return jnp.dot(a, b, preferred_element_type=F32)
    return lax.dot_general(a, b, dims, preferred_element_type=F32)

def toep(row, width):
    win = row.shape[1]
    wide = jnp.concatenate([row, jnp.zeros((1, width - win), F32)], 1)
    return pltpu.roll(jnp.broadcast_to(wide, (SB, width)), 0, 1, stride=1, stride_axis=0)

def unskew(p, win):
    rows = p.shape[0]; width = p.shape[1]
    while rows > 8:
        rows //= 2
        p = p[:rows] + pltpu.roll(p[rows:], width - rows, 1)
    r = lax.broadcasted_iota(jnp.int32, (8, 1), 0)
    for s in (1, 2, 4):
        p = jnp.where((r & s) != 0, pltpu.roll(p, width - s, 1), p)
    return jnp.sum(p, 0, keepdims=True)[:, :win]

def fill_mask(mask_s, dq_ref, dk_ref, pk_ref, span, half):
    S = mask_s.shape[0]
    for a in range(S // SB):
        dq = dq_ref[a*SB:(a+1)*SB, :]
        dk = dk_ref[:, a*SB:a*SB+span]
        pk = pk_ref[:, a*SB:a*SB+span]
        r = lax.broadcasted_iota(jnp.int32, (SB, span), 0)
        c = lax.broadcasted_iota(jnp.int32, (SB, span), 1)
        ok = (dq == dk) & ((pk == 1) | (c == r + half))
        mask_s[a*SB:(a+1)*SB, :] = jnp.where(ok, 1.0, 0.0)

def halves(x):
    lane = lax.broadcasted_iota(jnp.int32, x.shape, 1)
    z = jnp.zeros_like(x)
    return jnp.where(lane < 64, x, z), jnp.where(lane >= 64, x, z)

def pick(a, b):
    lane = lax.broadcasted_iota(jnp.int32, a.shape, 1)
    return jnp.where(lane < 64, a, b)

def fwd_kernel(CH, dq_ref, dk_ref, pk_ref, bias_ref, q_ref, k_ref, v_ref, att_ref, inv_ref, mask_s, t_s, w_s, v_s):
    S = q_ref.shape[0]; win = bias_ref.shape[1]; span = win + SB
    p = pl.program_id(0)
    @pl.when(p == 0)
    def _():
        fill_mask(mask_s, dq_ref, dk_ref, pk_ref, span, win // 2)
        v_s[:, 128:] = jnp.ones((v_s.shape[0], 128), BF16)
    rows = jnp.exp(bias_ref[pl.ds(pl.multiple_of(p * 8, 8), 8), :])
    for i in range(2):
        t_s[i*SB:(i+1)*SB, :] = toep(rows[i:i+1], span)
    v_s[:, :128] = v_ref[...]
    for a in range(S // SB):
        qa, qb = halves(q_ref[a*SB:(a+1)*SB, :])
        qq = jnp.concatenate([qa, qb], 0)
        for c in range(0, span, CH):
            s = dot(qq, k_ref[a*SB+c:a*SB+c+CH, :], NT)
            m = mask_s[a*SB:(a+1)*SB, c:c+CH]
            t = t_s[:, c:c+CH]
            w_s[:SB, c:c+CH] = (s[:SB] * (t[:SB] * m)).astype(BF16)
            w_s[SB:, c:c+CH] = (s[SB:] * (t[SB:] * m)).astype(BF16)
        o = dot(w_s[...], v_s[a*SB:a*SB+span, :])
        inv = 1.0 / pick(o[:SB, 128:], o[SB:, 128:])
        att_ref[a*SB:(a+1)*SB, :] = pick(o[:SB, :128], o[SB:, :128]) * inv
        inv_ref[a*SB:(a+1)*SB, :] = inv

def bias_rows(rel_bias):
    h, w = rel_bias.shape
    x = rel_bias.reshape(h // 2, 2, w)
    return jnp.pad(x, ((0, 0), (0, 6), (0, 0))).reshape(h // 2 * 8, w)

def attn_fwd(dq, dk, pk, bias8, q, k, v, CH=384):
    S, D = q.shape; KS = k.shape[0]; win = bias8.shape[1]; span = win + SB
    full = lambda *s: pl.BlockSpec(s, lambda p: (0,) * len(s))
    col = lambda n: pl.BlockSpec((n, 128), lambda p: (0, p))
    return pl.pallas_call(
        functools.partial(fwd_kernel, CH),
        grid=(D // 128,),
        out_shape=(jax.ShapeDtypeStruct((S, D), F32), jax.ShapeDtypeStruct((S, D), F32)),
        in_specs=[full(S, 1), full(1, KS), full(1, KS), full(*bias8.shape), col(S), col(KS), col(KS)],
        out_specs=(col(S), col(S)),
        scratch_shapes=[pltpu.VMEM((S, span), F32), pltpu.VMEM((2*SB, span), F32), pltpu.VMEM((2*SB, span), BF16), pltpu.VMEM((KS, 256), BF16)],
        compiler_params=pltpu.CompilerParams(vmem_limit_bytes=48 << 20),
        name="attn_fwd",
    )(dq, dk, pk, bias8, q, k, v)

def bwd_kernel(CH, dq_ref, dk_ref, pk_ref, bias_ref, q_ref, k_ref, v_ref, att_ref, inv_ref, ga_ref,
               gq_ref, gk_ref, gv_ref, gb_ref, mask_s, t_s, w_s, gs_s, p_s, v_s, gk_s, gv_s):
    S = q_ref.shape[0]; win = bias_ref.shape[1]; span = win + SB
    p = pl.program_id(0)
    @pl.when(p == 0)
    def _():
        fill_mask(mask_s, dq_ref, dk_ref, pk_ref, span, win // 2)
        v_s[:, 128:] = jnp.ones((v_s.shape[0], 128), BF16)
    rows = jnp.exp(bias_ref[pl.ds(pl.multiple_of(p * 8, 8), 8), :])
    for i in range(2):
        t_s[i*SB:(i+1)*SB, :] = toep(rows[i:i+1], span)
    v_s[:, :128] = v_ref[...]
    gk_s[...] = jnp.zeros_like(gk_s)
    gv_s[...] = jnp.zeros_like(gv_s)
    for a in range(S // SB):
        rs = slice(a*SB, (a+1)*SB)
        qa, qb = halves(q_ref[rs, :])
        qq = jnp.concatenate([qa, qb], 0)
        ga = ga_ref[rs, :]
        inv = inv_ref[rs, :]
        gw = (ga * inv).astype(BF16)
        gwa, gwb = halves(gw)
        pr = ga * att_ref[rs, :] * inv
        pa, pb = halves(pr)
        lane = lax.broadcasted_iota(jnp.int32, (SB, 128), 1)
        def ext(x):
            g = -jnp.sum(x, 1, keepdims=True)
            hi = g.astype(BF16)
            lo = (g - hi.astype(F32)).astype(BF16)
            z = jnp.zeros((SB, 128), BF16)
            return jnp.where(lane == 0, hi, jnp.where(lane == 1, lo, z))
        gg = jnp.concatenate([jnp.concatenate([gwa, ext(pa)], 1), jnp.concatenate([gwb, ext(pb)], 1)], 0)
        for c in range(0, span, CH):
            s = dot(qq, k_ref[a*SB+c:a*SB+c+CH, :], NT)
            g = dot(gg, v_s[a*SB+c:a*SB+c+CH, :], NT)
            m = mask_s[rs, c:c+CH]
            for h in range(2):
                hs = slice(h*SB, (h+1)*SB)
                cm = t_s[hs, c:c+CH] * m
                w = s[hs] * cm
                w_s[hs, c:c+CH] = w.astype(BF16)
                gs_s[hs, c:c+CH] = (g[hs] * cm).astype(BF16)
                pw = g[hs] * w
                if a == 0:
                    p_s[hs, c:c+CH] = pw
                else:
                    p_s[hs, c:c+CH] += pw
        gq = dot(gs_s[...], k_ref[a*SB:a*SB+span, :])
        gq_ref[rs, :] = pick(gq[:SB], gq[SB:])
        gk_s[:, a*SB:a*SB+span] += dot(qq, gs_s[...], TN)
        gwq = jnp.concatenate([gwa, gwb], 0)
        gv_s[:, a*SB:a*SB+span] += dot(gwq, w_s[...], TN)
    gk_ref[...] = gk_s[...].T
    gv_ref[...] = gv_s[...].T
    gb_ref[...] = jnp.concatenate([unskew(p_s[:SB, :], win), unskew(p_s[SB:, :], win), jnp.zeros((6, win), F32)], 0)

def attn_bwd(dq, dk, pk, bias8, q, k, v, att, inv, ga, CH=384):
    S, D = q.shape; KS = k.shape[0]; win = bias8.shape[1]; span = win + SB
    full = lambda *s: pl.BlockSpec(s, lambda p: (0,) * len(s))
    col = lambda n: pl.BlockSpec((n, 128), lambda p: (0, p))
    V = pltpu.VMEM
    return pl.pallas_call(
        functools.partial(bwd_kernel, CH),
        grid=(D // 128,),
        out_shape=(jax.ShapeDtypeStruct((S, D), F32), jax.ShapeDtypeStruct((KS, D), F32), jax.ShapeDtypeStruct((KS, D), F32),
                   jax.ShapeDtypeStruct(bias8.shape, F32)),
        in_specs=[full(S, 1), full(1, KS), full(1, KS), full(*bias8.shape), col(S), col(KS), col(KS), col(S), col(S), col(S)],
        out_specs=(col(S), col(KS), col(KS), pl.BlockSpec((8, win), lambda p: (p, 0))),
        scratch_shapes=[V((S, span), F32), V((2*SB, span), F32), V((2*SB, span), BF16), V((2*SB, span), BF16), V((2*SB, span), F32),
                        V((KS, 256), BF16), V((128, KS), F32), V((128, KS), F32)],
        compiler_params=pltpu.CompilerParams(vmem_limit_bytes=56 << 20),
        name="attn_bwd",
    )(dq, dk, pk, bias8, q, k, v, att, inv, ga)


EPS = 1e-06
EXACT_MATMUL = lax.Precision.HIGHEST


def padded_2(cells, sides, width):
    for axis, dim in sides:
        count = lax.axis_size(axis)
        ends = count - 1
        head = lax.slice_in_dim(cells, 0, width, axis=dim)
        tail = lax.slice_in_dim(cells, cells.shape[dim] - width, cells.shape[dim], axis=dim)
        cells = jnp.concatenate(
            [
                lax.ppermute(tail, axis, [(i, (i + 1) % count) for i in range(ends)]),
                cells,
                lax.ppermute(head, axis, [((i + 1) % count, i) for i in range(ends)]),
            ],
            axis=dim,
        )
    return cells


def passed_along(block, axis, distance):
    devices = range(lax.axis_size(axis))
    route = [(i - distance, i) for i in devices if i - distance in devices]
    return lax.ppermute(block, axis, route)


def layer_norm(values, gain, shift):
    center = values - jnp.mean(values, -1, keepdims=True)
    spread = jnp.mean(center * center, -1, keepdims=True)
    return center * lax.rsqrt(spread + EPS) * gain + shift


def feature_map(heads_in, random_features):
    scaled_input = heads_in * heads_in.shape[-1] ** (-0.25)
    projected_rows = jnp.einsum(
        "ykb,kib->yki", scaled_input, random_features, precision=EXACT_MATMUL
    )
    half_square = 0.5 * jnp.sum(scaled_input * scaled_input, -1, keepdims=True)
    return jnp.exp(projected_rows - half_square) * random_features.shape[1] ** (-0.5)


def document_numbers(positions, lengths_row):
    ends = jnp.cumsum(lengths_row)
    counted = jnp.sum((positions[:, None] >= ends[None, :]).astype(jnp.int32), -1)
    return jnp.where(positions < 0, -1, counted)


def on_device(
    tokens,
    cotangent,
    lengths,
    padding,
    feature_draws,
    rel_bias,
    w_qkv,
    b_qkv,
    w_out,
    b_out,
    gain_attn,
    shift_attn,
    w_up,
    b_up,
    w_down,
    b_down,
    gain_ffn,
    shift_ffn,
):
    local = tokens[0]
    seq_len = local.shape[0]
    model_width = local.shape[1]
    head_count = rel_bias.shape[0]
    window_len = rel_bias.shape[1]
    half_win = window_len // 2
    feat_count = feature_draws.shape[1]
    head_dim = model_width // head_count
    feat_cols = head_count * feat_count
    params = (
        lax.all_gather(w_qkv, ("seq", "row"), axis=0, tiled=True),
        lax.all_gather(b_qkv, ("seq", "row"), axis=0, tiled=True),
        lax.all_gather(w_out, ("seq", "row"), axis=0, tiled=True),
        lax.all_gather(b_out, ("seq", "row"), axis=0, tiled=True),
        lax.all_gather(gain_attn, ("seq", "row"), axis=0, tiled=True),
        lax.all_gather(shift_attn, ("seq", "row"), axis=0, tiled=True),
        lax.all_gather(w_up, ("seq", "row"), axis=0, tiled=True),
        lax.all_gather(b_up, ("seq", "row"), axis=0, tiled=True),
        lax.all_gather(w_down, ("seq", "row"), axis=0, tiled=True),
        lax.all_gather(b_down, ("seq", "row"), axis=0, tiled=True),
        lax.all_gather(gain_ffn, ("seq", "row"), axis=0, tiled=True),
        lax.all_gather(shift_ffn, ("seq", "row"), axis=0, tiled=True),
    )
    (
        qkv_w,
        qkv_b,
        out_w,
        out_b,
        first_norm_gain,
        shift_one,
        up_w,
        up_b,
        down_w,
        down_b,
        gain_two,
        shift_two,
    ) = params
    seq_pos = lax.axis_index("seq")
    start_pos = seq_pos * seq_len
    positions = start_pos + jnp.arange(seq_len, dtype=jnp.int32)
    ext_pos = start_pos - half_win + jnp.arange(seq_len + window_len, dtype=jnp.int32)
    doc_query = document_numbers(positions, lengths[0])
    doc_keys = document_numbers(ext_pos, lengths[0])
    pad_local = padding[0]
    pad_ones = jnp.ones((half_win,), jnp.int32)
    pad_keys = jnp.concatenate([pad_ones, pad_local, pad_ones])
    proj_qkv = jnp.dot(local, qkv_w, preferred_element_type=jnp.float32) + qkv_b
    queries = proj_qkv[:, :model_width].reshape(seq_len, head_count, head_dim)
    keys_in = proj_qkv[:, model_width : 2 * model_width].reshape(seq_len, head_count, head_dim)
    q_full, query_back = jax.vjp(partial(feature_map, random_features=feature_draws), queries)
    k_full, key_back = jax.vjp(partial(feature_map, random_features=feature_draws), keys_in)
    q_feat = q_full.astype(jnp.bfloat16)
    k_flat = k_full.astype(jnp.bfloat16).reshape(seq_len, feat_cols)
    values_low = proj_qkv[:, 2 * model_width :].astype(jnp.bfloat16)
    own_keys = jnp.concatenate([k_flat, values_low], 1)
    masked_keys = jnp.concatenate([k_flat * pad_local.astype(jnp.bfloat16)[:, None], values_low], 1)
    rims = padded_2(masked_keys, (("seq", 0),), half_win)
    key_ext = jnp.concatenate([rims[:half_win], own_keys, rims[half_win + seq_len :]], 0)

    dq, dk, pk = doc_query[:, None], doc_keys[None, :], pad_keys[None, :]
    bias8 = bias_rows(rel_bias)
    q_low = q_feat.reshape(seq_len, feat_cols)
    keys_x, vals_x = key_ext[:, :feat_cols], key_ext[:, feat_cols:]
    attended, inv_tot = attn_fwd(dq, dk, pk, bias8, q_low, keys_x, vals_x)
    att_low = attended.astype(jnp.bfloat16)
    branch = jnp.dot(att_low, out_w, preferred_element_type=jnp.float32) + out_b
    resid_one = local.astype(jnp.float32) + branch
    hidden_one, ln_one_back = jax.vjp(
        layer_norm, resid_one, first_norm_gain.astype(jnp.float32), shift_one.astype(jnp.float32)
    )
    hidden_low = hidden_one.astype(jnp.bfloat16)
    inner = jnp.dot(hidden_low, up_w, preferred_element_type=jnp.float32) + up_b
    active, gelu_back = jax.vjp(partial(jax.nn.gelu, approximate=False), inner)
    active_low = active.astype(jnp.bfloat16)
    ffn_out = jnp.dot(active_low, down_w, preferred_element_type=jnp.float32) + down_b
    result, ln_two_back = jax.vjp(
        layer_norm,
        hidden_one + ffn_out,
        gain_two.astype(jnp.float32),
        shift_two.astype(jnp.float32),
    )
    params = (
        lax.all_gather(w_qkv, ("seq", "row"), axis=0, tiled=True),
        lax.all_gather(b_qkv, ("seq", "row"), axis=0, tiled=True),
        lax.all_gather(w_out, ("seq", "row"), axis=0, tiled=True),
        lax.all_gather(b_out, ("seq", "row"), axis=0, tiled=True),
        lax.all_gather(gain_attn, ("seq", "row"), axis=0, tiled=True),
        lax.all_gather(shift_attn, ("seq", "row"), axis=0, tiled=True),
        lax.all_gather(w_up, ("seq", "row"), axis=0, tiled=True),
        lax.all_gather(b_up, ("seq", "row"), axis=0, tiled=True),
        lax.all_gather(w_down, ("seq", "row"), axis=0, tiled=True),
        lax.all_gather(b_down, ("seq", "row"), axis=0, tiled=True),
        lax.all_gather(gain_ffn, ("seq", "row"), axis=0, tiled=True),
        lax.all_gather(shift_ffn, ("seq", "row"), axis=0, tiled=True),
    )
    (
        qkv_w,
        qkv_b,
        out_w,
        out_b,
        first_norm_gain,
        shift_one,
        up_w,
        up_b,
        down_w,
        down_b,
        gain_two,
        shift_two,
    ) = params
    grad_two, grad_gain_two, grad_shift_two = ln_two_back(cotangent[0].astype(jnp.float32))
    grad_two_low = grad_two.astype(jnp.bfloat16)
    grad_down_w = jnp.einsum(
        "ti,tj->ij", active_low, grad_two_low, preferred_element_type=jnp.float32
    )
    grad_down_b = jnp.sum(grad_two_low, 0, dtype=jnp.float32)
    grad_active = jnp.dot(grad_two_low, down_w.T, preferred_element_type=jnp.float32)
    grad_inner_low = gelu_back(grad_active)[0].astype(jnp.bfloat16)
    grad_up_w = jnp.einsum(
        "ti,tj->ij", hidden_low, grad_inner_low, preferred_element_type=jnp.float32
    )
    grad_up_b = jnp.sum(grad_inner_low, 0, dtype=jnp.float32)
    grad_hidden = grad_two + jnp.dot(grad_inner_low, up_w.T, preferred_element_type=jnp.float32)
    grad_one, grad_gain_one, grad_shift_one = ln_one_back(grad_hidden)
    grad_one_low = grad_one.astype(jnp.bfloat16)
    grad_out_w = jnp.einsum("ti,tj->ij", att_low, grad_one_low, preferred_element_type=jnp.float32)
    grad_out_b = jnp.sum(grad_one_low, 0, dtype=jnp.float32)
    grad_att = jnp.dot(grad_one_low, out_w.T, preferred_element_type=jnp.float32)
    grad_fq_all, grad_kf, grad_vv, grad_b8 = attn_bwd(
        dq, dk, pk, bias8, q_low, keys_x, vals_x, attended, inv_tot, grad_att
    )
    grad_bias = grad_b8.reshape(head_count // 2, 8, window_len)[:, :2].reshape(head_count, window_len)
    lower_rim = jnp.concatenate([grad_kf[:half_win], grad_vv[:half_win]], 1)
    upper_rim = jnp.concatenate([grad_kf[half_win + seq_len :], grad_vv[half_win + seq_len :]], 1)
    from_right = passed_along(lower_rim.astype(jnp.bfloat16), "seq", -1).astype(lower_rim.dtype)
    from_left = passed_along(upper_rim.astype(jnp.bfloat16), "seq", 1).astype(upper_rim.dtype)
    returned = from_left + from_right
    pad_float = pad_local.astype(jnp.float32)[:, None]
    grad_kfeat = grad_kf[half_win : half_win + seq_len] + returned[:, :feat_cols] * pad_float
    value_gradient = grad_vv[half_win : half_win + seq_len] + returned[:, feat_cols:]
    grad_queries = query_back(grad_fq_all.reshape(seq_len, head_count, feat_count))[0]
    grad_keys_in = key_back(grad_kfeat.reshape(seq_len, head_count, feat_count))[0]
    grad_proj_low = jnp.concatenate(
        [
            grad_queries.reshape(seq_len, model_width),
            grad_keys_in.reshape(seq_len, model_width),
            value_gradient,
        ],
        1,
    ).astype(jnp.bfloat16)
    grad_qkv_w = jnp.einsum("ti,tj->ij", local, grad_proj_low, preferred_element_type=jnp.float32)
    grad_qkv_b = jnp.sum(grad_proj_low, 0, dtype=jnp.float32)
    grad_input = grad_one + jnp.dot(grad_proj_low, qkv_w.T, preferred_element_type=jnp.float32)
    grad_rel = lax.psum(grad_bias, ("seq", "row"))
    summed = (
        lax.psum_scatter(grad_qkv_w, ("seq", "row"), scatter_dimension=0, tiled=True),
        lax.psum_scatter(grad_qkv_b, ("seq", "row"), scatter_dimension=0, tiled=True),
        lax.psum_scatter(grad_out_w, ("seq", "row"), scatter_dimension=0, tiled=True),
        lax.psum_scatter(grad_out_b, ("seq", "row"), scatter_dimension=0, tiled=True),
        lax.psum_scatter(grad_gain_one, ("seq", "row"), scatter_dimension=0, tiled=True),
        lax.psum_scatter(grad_shift_one, ("seq", "row"), scatter_dimension=0, tiled=True),
        lax.psum_scatter(grad_up_w, ("seq", "row"), scatter_dimension=0, tiled=True),
        lax.psum_scatter(grad_up_b, ("seq", "row"), scatter_dimension=0, tiled=True),
        lax.psum_scatter(grad_down_w, ("seq", "row"), scatter_dimension=0, tiled=True),
        lax.psum_scatter(grad_down_b, ("seq", "row"), scatter_dimension=0, tiled=True),
        lax.psum_scatter(grad_gain_two, ("seq", "row"), scatter_dimension=0, tiled=True),
        lax.psum_scatter(grad_shift_two, ("seq", "row"), scatter_dimension=0, tiled=True),
    )
    return (
        result[None].astype(jnp.bfloat16),
        grad_input[None],
        grad_rel,
        summed[0],
        summed[1],
        summed[2],
        summed[3],
        summed[4],
        summed[5],
        summed[6],
        summed[7],
        summed[8],
        summed[9],
        summed[10],
        summed[11],
    )


def solution(mesh):
    in_specs = (
        P("row", "seq", None),
        P("row", "seq", None),
        P("row", None),
        P("row", "seq"),
        P(),
        P(),
        P(("seq", "row"), None),
        P(("seq", "row")),
        P(("seq", "row"), None),
        P(("seq", "row")),
        P(("seq", "row")),
        P(("seq", "row")),
        P(("seq", "row"), None),
        P(("seq", "row")),
        P(("seq", "row"), None),
        P(("seq", "row")),
        P(("seq", "row")),
        P(("seq", "row")),
    )
    out_specs = (
        P("row", "seq", None),
        P("row", "seq", None),
        P(),
        P(("seq", "row"), None),
        P(("seq", "row")),
        P(("seq", "row"), None),
        P(("seq", "row")),
        P(("seq", "row")),
        P(("seq", "row")),
        P(("seq", "row"), None),
        P(("seq", "row")),
        P(("seq", "row"), None),
        P(("seq", "row")),
        P(("seq", "row")),
        P(("seq", "row")),
    )
    return jax.shard_map(
        on_device, mesh=mesh, in_specs=in_specs, out_specs=out_specs, check_vma=False
    )
```

```python
from functools import partial

import functools
import jax
import jax.numpy as jnp
from jax import lax
from jax.experimental import pallas as pl
from jax.experimental.pallas import tpu as pltpu
from jax.sharding import PartitionSpec as P

F32, BF16 = jnp.float32, jnp.bfloat16
NT = (((1,), (1,)), ((), ()))
TN = (((0,), (0,)), ((), ()))
SB = 128

def dot(a, b, dims=None):
    if dims is None:
        return jnp.dot(a, b, preferred_element_type=F32)
    return lax.dot_general(a, b, dims, preferred_element_type=F32)

def toep(row, width):
    win = row.shape[1]
    wide = jnp.concatenate([row, jnp.zeros((1, width - win), F32)], 1)
    return pltpu.roll(jnp.broadcast_to(wide, (SB, width)), 0, 1, stride=1, stride_axis=0)

def unskew(p, win):
    rows = p.shape[0]; width = p.shape[1]
    while rows > 8:
        rows //= 2
        p = p[:rows] + pltpu.roll(p[rows:], width - rows, 1)
    r = lax.broadcasted_iota(jnp.int32, (8, 1), 0)
    for s in (1, 2, 4):
        p = jnp.where((r & s) != 0, pltpu.roll(p, width - s, 1), p)
    return jnp.sum(p, 0, keepdims=True)[:, :win]

def fill_mask(mask_s, dq_ref, dk_ref, pk_ref, span, half):
    S = mask_s.shape[0]
    for a in range(S // SB):
        dq = dq_ref[a*SB:(a+1)*SB, :]
        dk = dk_ref[:, a*SB:a*SB+span]
        pk = pk_ref[:, a*SB:a*SB+span]
        r = lax.broadcasted_iota(jnp.int32, (SB, span), 0)
        c = lax.broadcasted_iota(jnp.int32, (SB, span), 1)
        ok = (dq == dk) & ((pk == 1) | (c == r + half))
        mask_s[a*SB:(a+1)*SB, :] = jnp.where(ok, 1.0, 0.0)

def halves(x):
    lane = lax.broadcasted_iota(jnp.int32, x.shape, 1)
    z = jnp.zeros_like(x)
    return jnp.where(lane < 64, x, z), jnp.where(lane >= 64, x, z)

def pick(a, b):
    lane = lax.broadcasted_iota(jnp.int32, a.shape, 1)
    return jnp.where(lane < 64, a, b)

def fwd_kernel(CH, dq_ref, dk_ref, pk_ref, bias_ref, q_ref, k_ref, v_ref, att_ref, inv_ref, mask_s, t_s, w_s, v_s):
    S = q_ref.shape[0]; win = bias_ref.shape[1]; span = win + SB
    p = pl.program_id(0)
    @pl.when(p == 0)
    def _():
        fill_mask(mask_s, dq_ref, dk_ref, pk_ref, span, win // 2)
        v_s[:, 128:] = jnp.ones((v_s.shape[0], 128), BF16)
    rows = jnp.exp(bias_ref[pl.ds(pl.multiple_of(p * 8, 8), 8), :])
    for i in range(2):
        t_s[i*SB:(i+1)*SB, :] = toep(rows[i:i+1], span)
    v_s[:, :128] = v_ref[...]
    for a in range(S // SB):
        qa, qb = halves(q_ref[a*SB:(a+1)*SB, :])
        qq = jnp.concatenate([qa, qb], 0)
        for c in range(0, span, CH):
            s = dot(qq, k_ref[a*SB+c:a*SB+c+CH, :], NT)
            m = mask_s[a*SB:(a+1)*SB, c:c+CH]
            t = t_s[:, c:c+CH]
            w_s[:SB, c:c+CH] = (s[:SB] * (t[:SB] * m)).astype(BF16)
            w_s[SB:, c:c+CH] = (s[SB:] * (t[SB:] * m)).astype(BF16)
        o = dot(w_s[...], v_s[a*SB:a*SB+span, :])
        inv = 1.0 / pick(o[:SB, 128:], o[SB:, 128:])
        att_ref[a*SB:(a+1)*SB, :] = pick(o[:SB, :128], o[SB:, :128]) * inv
        inv_ref[a*SB:(a+1)*SB, :] = inv

def bias_rows(rel_bias):
    h, w = rel_bias.shape
    x = rel_bias.reshape(h // 2, 2, w)
    return jnp.pad(x, ((0, 0), (0, 6), (0, 0))).reshape(h // 2 * 8, w)

def attn_fwd(dq, dk, pk, bias8, q, k, v, CH=384):
    S, D = q.shape; KS = k.shape[0]; win = bias8.shape[1]; span = win + SB
    full = lambda *s: pl.BlockSpec(s, lambda p: (0,) * len(s))
    col = lambda n: pl.BlockSpec((n, 128), lambda p: (0, p))
    return pl.pallas_call(
        functools.partial(fwd_kernel, CH),
        grid=(D // 128,),
        out_shape=(jax.ShapeDtypeStruct((S, D), F32), jax.ShapeDtypeStruct((S, D), F32)),
        in_specs=[full(S, 1), full(1, KS), full(1, KS), full(*bias8.shape), col(S), col(KS), col(KS)],
        out_specs=(col(S), col(S)),
        scratch_shapes=[pltpu.VMEM((S, span), F32), pltpu.VMEM((2*SB, span), F32), pltpu.VMEM((2*SB, span), BF16), pltpu.VMEM((KS, 256), BF16)],
        compiler_params=pltpu.CompilerParams(vmem_limit_bytes=48 << 20),
        name="attn_fwd",
    )(dq, dk, pk, bias8, q, k, v)

def bwd_kernel(CH, dq_ref, dk_ref, pk_ref, bias_ref, q_ref, k_ref, v_ref, att_ref, inv_ref, ga_ref,
               gq_ref, gk_ref, gv_ref, gb_ref, mask_s, t_s, w_s, gs_s, p_s, v_s, gk_s, gv_s):
    S = q_ref.shape[0]; win = bias_ref.shape[1]; span = win + SB
    p = pl.program_id(0)
    @pl.when(p == 0)
    def _():
        fill_mask(mask_s, dq_ref, dk_ref, pk_ref, span, win // 2)
        v_s[:, 128:] = jnp.ones((v_s.shape[0], 128), BF16)
    rows = jnp.exp(bias_ref[pl.ds(pl.multiple_of(p * 8, 8), 8), :])
    for i in range(2):
        t_s[i*SB:(i+1)*SB, :] = toep(rows[i:i+1], span)
    v_s[:, :128] = v_ref[...]
    gk_s[...] = jnp.zeros_like(gk_s)
    gv_s[...] = jnp.zeros_like(gv_s)
    for a in range(S // SB):
        rs = slice(a*SB, (a+1)*SB)
        qa, qb = halves(q_ref[rs, :])
        qq = jnp.concatenate([qa, qb], 0)
        ga = ga_ref[rs, :]
        inv = inv_ref[rs, :]
        gw = (ga * inv).astype(BF16)
        gwa, gwb = halves(gw)
        pr = ga * att_ref[rs, :] * inv
        pa, pb = halves(pr)
        lane = lax.broadcasted_iota(jnp.int32, (SB, 128), 1)
        def ext(x):
            g = -jnp.sum(x, 1, keepdims=True)
            hi = g.astype(BF16)
            lo = (g - hi.astype(F32)).astype(BF16)
            z = jnp.zeros((SB, 128), BF16)
            return jnp.where(lane == 0, hi, jnp.where(lane == 1, lo, z))
        gg = jnp.concatenate([jnp.concatenate([gwa, ext(pa)], 1), jnp.concatenate([gwb, ext(pb)], 1)], 0)
        for c in range(0, span, CH):
            s = dot(qq, k_ref[a*SB+c:a*SB+c+CH, :], NT)
            g = dot(gg, v_s[a*SB+c:a*SB+c+CH, :], NT)
            m = mask_s[rs, c:c+CH]
            for h in range(2):
                hs = slice(h*SB, (h+1)*SB)
                cm = t_s[hs, c:c+CH] * m
                w = s[hs] * cm
                w_s[hs, c:c+CH] = w.astype(BF16)
                gs_s[hs, c:c+CH] = (g[hs] * cm).astype(BF16)
                pw = g[hs] * w
                if a == 0:
                    p_s[hs, c:c+CH] = pw
                else:
                    p_s[hs, c:c+CH] += pw
        gq = dot(gs_s[...], k_ref[a*SB:a*SB+span, :])
        gq_ref[rs, :] = pick(gq[:SB], gq[SB:])
        gk_s[:, a*SB:a*SB+span] += dot(qq, gs_s[...], TN)
        gwq = jnp.concatenate([gwa, gwb], 0)
        gv_s[:, a*SB:a*SB+span] += dot(gwq, w_s[...], TN)
    gk_ref[...] = gk_s[...].T
    gv_ref[...] = gv_s[...].T
    gb_ref[...] = jnp.concatenate([unskew(p_s[:SB, :], win), unskew(p_s[SB:, :], win), jnp.zeros((6, win), F32)], 0)

def attn_bwd(dq, dk, pk, bias8, q, k, v, att, inv, ga, CH=384):
    S, D = q.shape; KS = k.shape[0]; win = bias8.shape[1]; span = win + SB
    full = lambda *s: pl.BlockSpec(s, lambda p: (0,) * len(s))
    col = lambda n: pl.BlockSpec((n, 128), lambda p: (0, p))
    V = pltpu.VMEM
    return pl.pallas_call(
        functools.partial(bwd_kernel, CH),
        grid=(D // 128,),
        out_shape=(jax.ShapeDtypeStruct((S, D), F32), jax.ShapeDtypeStruct((KS, D), F32), jax.ShapeDtypeStruct((KS, D), F32),
                   jax.ShapeDtypeStruct(bias8.shape, F32)),
        in_specs=[full(S, 1), full(1, KS), full(1, KS), full(*bias8.shape), col(S), col(KS), col(KS), col(S), col(S), col(S)],
        out_specs=(col(S), col(KS), col(KS), pl.BlockSpec((8, win), lambda p: (p, 0))),
        scratch_shapes=[V((S, span), F32), V((2*SB, span), F32), V((2*SB, span), BF16), V((2*SB, span), BF16), V((2*SB, span), F32),
                        V((KS, 256), BF16), V((128, KS), F32), V((128, KS), F32)],
        compiler_params=pltpu.CompilerParams(vmem_limit_bytes=56 << 20),
        name="attn_bwd",
    )(dq, dk, pk, bias8, q, k, v, att, inv, ga)


MESH = pl.DeviceIdType.MESH

class Place:
    def __init__(self, n_seq):
        self.Z = n_seq // 4
        s, self.x = lax.axis_index("seq"), lax.axis_index("row")
        self.s = s
        self.c, self.y, self.z = lax.rem(s, 2), lax.rem(s // 2, 2), s // 4

    def seq(self, z, y, c):
        return (z * 2 + y) * 2 + c

    def zcol(self, dz):
        return lax.rem(self.z + dz + self.Z, self.Z)

    def sibling(self):
        return (self.seq(self.z, self.y, 1 - self.c), self.x)

    def xpeer(self):
        return (self.s, 1 - self.x)

    def ypeer(self):
        return (self.seq(self.z, 1 - self.y, self.c), self.x)

    def zpeer(self, dz):
        return (self.seq(self.zcol(dz), self.y, self.c), self.x)

    def greet(self):
        b = pltpu.get_barrier_semaphore()
        peers = [self.sibling(), self.xpeer(), self.ypeer()] + [self.zpeer(d) for d in range(1, self.Z)]
        for p in peers:
            pl.semaphore_signal(b, inc=1, device_id=p, device_id_type=MESH)
        pl.semaphore_wait(b, len(peers))


def remote(src, dst, snd, rcv, dev):
    return pltpu.make_async_remote_copy(src_ref=src, dst_ref=dst, send_sem=snd, recv_sem=rcv, device_id=dev, device_id_type=MESH)


class Gather:
    def __init__(self, pl_, own, G, snd, rcv, chunks):
        self.p, self.own, self.G, self.snd, self.rcv, self.chunks = pl_, own, G, snd, rcv, chunks
        self.sent = []

    @staticmethod
    def sems(Z):
        return 9 * Z - 1

    def _copy(self, k, sem, s, x, dev, lo=None, n=None, own=False):
        r0, rows = self.chunks[k]
        lo, n = (r0, rows) if lo is None else (lo, n)
        dst = self.G.at[s, x, pl.ds(lo, n)]
        src = self.own.at[pl.ds(lo, n)] if own else dst
        return remote(src, dst, self.snd.at[k, sem], self.rcv.at[k, sem], dev)

    def _send(self, *a, **kw):
        c = self._copy(*a, **kw)
        c.start()
        self.sent.append(c)

    def halves(self, k):
        r0, rows = self.chunks[k]
        h = rows // 32 * 16
        return (r0, h), (r0 + h, rows - h)

    def begin(self, k):
        p, Z = self.p, self.p.Z
        for dz in range(1, Z):
            self._send(k, dz - 1, p.s, p.x, p.zpeer(dz), own=True)
        self._send(k, Z - 1, p.s, p.x, p.xpeer(), own=True)
        self._send(k, 2 * Z - 1, p.s, p.x, p.ypeer(), own=True)
        self._send(k, 5 * Z - 1, p.s, p.x, p.sibling(), own=True)

    def pass_z(self, k):
        p, Z = self.p, self.p.Z
        for dz in range(1, Z):
            o = p.seq(p.zcol(-dz), p.y, p.c)
            self._copy(k, dz - 1, o, p.x, p.zpeer(dz)).wait_recv()
            self._send(k, Z - 1 + dz, o, p.x, p.xpeer())
            self._send(k, 2 * Z - 1 + dz, o, p.x, p.ypeer())
            self._send(k, 5 * Z - 1 + dz, o, p.x, p.sibling())

    def pass_xy(self, k):
        p, Z = self.p, self.p.Z
        (a0, an), (b0, bn) = self.halves(k)
        for dz in range(Z):
            ox = p.seq(p.zcol(-dz), p.y, p.c)
            self._copy(k, Z - 1 + dz, ox, 1 - p.x, p.xpeer()).wait_recv()
            self._send(k, 3 * Z - 1 + dz, ox, 1 - p.x, p.ypeer(), a0, an)
            self._send(k, 6 * Z - 1 + dz, ox, 1 - p.x, p.sibling())
            oy = p.seq(p.zcol(-dz), 1 - p.y, p.c)
            self._copy(k, 2 * Z - 1 + dz, oy, p.x, p.ypeer()).wait_recv()
            self._send(k, 4 * Z - 1 + dz, oy, p.x, p.xpeer(), b0, bn)
            self._send(k, 7 * Z - 1 + dz, oy, p.x, p.sibling())

    def pass_diag(self, k):
        p, Z = self.p, self.p.Z
        (a0, an), (b0, bn) = self.halves(k)
        for dz in range(Z):
            o = p.seq(p.zcol(-dz), 1 - p.y, p.c)
            self._copy(k, 3 * Z - 1 + dz, o, 1 - p.x, p.ypeer(), a0, an).wait_recv()
            self._copy(k, 4 * Z - 1 + dz, o, 1 - p.x, p.xpeer(), b0, bn).wait_recv()
            self._send(k, 8 * Z - 1 + dz, o, 1 - p.x, p.sibling())

    def finish(self, k):
        p, Z = self.p, self.p.Z
        for t, (fy, fx) in enumerate(((0, 0), (0, 1), (1, 0), (1, 1))):
            for dz in range(Z):
                o = p.seq(p.zcol(-dz), (p.y + fy) % 2, 1 - p.c)
                self._copy(k, (5 + t) * Z - 1 + dz, o, (p.x + fx) % 2, p.sibling()).wait_recv()

    def drain(self):
        for c in self.sent:
            c.wait_send()
        self.sent = []


class Scatter:
    def __init__(self, pl_, P, R0, R1, R2, R3, out, snd, rcv, chunks):
        self.p, self.P, self.R0, self.R1, self.R2, self.R3, self.out = pl_, P, R0, R1, R2, R3, out
        self.snd, self.rcv, self.chunks = snd, rcv, chunks
        self.sent = []

    @staticmethod
    def sems(Z):
        return 6 * Z - 1

    def halves(self, k):
        r0, rows = self.chunks[k]
        h = rows // 32 * 16
        return pl.ds(r0, h), pl.ds(r0 + h, rows - h)

    def rows(self, k):
        return pl.ds(*self.chunks[k])

    def _go(self, src, dst, k, sem, dev, start):
        c = remote(src, dst, self.snd.at[k, sem], self.rcv.at[k, sem], dev)
        if start:
            c.start()
            self.sent.append(c)
        else:
            c.wait_recv()

    def order(self):
        return list(range(1, self.p.Z)) + [0]

    def _c0(self, k, dz, start):
        p = self.p
        zy = pl.ds(2 * p.zcol(dz), 2)
        r = self.rows(k)
        self._go(self.P.at[zy, 1 - p.c, :, r], self.R0.at[zy, :, r], k, dz, p.sibling(), start)

    def _c1(self, k, dz, start):
        p = self.p
        z = p.zcol(dz)
        a, b = self.halves(k)
        self._go(self.R0.at[pl.ds(2 * z, 2), 1 - p.x, a], self.R1.at[z, :, a], k, p.Z + dz, p.xpeer(), start)
        self._go(self.R0.at[2 * z + 1 - p.y, :, b], self.R1.at[z, :, b], k, 2 * p.Z + dz, p.ypeer(), start)

    def _c2(self, k, dz, start):
        p = self.p
        z = p.zcol(dz)
        a, b = self.halves(k)
        self._go(self.R1.at[z, 1 - p.y, a], self.R2.at[z, a], k, 3 * p.Z + dz, p.ypeer(), start)
        self._go(self.R1.at[z, 1 - p.x, b], self.R2.at[z, b], k, 4 * p.Z + dz, p.xpeer(), start)

    def _c3(self, k, dz, start):
        p = self.p
        self._go(self.R2.at[p.zcol(dz), self.rows(k)], self.R3.at[dz - 1, self.rows(k)], k, 5 * p.Z + dz - 1, p.zpeer(dz), start)

    def begin(self, k):
        for dz in self.order():
            self._c0(k, dz, True)

    @staticmethod
    def _add(dst, src):
        dst[...] = (dst[...].astype(F32) + src[...].astype(F32)).astype(BF16)

    def add_core(self, k):
        p, r = self.p, self.rows(k)
        for dz in self.order():
            self._c0(k, dz, False)
            z = p.zcol(dz)
            for y in range(2):
                for x in range(2):
                    self._add(self.R0.at[2 * z + y, x, r], self.P.at[2 * z + y, p.c, x, r])
            self._c1(k, dz, True)

    def add_one(self, k):
        p = self.p
        a, b = self.halves(k)
        for dz in self.order():
            self._c1(k, dz, False)
            z = p.zcol(dz)
            for i in range(2):
                self._add(self.R1.at[z, i, a], self.R0.at[2 * z + i, p.x, a])
                self._add(self.R1.at[z, i, b], self.R0.at[2 * z + p.y, i, b])
            self._c2(k, dz, True)

    def add_two(self, k):
        p = self.p
        a, b = self.halves(k)
        for dz in self.order():
            self._c2(k, dz, False)
            z = p.zcol(dz)
            self._add(self.R2.at[z, a], self.R1.at[z, p.y, a])
            self._add(self.R2.at[z, b], self.R1.at[z, p.x, b])
            if dz:
                self._c3(k, dz, True)

    def finish(self, k):
        p, r = self.p, self.rows(k)
        total = self.R2[p.z, r].astype(F32)
        for dz in range(1, p.Z):
            self._c3(k, dz, False)
            total = total + self.R3[dz - 1, r].astype(F32)
        self.out[r, :] = total

    def drain(self):
        for c in self.sent:
            c.wait_send()
        self.sent = []


class SumAll:
    def __init__(self, pl_, cur, got, snd, rcv):
        self.p, self.cur, self.got, self.snd, self.rcv = pl_, cur, got, snd, rcv
        p = pl_
        self.peers = [p.sibling(), p.xpeer(), p.ypeer()]
        d = 1
        while d < p.Z:
            up = 1 - 2 * lax.rem(p.z // d, 2)
            self.peers.append((p.seq(p.z + up * d, p.y, p.c), p.x))
            d *= 2

    @staticmethod
    def steps(Z):
        return 3 + (Z - 1).bit_length()

    def _copy(self, i):
        return remote(self.cur.at[i], self.got.at[i], self.snd.at[i], self.rcv.at[i], self.peers[i])

    def start(self, i):
        self._copy(i).start()

    def step(self, i):
        self._copy(i).wait()
        self.cur[i + 1] = self.cur[i] + self.got[i]


def gather_kernel(n_seq, chunks, own_ref, qkv_ref, out_ref, up_ref, down_ref, vec_ref, G, snd, rcv):
    p = Place(n_seq)
    p.greet()
    g = Gather(p, own_ref, G, snd, rcv, chunks)
    K = len(chunks)
    for k in range(K):
        g.begin(k)
    G[p.s, p.x] = own_ref[...]
    for k in range(K):
        g.pass_z(k)
        if k:
            g.pass_diag(k - 1)
        g.pass_xy(k)
        if k:
            g.finish(k - 1)
            unpack(g, k - 1, qkv_ref, out_ref, up_ref, down_ref, vec_ref)
    g.pass_diag(K - 1)
    g.finish(K - 1)
    unpack(g, K - 1, qkv_ref, out_ref, up_ref, down_ref, vec_ref)
    g.drain()


VEC = 16


def unpack(g, k, qkv_ref, out_ref, up_ref, down_ref, vec_ref):
    G = g.G
    n_seq = G.shape[0]
    W = G.shape[3]
    f = out_ref.shape[0] // (2 * n_seq)
    if k == 0:
        total = jnp.zeros((VEC, W), F32)
        for s in range(n_seq):
            total = total + G[s, 0, :VEC].astype(F32) + G[s, 1, :VEC].astype(F32)
        vec_ref[...] = total

    def pair(s, _):
        rows = pl.ds(pl.multiple_of(s * 2 * f, 2 * f), 2 * f)
        lo, n = g.chunks[k]
        if k == 0:
            lo, n = lo + VEC, n - VEC
        if k < 2:
            a = G[s, 0, lo:lo + n].astype(F32)
            b = G[s, 1, lo:lo + n].astype(F32)
            for j in range(n // f):
                v = jnp.concatenate([a[j * f:(j + 1) * f], b[j * f:(j + 1) * f]], 0).astype(BF16)
                if k == 0 and j < 3:
                    qkv_ref[rows, j * W:(j + 1) * W] = v
                elif k == 0:
                    out_ref[rows, :] = v
                else:
                    up_ref[rows, j * W:(j + 1) * W] = v
        else:
            for x in range(2):
                down_ref[pl.ds(pl.multiple_of(s * 2 * n + x * n, n), n), :] = G[s, x, lo:lo + n]
        return 0

    lax.fori_loop(0, n_seq, pair, 0)


def gather_all(n_seq, own, f, W):
    R = own.shape[0]
    n_dev = 2 * n_seq
    chunks = ((0, VEC + 4 * f), (VEC + 4 * f, 4 * f), (VEC + 8 * f, 4 * f))
    V = pltpu.VMEM
    vm = pl.BlockSpec(memory_space=pltpu.VMEM)
    M = Gather.sems(n_seq // 4)
    D = f * n_dev
    return pl.pallas_call(
        functools.partial(gather_kernel, n_seq, chunks),
        out_shape=(jax.ShapeDtypeStruct((D, 3 * W), BF16), jax.ShapeDtypeStruct((D, W), BF16), jax.ShapeDtypeStruct((D, 4 * W), BF16),
                   jax.ShapeDtypeStruct((4 * D, W), BF16), jax.ShapeDtypeStruct((VEC, W), F32)),
        in_specs=[vm], out_specs=(vm,) * 5,
        scratch_shapes=[V((n_seq, 2, R, W), BF16), pltpu.SemaphoreType.DMA((3, M)), pltpu.SemaphoreType.DMA((3, M))],
        compiler_params=pltpu.CompilerParams(collective_id=1, has_side_effects=True, vmem_limit_bytes=56 << 20),
        name="gather_all",
    )(own)


def scatter_kernel(n_seq, chunks, P, v_ref, out_ref, vout_ref, R0, R1, R2, R3, cur, got, snd, rcv, vsnd, vrcv):
    p = Place(n_seq)
    p.greet()
    sc = Scatter(p, P, R0, R1, R2, R3, out_ref, snd, rcv, chunks)
    K = len(chunks)
    va = SumAll(p, cur, got, vsnd, vrcv)
    n = SumAll.steps(p.Z)
    for k in range(K):
        sc.begin(k)
    cur[0] = v_ref[...]
    va.start(0)
    sc.add_core(0)
    va.step(0); va.start(1)
    for k in range(K):
        if k + 1 < K:
            sc.add_core(k + 1)
        if k == 0:
            va.step(1); va.start(2)
        sc.add_one(k)
        if k:
            sc.add_two(k - 1)
            va.step(k + 1); va.start(k + 2)
    sc.add_two(K - 1)
    va.step(K + 1)
    for i in range(K + 2, n):
        va.start(i); va.step(i)
    vout_ref[...] = cur[n]
    for k in range(K):
        sc.finish(k)
    sc.drain()


def scatter_all(n_seq, P, v, chunks):
    R, W = P.shape[-2:]
    Z = n_seq // 4
    V = pltpu.VMEM
    vm = pl.BlockSpec(memory_space=pltpu.VMEM)
    M = Scatter.sems(Z)
    n = SumAll.steps(Z)
    D = pltpu.SemaphoreType.DMA
    return pl.pallas_call(
        functools.partial(scatter_kernel, n_seq, chunks),
        out_shape=(jax.ShapeDtypeStruct((R, W), F32), jax.ShapeDtypeStruct(v.shape, F32)),
        in_specs=[vm] * 2, out_specs=(vm,) * 2,
        scratch_shapes=[V((2 * Z, 2, R, W), BF16), V((Z, 2, R, W), BF16), V((Z, R, W), BF16), V((Z - 1, R, W), BF16),
                        V((n + 1,) + v.shape, F32), V((n,) + v.shape, F32),
                        D((len(chunks), M)), D((len(chunks), M)), D((n,)), D((n,))],
        compiler_params=pltpu.CompilerParams(collective_id=2, has_side_effects=True, vmem_limit_bytes=56 << 20),
        name="scatter_all",
    )(P, v)


EPS = 1e-06
EXACT_MATMUL = lax.Precision.HIGHEST


def padded_2(cells, sides, width):
    for axis, dim in sides:
        count = lax.axis_size(axis)
        ends = count - 1
        head = lax.slice_in_dim(cells, 0, width, axis=dim)
        tail = lax.slice_in_dim(cells, cells.shape[dim] - width, cells.shape[dim], axis=dim)
        cells = jnp.concatenate(
            [
                lax.ppermute(tail, axis, [(i, (i + 1) % count) for i in range(ends)]),
                cells,
                lax.ppermute(head, axis, [((i + 1) % count, i) for i in range(ends)]),
            ],
            axis=dim,
        )
    return cells


def passed_along(block, axis, distance):
    devices = range(lax.axis_size(axis))
    route = [(i - distance, i) for i in devices if i - distance in devices]
    return lax.ppermute(block, axis, route)


def layer_norm(values, gain, shift):
    center = values - jnp.mean(values, -1, keepdims=True)
    spread = jnp.mean(center * center, -1, keepdims=True)
    return center * lax.rsqrt(spread + EPS) * gain + shift


def feature_map(heads_in, random_features):
    scaled_input = heads_in * heads_in.shape[-1] ** (-0.25)
    projected_rows = jnp.einsum(
        "ykb,kib->yki", scaled_input, random_features, precision=EXACT_MATMUL
    )
    half_square = 0.5 * jnp.sum(scaled_input * scaled_input, -1, keepdims=True)
    return jnp.exp(projected_rows - half_square) * random_features.shape[1] ** (-0.5)


def document_numbers(positions, lengths_row):
    ends = jnp.cumsum(lengths_row)
    counted = jnp.sum((positions[:, None] >= ends[None, :]).astype(jnp.int32), -1)
    return jnp.where(positions < 0, -1, counted)


def fits(n_seq, n_row, f):
    return n_row == 2 and n_seq in (8, 16) and f % 8 == 0


def gathered(weights, n_seq):
    w_qkv, b_qkv, w_out, b_out, gain_a, shift_a, w_up, b_up, w_down, b_down, gain_f, shift_f = weights
    f, W = w_out.shape
    n_dev = 2 * n_seq
    me = lax.axis_index("seq") * 2 + lax.axis_index("row")

    def placed(v):
        n = v.shape[0]
        lanes = jnp.arange(n * n_dev, dtype=jnp.int32) // n
        return jnp.where(lanes == me, jnp.tile(v, n_dev), jnp.zeros((), v.dtype)).reshape(-1, W)

    def blocks(w):
        return [w[:, j * W : (j + 1) * W] for j in range(w.shape[1] // W)]

    vecs = [placed(v) for v in (b_qkv, b_up, b_out, gain_a, shift_a, b_down, gain_f, shift_f)]
    rows = sum(v.shape[0] for v in vecs)
    pad = jnp.zeros((VEC - rows, W), BF16)
    own = jnp.concatenate(vecs + [pad] + blocks(w_qkv) + [w_out] + blocks(w_up) + [w_down], 0)
    qkv, out, up, down, vec = gather_all(n_seq, own, f, W)
    vec = vec.astype(BF16)
    return (qkv, vec[0:3].reshape(-1), out, vec[7], vec[8], vec[9], up, vec[3:7].reshape(-1), down, vec[10], vec[11], vec[12])


def scattered(grads, grad_bias, n_seq):
    qkv, b_qkv, out, b_out, gain_a, shift_a, up, b_up, down, b_down, gain_f, shift_f = grads
    W = out.shape[1]
    n_dev = 2 * n_seq
    f = out.shape[0] // n_dev
    me = lax.axis_index("seq") * 2 + lax.axis_index("row")

    def slabs(g):
        k = g.shape[1] // W
        return g.astype(BF16).reshape(n_dev, f, k, W).transpose(0, 2, 1, 3).reshape(n_dev, k * f, W)

    P_ = jnp.concatenate([down.astype(BF16).reshape(n_dev, 4 * f, W), slabs(up), slabs(qkv), slabs(out)], 1)
    P_ = P_.reshape(n_seq // 2, 2, 2, 12 * f, W)
    rel_rows = grad_bias.size // W
    v = jnp.concatenate([grad_bias.reshape(rel_rows, W), b_qkv.reshape(3, W), b_up.reshape(4, W)]
                        + [g[None] for g in (b_out, gain_a, shift_a, b_down, gain_f, shift_f)], 0)
    used = v.shape[0]
    v = jnp.pad(v, ((0, -used % 8), (0, 0)))
    chunks = ((0, 4 * f), (4 * f, 4 * f), (8 * f, 4 * f))
    o, vo = scatter_all(n_seq, P_, v, chunks)

    def cols(x, k):
        return x.reshape(k, f, W).transpose(1, 0, 2).reshape(f, k * W)

    vo, rel = vo[rel_rows:], vo[:rel_rows].reshape(grad_bias.shape)

    def mine(x, n):
        return lax.dynamic_slice(x.reshape(-1), (me * n,), (n,))

    rest = [mine(vo[7 + i], f) for i in range(6)]
    return rel, (cols(o[8 * f : 11 * f], 3), mine(vo[0:3], 3 * f), o[11 * f :], rest[0], rest[1], rest[2],
                 cols(o[4 * f : 8 * f], 4), mine(vo[3:7], 4 * f), o[: 4 * f], rest[3], rest[4], rest[5])


def on_device(
    tokens,
    cotangent,
    lengths,
    padding,
    feature_draws,
    rel_bias,
    w_qkv,
    b_qkv,
    w_out,
    b_out,
    gain_attn,
    shift_attn,
    w_up,
    b_up,
    w_down,
    b_down,
    gain_ffn,
    shift_ffn,
):
    local = tokens[0]
    seq_len = local.shape[0]
    model_width = local.shape[1]
    head_count = rel_bias.shape[0]
    window_len = rel_bias.shape[1]
    half_win = window_len // 2
    feat_count = feature_draws.shape[1]
    head_dim = model_width // head_count
    feat_cols = head_count * feat_count
    weights = (w_qkv, b_qkv, w_out, b_out, gain_attn, shift_attn, w_up, b_up, w_down, b_down, gain_ffn, shift_ffn)
    n_seq, n_row = lax.axis_size("seq"), lax.axis_size("row")
    own_kernels = fits(n_seq, n_row, w_out.shape[0])
    if own_kernels:
        params = gathered(weights, n_seq)
    else:
        params = tuple(lax.all_gather(w, ("seq", "row"), axis=0, tiled=True) for w in weights)
    (
        qkv_w,
        qkv_b,
        out_w,
        out_b,
        first_norm_gain,
        shift_one,
        up_w,
        up_b,
        down_w,
        down_b,
        gain_two,
        shift_two,
    ) = params
    seq_pos = lax.axis_index("seq")
    start_pos = seq_pos * seq_len
    positions = start_pos + jnp.arange(seq_len, dtype=jnp.int32)
    ext_pos = start_pos - half_win + jnp.arange(seq_len + window_len, dtype=jnp.int32)
    doc_query = document_numbers(positions, lengths[0])
    doc_keys = document_numbers(ext_pos, lengths[0])
    pad_local = padding[0]
    pad_ones = jnp.ones((half_win,), jnp.int32)
    pad_keys = jnp.concatenate([pad_ones, pad_local, pad_ones])
    proj_qkv = jnp.dot(local, qkv_w, preferred_element_type=jnp.float32) + qkv_b
    queries = proj_qkv[:, :model_width].reshape(seq_len, head_count, head_dim)
    keys_in = proj_qkv[:, model_width : 2 * model_width].reshape(seq_len, head_count, head_dim)
    q_full, query_back = jax.vjp(partial(feature_map, random_features=feature_draws), queries)
    k_full, key_back = jax.vjp(partial(feature_map, random_features=feature_draws), keys_in)
    q_feat = q_full.astype(jnp.bfloat16)
    k_flat = k_full.astype(jnp.bfloat16).reshape(seq_len, feat_cols)
    values_low = proj_qkv[:, 2 * model_width :].astype(jnp.bfloat16)
    own_keys = jnp.concatenate([k_flat, values_low], 1)
    masked_keys = jnp.concatenate([k_flat * pad_local.astype(jnp.bfloat16)[:, None], values_low], 1)
    rims = padded_2(masked_keys, (("seq", 0),), half_win)
    key_ext = jnp.concatenate([rims[:half_win], own_keys, rims[half_win + seq_len :]], 0)

    dq, dk, pk = doc_query[:, None], doc_keys[None, :], pad_keys[None, :]
    bias8 = bias_rows(rel_bias)
    q_low = q_feat.reshape(seq_len, feat_cols)
    keys_x, vals_x = key_ext[:, :feat_cols], key_ext[:, feat_cols:]
    attended, inv_tot = attn_fwd(dq, dk, pk, bias8, q_low, keys_x, vals_x)
    att_low = attended.astype(jnp.bfloat16)
    branch = jnp.dot(att_low, out_w, preferred_element_type=jnp.float32) + out_b
    resid_one = local.astype(jnp.float32) + branch
    hidden_one, ln_one_back = jax.vjp(
        layer_norm, resid_one, first_norm_gain.astype(jnp.float32), shift_one.astype(jnp.float32)
    )
    hidden_low = hidden_one.astype(jnp.bfloat16)
    inner = jnp.dot(hidden_low, up_w, preferred_element_type=jnp.float32) + up_b
    active, gelu_back = jax.vjp(partial(jax.nn.gelu, approximate=False), inner)
    active_low = active.astype(jnp.bfloat16)
    ffn_out = jnp.dot(active_low, down_w, preferred_element_type=jnp.float32) + down_b
    result, ln_two_back = jax.vjp(
        layer_norm,
        hidden_one + ffn_out,
        gain_two.astype(jnp.float32),
        shift_two.astype(jnp.float32),
    )
    grad_two, grad_gain_two, grad_shift_two = ln_two_back(cotangent[0].astype(jnp.float32))
    grad_two_low = grad_two.astype(jnp.bfloat16)
    grad_down_w = jnp.einsum(
        "ti,tj->ij", active_low, grad_two_low, preferred_element_type=jnp.float32
    )
    grad_down_b = jnp.sum(grad_two_low, 0, dtype=jnp.float32)
    grad_active = jnp.dot(grad_two_low, down_w.T, preferred_element_type=jnp.float32)
    grad_inner_low = gelu_back(grad_active)[0].astype(jnp.bfloat16)
    grad_up_w = jnp.einsum(
        "ti,tj->ij", hidden_low, grad_inner_low, preferred_element_type=jnp.float32
    )
    grad_up_b = jnp.sum(grad_inner_low, 0, dtype=jnp.float32)
    grad_hidden = grad_two + jnp.dot(grad_inner_low, up_w.T, preferred_element_type=jnp.float32)
    grad_one, grad_gain_one, grad_shift_one = ln_one_back(grad_hidden)
    grad_one_low = grad_one.astype(jnp.bfloat16)
    grad_out_w = jnp.einsum("ti,tj->ij", att_low, grad_one_low, preferred_element_type=jnp.float32)
    grad_out_b = jnp.sum(grad_one_low, 0, dtype=jnp.float32)
    grad_att = jnp.dot(grad_one_low, out_w.T, preferred_element_type=jnp.float32)
    grad_fq_all, grad_kf, grad_vv, grad_b8 = attn_bwd(
        dq, dk, pk, bias8, q_low, keys_x, vals_x, attended, inv_tot, grad_att
    )
    grad_bias = grad_b8.reshape(head_count // 2, 8, window_len)[:, :2].reshape(head_count, window_len)
    lower_rim = jnp.concatenate([grad_kf[:half_win], grad_vv[:half_win]], 1)
    upper_rim = jnp.concatenate([grad_kf[half_win + seq_len :], grad_vv[half_win + seq_len :]], 1)
    from_right = passed_along(lower_rim.astype(jnp.bfloat16), "seq", -1).astype(lower_rim.dtype)
    from_left = passed_along(upper_rim.astype(jnp.bfloat16), "seq", 1).astype(upper_rim.dtype)
    returned = from_left + from_right
    pad_float = pad_local.astype(jnp.float32)[:, None]
    grad_kfeat = grad_kf[half_win : half_win + seq_len] + returned[:, :feat_cols] * pad_float
    value_gradient = grad_vv[half_win : half_win + seq_len] + returned[:, feat_cols:]
    grad_queries = query_back(grad_fq_all.reshape(seq_len, head_count, feat_count))[0]
    grad_keys_in = key_back(grad_kfeat.reshape(seq_len, head_count, feat_count))[0]
    grad_proj_low = jnp.concatenate(
        [
            grad_queries.reshape(seq_len, model_width),
            grad_keys_in.reshape(seq_len, model_width),
            value_gradient,
        ],
        1,
    ).astype(jnp.bfloat16)
    grad_qkv_w = jnp.einsum("ti,tj->ij", local, grad_proj_low, preferred_element_type=jnp.float32)
    grad_qkv_b = jnp.sum(grad_proj_low, 0, dtype=jnp.float32)
    grad_input = grad_one + jnp.dot(grad_proj_low, qkv_w.T, preferred_element_type=jnp.float32)
    grads = (
        grad_qkv_w, grad_qkv_b, grad_out_w, grad_out_b, grad_gain_one, grad_shift_one,
        grad_up_w, grad_up_b, grad_down_w, grad_down_b, grad_gain_two, grad_shift_two,
    )
    if own_kernels:
        grad_rel, summed = scattered(grads, grad_bias, n_seq)
    else:
        grad_rel = lax.psum(grad_bias, ("seq", "row"))
        summed = tuple(lax.psum_scatter(g, ("seq", "row"), scatter_dimension=0, tiled=True) for g in grads)
    return (
        result[None].astype(jnp.bfloat16),
        grad_input[None],
        grad_rel,
        summed[0],
        summed[1],
        summed[2],
        summed[3],
        summed[4],
        summed[5],
        summed[6],
        summed[7],
        summed[8],
        summed[9],
        summed[10],
        summed[11],
    )


def solution(mesh):
    in_specs = (
        P("row", "seq", None),
        P("row", "seq", None),
        P("row", None),
        P("row", "seq"),
        P(),
        P(),
        P(("seq", "row"), None),
        P(("seq", "row")),
        P(("seq", "row"), None),
        P(("seq", "row")),
        P(("seq", "row")),
        P(("seq", "row")),
        P(("seq", "row"), None),
        P(("seq", "row")),
        P(("seq", "row"), None),
        P(("seq", "row")),
        P(("seq", "row")),
        P(("seq", "row")),
    )
    out_specs = (
        P("row", "seq", None),
        P("row", "seq", None),
        P(),
        P(("seq", "row"), None),
        P(("seq", "row")),
        P(("seq", "row"), None),
        P(("seq", "row")),
        P(("seq", "row")),
        P(("seq", "row")),
        P(("seq", "row"), None),
        P(("seq", "row")),
        P(("seq", "row"), None),
        P(("seq", "row")),
        P(("seq", "row")),
        P(("seq", "row")),
    )
    return jax.shard_map(
        on_device, mesh=mesh, in_specs=in_specs, out_specs=out_specs, check_vma=False
    )
```

```python
from functools import partial

import functools
import jax
import jax.numpy as jnp
from jax import lax
from jax.experimental import pallas as pl
from jax.experimental.pallas import tpu as pltpu
from jax.sharding import PartitionSpec as P

F32, BF16 = jnp.float32, jnp.bfloat16
NT = (((1,), (1,)), ((), ()))
TN = (((0,), (0,)), ((), ()))
SB = 128

def dot(a, b, dims=None):
    if dims is None:
        return jnp.dot(a, b, preferred_element_type=F32)
    return lax.dot_general(a, b, dims, preferred_element_type=F32)

def toep(row, width):
    win = row.shape[1]
    wide = jnp.concatenate([row, jnp.zeros((1, width - win), F32)], 1)
    return pltpu.roll(jnp.broadcast_to(wide, (SB, width)), 0, 1, stride=1, stride_axis=0)

def unskew(p, win):
    rows = p.shape[0]; width = p.shape[1]
    while rows > 8:
        rows //= 2
        p = p[:rows] + pltpu.roll(p[rows:], width - rows, 1)
    r = lax.broadcasted_iota(jnp.int32, (8, 1), 0)
    for s in (1, 2, 4):
        p = jnp.where((r & s) != 0, pltpu.roll(p, width - s, 1), p)
    return jnp.sum(p, 0, keepdims=True)[:, :win]

def fill_mask(mask_s, dq_ref, dk_ref, pk_ref, span, half):
    S = mask_s.shape[0]
    for a in range(S // SB):
        dq = dq_ref[a*SB:(a+1)*SB, :]
        dk = dk_ref[:, a*SB:a*SB+span]
        pk = pk_ref[:, a*SB:a*SB+span]
        r = lax.broadcasted_iota(jnp.int32, (SB, span), 0)
        c = lax.broadcasted_iota(jnp.int32, (SB, span), 1)
        ok = (dq == dk) & ((pk == 1) | (c == r + half))
        mask_s[a*SB:(a+1)*SB, :] = jnp.where(ok, 1.0, 0.0)

def halves(x):
    lane = lax.broadcasted_iota(jnp.int32, x.shape, 1)
    z = jnp.zeros_like(x)
    return jnp.where(lane < 64, x, z), jnp.where(lane >= 64, x, z)

def pick(a, b):
    lane = lax.broadcasted_iota(jnp.int32, a.shape, 1)
    return jnp.where(lane < 64, a, b)

def fwd_kernel(CH, dq_ref, dk_ref, pk_ref, bias_ref, q_ref, k_ref, v_ref, att_ref, inv_ref, mask_s, t_s, w_s, v_s):
    S = q_ref.shape[0]; win = bias_ref.shape[1]; span = win + SB
    p = pl.program_id(0)
    @pl.when(p == 0)
    def _():
        fill_mask(mask_s, dq_ref, dk_ref, pk_ref, span, win // 2)
        v_s[:, 128:] = jnp.ones((v_s.shape[0], 128), BF16)
    rows = jnp.exp(bias_ref[pl.ds(pl.multiple_of(p * 8, 8), 8), :])
    for i in range(2):
        t_s[i*SB:(i+1)*SB, :] = toep(rows[i:i+1], span)
    v_s[:, :128] = v_ref[...]
    for a in range(S // SB):
        qa, qb = halves(q_ref[a*SB:(a+1)*SB, :])
        qq = jnp.concatenate([qa, qb], 0)
        for c in range(0, span, CH):
            s = dot(qq, k_ref[a*SB+c:a*SB+c+CH, :], NT)
            m = mask_s[a*SB:(a+1)*SB, c:c+CH]
            t = t_s[:, c:c+CH]
            w_s[:SB, c:c+CH] = (s[:SB] * (t[:SB] * m)).astype(BF16)
            w_s[SB:, c:c+CH] = (s[SB:] * (t[SB:] * m)).astype(BF16)
        o = dot(w_s[...], v_s[a*SB:a*SB+span, :])
        inv = 1.0 / pick(o[:SB, 128:], o[SB:, 128:])
        att_ref[a*SB:(a+1)*SB, :] = pick(o[:SB, :128], o[SB:, :128]) * inv
        inv_ref[a*SB:(a+1)*SB, :] = inv

def bias_rows(rel_bias):
    h, w = rel_bias.shape
    x = rel_bias.reshape(h // 2, 2, w)
    return jnp.pad(x, ((0, 0), (0, 6), (0, 0))).reshape(h // 2 * 8, w)

def attn_fwd(dq, dk, pk, bias8, q, k, v, CH=384):
    S, D = q.shape; KS = k.shape[0]; win = bias8.shape[1]; span = win + SB
    full = lambda *s: pl.BlockSpec(s, lambda p: (0,) * len(s))
    col = lambda n: pl.BlockSpec((n, 128), lambda p: (0, p))
    return pl.pallas_call(
        functools.partial(fwd_kernel, CH),
        grid=(D // 128,),
        out_shape=(jax.ShapeDtypeStruct((S, D), F32), jax.ShapeDtypeStruct((S, D), F32)),
        in_specs=[full(S, 1), full(1, KS), full(1, KS), full(*bias8.shape), col(S), col(KS), col(KS)],
        out_specs=(col(S), col(S)),
        scratch_shapes=[pltpu.VMEM((S, span), F32), pltpu.VMEM((2*SB, span), F32), pltpu.VMEM((2*SB, span), BF16), pltpu.VMEM((KS, 256), BF16)],
        compiler_params=pltpu.CompilerParams(vmem_limit_bytes=48 << 20),
        name="attn_fwd",
    )(dq, dk, pk, bias8, q, k, v)

def bwd_kernel(CH, dq_ref, dk_ref, pk_ref, bias_ref, q_ref, k_ref, v_ref, att_ref, inv_ref, ga_ref,
               gq_ref, gk_ref, gv_ref, gb_ref, mask_s, t_s, w_s, gs_s, p_s, v_s, gk_s, gv_s):
    S = q_ref.shape[0]; win = bias_ref.shape[1]; span = win + SB
    p = pl.program_id(0)
    @pl.when(p == 0)
    def _():
        fill_mask(mask_s, dq_ref, dk_ref, pk_ref, span, win // 2)
        v_s[:, 128:] = jnp.ones((v_s.shape[0], 128), BF16)
    rows = jnp.exp(bias_ref[pl.ds(pl.multiple_of(p * 8, 8), 8), :])
    for i in range(2):
        t_s[i*SB:(i+1)*SB, :] = toep(rows[i:i+1], span)
    v_s[:, :128] = v_ref[...]
    gk_s[...] = jnp.zeros_like(gk_s)
    gv_s[...] = jnp.zeros_like(gv_s)
    for a in range(S // SB):
        rs = slice(a*SB, (a+1)*SB)
        qa, qb = halves(q_ref[rs, :])
        qq = jnp.concatenate([qa, qb], 0)
        ga = ga_ref[rs, :]
        inv = inv_ref[rs, :]
        gw = (ga * inv).astype(BF16)
        gwa, gwb = halves(gw)
        pr = ga * att_ref[rs, :] * inv
        pa, pb = halves(pr)
        lane = lax.broadcasted_iota(jnp.int32, (SB, 128), 1)
        def ext(x):
            g = -jnp.sum(x, 1, keepdims=True)
            hi = g.astype(BF16)
            lo = (g - hi.astype(F32)).astype(BF16)
            z = jnp.zeros((SB, 128), BF16)
            return jnp.where(lane == 0, hi, jnp.where(lane == 1, lo, z))
        gg = jnp.concatenate([jnp.concatenate([gwa, ext(pa)], 1), jnp.concatenate([gwb, ext(pb)], 1)], 0)
        for c in range(0, span, CH):
            s = dot(qq, k_ref[a*SB+c:a*SB+c+CH, :], NT)
            g = dot(gg, v_s[a*SB+c:a*SB+c+CH, :], NT)
            m = mask_s[rs, c:c+CH]
            for h in range(2):
                hs = slice(h*SB, (h+1)*SB)
                cm = t_s[hs, c:c+CH] * m
                w = s[hs] * cm
                w_s[hs, c:c+CH] = w.astype(BF16)
                gs_s[hs, c:c+CH] = (g[hs] * cm).astype(BF16)
                pw = g[hs] * w
                if a == 0:
                    p_s[hs, c:c+CH] = pw
                else:
                    p_s[hs, c:c+CH] += pw
        gq = dot(gs_s[...], k_ref[a*SB:a*SB+span, :])
        gq_ref[rs, :] = pick(gq[:SB], gq[SB:])
        gk_s[:, a*SB:a*SB+span] += dot(qq, gs_s[...], TN)
        gwq = jnp.concatenate([gwa, gwb], 0)
        gv_s[:, a*SB:a*SB+span] += dot(gwq, w_s[...], TN)
    gk_ref[...] = gk_s[...].T
    gv_ref[...] = gv_s[...].T
    gb_ref[...] = jnp.concatenate([unskew(p_s[:SB, :], win), unskew(p_s[SB:, :], win), jnp.zeros((6, win), F32)], 0)

def attn_bwd(dq, dk, pk, bias8, q, k, v, att, inv, ga, CH=384):
    S, D = q.shape; KS = k.shape[0]; win = bias8.shape[1]; span = win + SB
    full = lambda *s: pl.BlockSpec(s, lambda p: (0,) * len(s))
    col = lambda n: pl.BlockSpec((n, 128), lambda p: (0, p))
    V = pltpu.VMEM
    return pl.pallas_call(
        functools.partial(bwd_kernel, CH),
        grid=(D // 128,),
        out_shape=(jax.ShapeDtypeStruct((S, D), F32), jax.ShapeDtypeStruct((KS, D), F32), jax.ShapeDtypeStruct((KS, D), F32),
                   jax.ShapeDtypeStruct(bias8.shape, F32)),
        in_specs=[full(S, 1), full(1, KS), full(1, KS), full(*bias8.shape), col(S), col(KS), col(KS), col(S), col(S), col(S)],
        out_specs=(col(S), col(KS), col(KS), pl.BlockSpec((8, win), lambda p: (p, 0))),
        scratch_shapes=[V((S, span), F32), V((2*SB, span), F32), V((2*SB, span), BF16), V((2*SB, span), BF16), V((2*SB, span), F32),
                        V((KS, 256), BF16), V((128, KS), F32), V((128, KS), F32)],
        compiler_params=pltpu.CompilerParams(vmem_limit_bytes=56 << 20),
        name="attn_bwd",
    )(dq, dk, pk, bias8, q, k, v, att, inv, ga)


MESH = pl.DeviceIdType.MESH

class Place:
    def __init__(self, n_seq):
        self.Z = n_seq // 4
        s, self.x = lax.axis_index("seq"), lax.axis_index("row")
        self.s = s
        self.c, self.y, self.z = lax.rem(s, 2), lax.rem(s // 2, 2), s // 4

    def seq(self, z, y, c):
        return (z * 2 + y) * 2 + c

    def zcol(self, dz):
        return lax.rem(self.z + dz + self.Z, self.Z)

    def sibling(self):
        return (self.seq(self.z, self.y, 1 - self.c), self.x)

    def xpeer(self):
        return (self.s, 1 - self.x)

    def ypeer(self):
        return (self.seq(self.z, 1 - self.y, self.c), self.x)

    def zpeer(self, dz):
        return (self.seq(self.zcol(dz), self.y, self.c), self.x)

    def along(self, d):
        n = 4 * self.Z
        return (lax.rem(self.s + d + n, n), self.x)

    def greet(self):
        b = pltpu.get_barrier_semaphore()
        peers = [self.sibling(), self.xpeer(), self.ypeer(), self.along(1), self.along(-1)]
        peers += [self.zpeer(d) for d in range(1, self.Z)]
        for p in peers:
            pl.semaphore_signal(b, inc=1, device_id=p, device_id_type=MESH)
        pl.semaphore_wait(b, len(peers))


def remote(src, dst, snd, rcv, dev):
    return pltpu.make_async_remote_copy(src_ref=src, dst_ref=dst, send_sem=snd, recv_sem=rcv, device_id=dev, device_id_type=MESH)


class Gather:
    def __init__(self, pl_, own, G, snd, rcv, chunks):
        self.p, self.own, self.G, self.snd, self.rcv, self.chunks = pl_, own, G, snd, rcv, chunks
        self.sent = []

    @staticmethod
    def sems(Z):
        return 9 * Z - 1

    def _copy(self, k, sem, s, x, dev, lo=None, n=None, own=False):
        r0, rows = self.chunks[k]
        lo, n = (r0, rows) if lo is None else (lo, n)
        dst = self.G.at[s, x, pl.ds(lo, n)]
        src = self.own.at[pl.ds(lo, n)] if own else dst
        return remote(src, dst, self.snd.at[k, sem], self.rcv.at[k, sem], dev)

    def _send(self, *a, **kw):
        c = self._copy(*a, **kw)
        c.start()
        self.sent.append(c)

    def halves(self, k):
        r0, rows = self.chunks[k]
        h = rows // 32 * 16
        return (r0, h), (r0 + h, rows - h)

    def begin_z(self, k):
        p = self.p
        for dz in range(1, p.Z):
            self._send(k, dz - 1, p.s, p.x, p.zpeer(dz), own=True)

    def begin_xy(self, k):
        p, Z = self.p, self.p.Z
        self._send(k, Z - 1, p.s, p.x, p.xpeer(), own=True)
        self._send(k, 2 * Z - 1, p.s, p.x, p.ypeer(), own=True)
        self._send(k, 5 * Z - 1, p.s, p.x, p.sibling(), own=True)

    def pass_z(self, k):
        p, Z = self.p, self.p.Z
        for dz in range(1, Z):
            o = p.seq(p.zcol(-dz), p.y, p.c)
            self._copy(k, dz - 1, o, p.x, p.zpeer(dz)).wait_recv()
            self._send(k, Z - 1 + dz, o, p.x, p.xpeer())
            self._send(k, 2 * Z - 1 + dz, o, p.x, p.ypeer())
            self._send(k, 5 * Z - 1 + dz, o, p.x, p.sibling())

    def pass_xy(self, k):
        p, Z = self.p, self.p.Z
        (a0, an), (b0, bn) = self.halves(k)
        for dz in range(Z):
            ox = p.seq(p.zcol(-dz), p.y, p.c)
            self._copy(k, Z - 1 + dz, ox, 1 - p.x, p.xpeer()).wait_recv()
            self._send(k, 3 * Z - 1 + dz, ox, 1 - p.x, p.ypeer(), a0, an)
            self._send(k, 6 * Z - 1 + dz, ox, 1 - p.x, p.sibling())
            oy = p.seq(p.zcol(-dz), 1 - p.y, p.c)
            self._copy(k, 2 * Z - 1 + dz, oy, p.x, p.ypeer()).wait_recv()
            self._send(k, 4 * Z - 1 + dz, oy, p.x, p.xpeer(), b0, bn)
            self._send(k, 7 * Z - 1 + dz, oy, p.x, p.sibling())

    def pass_diag(self, k):
        p, Z = self.p, self.p.Z
        (a0, an), (b0, bn) = self.halves(k)
        for dz in range(Z):
            o = p.seq(p.zcol(-dz), 1 - p.y, p.c)
            self._copy(k, 3 * Z - 1 + dz, o, 1 - p.x, p.ypeer(), a0, an).wait_recv()
            self._copy(k, 4 * Z - 1 + dz, o, 1 - p.x, p.xpeer(), b0, bn).wait_recv()
            self._send(k, 8 * Z - 1 + dz, o, 1 - p.x, p.sibling())

    def finish(self, k):
        p, Z = self.p, self.p.Z
        for t, (fy, fx) in enumerate(((0, 0), (0, 1), (1, 0), (1, 1))):
            for dz in range(Z):
                o = p.seq(p.zcol(-dz), (p.y + fy) % 2, 1 - p.c)
                self._copy(k, (5 + t) * Z - 1 + dz, o, (p.x + fx) % 2, p.sibling()).wait_recv()

    def drain(self):
        for c in self.sent:
            c.wait_send()
        self.sent = []


class SumAll:
    def __init__(self, pl_, cur, got, snd, rcv):
        self.p, self.cur, self.got, self.snd, self.rcv = pl_, cur, got, snd, rcv
        p = pl_
        self.peers = [p.sibling(), p.xpeer(), p.ypeer()]
        d = 1
        while d < p.Z:
            up = 1 - 2 * lax.rem(p.z // d, 2)
            self.peers.append((p.seq(p.z + up * d, p.y, p.c), p.x))
            d *= 2

    @staticmethod
    def steps(Z):
        return 3 + (Z - 1).bit_length()

    def _copy(self, i):
        return remote(self.cur.at[i], self.got.at[i], self.snd.at[i], self.rcv.at[i], self.peers[i])

    def start(self, i):
        self._copy(i).start()

    def step(self, i):
        self._copy(i).wait()
        self.cur[i + 1] = self.cur[i] + self.got[i]


VEC = 16


def unpack(g, k, qkv_ref, out_ref, up_ref, down_ref, vec_ref):
    G = g.G
    n_seq = G.shape[0]
    W = G.shape[3]
    f = out_ref.shape[0] // (2 * n_seq)
    if k == 0:
        total = jnp.zeros((VEC, W), F32)
        for s in range(n_seq):
            total = total + G[s, 0, :VEC].astype(F32) + G[s, 1, :VEC].astype(F32)
        vec_ref[...] = total

    def pair(s, _):
        rows = pl.ds(pl.multiple_of(s * 2 * f, 2 * f), 2 * f)
        lo, n = g.chunks[k]
        if k == 0:
            lo, n = lo + VEC, n - VEC
        if k < 2:
            a = G[s, 0, lo:lo + n].astype(F32)
            b = G[s, 1, lo:lo + n].astype(F32)
            for j in range(n // f):
                v = jnp.concatenate([a[j * f:(j + 1) * f], b[j * f:(j + 1) * f]], 0).astype(BF16)
                if k == 0 and j < 3:
                    qkv_ref[rows, j * W:(j + 1) * W] = v
                elif k == 0:
                    out_ref[rows, :] = v
                else:
                    up_ref[rows, j * W:(j + 1) * W] = v
        else:
            for x in range(2):
                down_ref[pl.ds(pl.multiple_of(s * 2 * n + x * n, n), n), :] = G[s, x, lo:lo + n]
        return 0

    lax.fori_loop(0, n_seq, pair, 0)


def split2(x):
    hi = x.astype(BF16)
    return hi, (x - hi.astype(F32)).astype(BF16)


def phi(z, dh, dl, on, scale):
    s = z * scale
    sh, sl = split2(s)
    rows = dot(jnp.concatenate([sh, sl], 1), jnp.concatenate([dh, dh], 0)) + dot(sh, dl)
    half = dot(jnp.concatenate(split2(s * s * 0.5), 1), on)
    return jnp.exp(rows - half) * (dh.shape[1] // 2) ** -0.5


def fwd_attend(S, span, half_win, p, bias_ref, q_s, k_s, v_s, mask_s, t_s, w_s, vv_s, att_ref, inv_ref):
    lanes = pl.ds(pl.multiple_of(p * 128, 128), 128)
    CH = span // 3
    rows = jnp.exp(bias_ref[pl.ds(pl.multiple_of(p * 8, 8), 8), :])
    for i in range(2):
        t_s[i * SB:(i + 1) * SB, :] = toep(rows[i:i + 1], span)
    vv_s[:, :128] = v_s[:, lanes]
    for a in range(S // SB):
        rs = slice(a * SB, (a + 1) * SB)
        qq = jnp.concatenate(halves(q_s[rs, lanes]), 0)
        for c in range(0, span, CH):
            s = dot(qq, k_s[a * SB + c:a * SB + c + CH, lanes], NT)
            m = mask_s[rs, c:c + CH]
            for h in range(2):
                hs = slice(h * SB, (h + 1) * SB)
                w_s[hs, c:c + CH] = (s[hs] * (t_s[hs, c:c + CH] * m)).astype(BF16)
        o = dot(w_s[...], vv_s[a * SB:a * SB + span, :])
        inv = 1.0 / pick(o[:SB, 128:], o[SB:, 128:])
        att_ref[rs, lanes] = pick(o[:SB, :128], o[SB:, :128]) * inv
        inv_ref[rs, lanes] = inv


def forward_kernel(n_seq, chunks, scale, own_ref, x_ref, pad_ref, dq_ref, dk_ref, bias_ref, dh_ref, dl_ref,
               qkv_ref, out_ref, up_ref, down_ref, vec_ref, zq_ref, zk_ref, q_ref, k_ref, v_ref, att_ref, inv_ref, pk_ref,
               G, X3, P3, mask_s, t_s, w_s, vv_s, snd, rcv, hsnd, hrcv):
    S, W = x_ref.shape
    win = bias_ref.shape[1]
    span = win + SB
    p = Place(n_seq)
    p.greet()
    g = Gather(p, own_ref, G, snd, rcv, chunks)
    to_right = remote(x_ref, X3.at[pl.ds(0, S)], hsnd.at[0], hrcv.at[0], p.along(1))
    to_left = remote(x_ref, X3.at[pl.ds(2 * S, S)], hsnd.at[1], hrcv.at[1], p.along(-1))
    g.begin_xy(0)
    g.begin_z(0)
    pad_right = remote(pad_ref, P3.at[0], hsnd.at[2], hrcv.at[2], p.along(1))
    pad_left = remote(pad_ref, P3.at[2], hsnd.at[3], hrcv.at[3], p.along(-1))
    halo = (to_right, to_left, pad_right, pad_left)
    for h in halo:
        h.start()
    X3[S:2 * S, :] = x_ref[...]
    G[p.s, p.x] = own_ref[...]
    P3[1] = pad_ref[...]
    vv_s[:, 128:] = jnp.ones((vv_s.shape[0], 128), BF16)
    g.pass_z(0)
    g.begin_z(1)
    g.pass_xy(0)
    g.begin_xy(1)
    g.pass_z(1)
    g.begin_z(2)
    g.pass_diag(0)
    g.finish(0)
    unpack(g, 0, qkv_ref, out_ref, up_ref, down_ref, vec_ref)
    for h in halo:
        h.wait_recv()
    pk_ref[...] = jnp.concatenate([P3[0, :1], P3[1, :1], P3[2, :1]], 1)
    fill_mask(mask_s, dq_ref, dk_ref, pk_ref, span, win // 2)
    lane = lax.broadcasted_iota(jnp.int32, (256, 128), 1) // 64
    row = lax.broadcasted_iota(jnp.int32, (256, 128), 0) // 64 % 2
    on = jnp.where(lane == row, 1.0, 0.0).astype(BF16)
    wide = 256

    def project(j):
        cs = slice(j * wide, (j + 1) * wide)
        bq, bk, bv = (vec_ref[i:i + 1, cs] for i in range(3))
        pairs = [(i, 2 * j + i) for i in range(wide // 128)]
        zq = dot(x_ref[...], qkv_ref[:, cs]) + bq
        zq_ref[:, cs] = zq
        for i, pp in pairs:
            q_ref[:, pp * 128:(pp + 1) * 128] = phi(zq[:, i * 128:(i + 1) * 128], dh_ref[pp], dl_ref[pp], on, scale).astype(BF16)

        def keys(r, _):
            rs = pl.ds(pl.multiple_of(r * S, S), S)
            x = X3[rs, :]
            zk = dot(x, qkv_ref[:, W + j * wide:W + (j + 1) * wide]) + bk

            @pl.when(r == 1)
            def _():
                zk_ref[:, cs] = zk
            for i, pp in pairs:
                k_ref[rs, pp * 128:(pp + 1) * 128] = phi(zk[:, i * 128:(i + 1) * 128], dh_ref[pp], dl_ref[pp], on, scale).astype(BF16)
            v_ref[rs, cs] = (dot(x, qkv_ref[:, 2 * W + j * wide:2 * W + (j + 1) * wide]) + bv).astype(BF16)
            return 0

        lax.fori_loop(0, 3, keys, 0)

    def pair(i, _):
        fwd_attend(S, span, win // 2, i, bias_ref, q_ref, k_ref, v_ref, mask_s, t_s, w_s, vv_s, att_ref, inv_ref)
        return 0

    project(0)
    g.pass_xy(1)
    g.begin_xy(2)
    g.pass_z(2)
    project(1)
    g.pass_diag(1)
    project(2)
    g.pass_xy(2)
    lax.fori_loop(0, W // 256, pair, 0)
    g.pass_diag(2)
    g.finish(1)
    unpack(g, 1, qkv_ref, out_ref, up_ref, down_ref, vec_ref)
    lax.fori_loop(W // 256, W // 128, pair, 0)
    g.finish(2)
    unpack(g, 2, qkv_ref, out_ref, up_ref, down_ref, vec_ref)
    for h in halo:
        h.wait_send()
    g.drain()


def forward(n_seq, own, x, pad, dq, dk, bias8, dh, dl, f, head_dim):
    S, W = x.shape
    R = own.shape[0]
    win = bias8.shape[1]
    span = win + SB
    KS = S + win
    chunks = ((0, VEC + 4 * f), (VEC + 4 * f, 4 * f), (VEC + 8 * f, 4 * f))
    V = pltpu.VMEM
    vm = pl.BlockSpec(memory_space=pltpu.VMEM)
    M = Gather.sems(n_seq // 4)
    D = f * 2 * n_seq
    sd = jax.ShapeDtypeStruct
    dma = pltpu.SemaphoreType.DMA
    return pl.pallas_call(
        functools.partial(forward_kernel, n_seq, chunks, head_dim ** -0.25),
        out_shape=(sd((D, 3 * W), BF16), sd((D, W), BF16), sd((D, 4 * W), BF16), sd((4 * D, W), BF16), sd((VEC, W), F32),
                   sd((S, W), F32), sd((S, W), F32), sd((S, W), BF16), sd((KS, W), BF16), sd((KS, W), BF16), sd((S, W), F32), sd((S, W), F32), sd((1, KS), jnp.int32)),
        in_specs=[vm] * 8, out_specs=(vm,) * 13,
        scratch_shapes=[V((n_seq, 2, R, W), BF16), V((3 * S, W), BF16), V((3, 8, S), jnp.int32), V((S, span), F32), V((2 * SB, span), F32), V((2 * SB, span), BF16),
                        V((KS, 256), BF16), dma((3, M)), dma((3, M)), dma((4,)), dma((4,))],
        compiler_params=pltpu.CompilerParams(collective_id=1, has_side_effects=True, vmem_limit_bytes=60 << 20),
        name="forward",
    )(own, x, pad, dq, dk, bias8, dh, dl)


def lane_mean(v):
    return jnp.mean(v, 1, keepdims=True)


def rows_loop(total, step, body):
    def one(i, c):
        body(pl.ds(pl.multiple_of(i * step, step), step))
        return c

    lax.fori_loop(0, total // step, one, 0)


def fold8(v):
    return jnp.sum(v.reshape(v.shape[0] // 8, 8, v.shape[1]), 0)


def normal_cdf_pdf(x):
    u = jnp.abs(x) * 0.7071067811865476
    t = 1.0 / (1.0 + 0.3275911 * u)
    e = jnp.exp(-0.5 * x * x)
    poly = t * (0.254829592 + t * (-0.284496736 + t * (1.421413741 + t * (-1.453152027 + t * 1.061405429))))
    tail = 0.5 * poly * e
    return jnp.where(x >= 0, 1.0 - tail, tail), e * 0.3989422804014327


def mid_kernel(x_ref, ct_ref, att_ref, ow_ref, up_ref, dw_ref, vec_ref, out_ref, g1_ref, ga_ref, P_ref, vg_ref,
               al_s, hl_s, hlt_s, h1_s, n1_s, i1_s, act_s, dg_s, gi_s, r_s, gl_s, acc_s):
    S, W = x_ref.shape
    FF_ = up_ref.shape[1]
    n_dev = P_ref.shape[0]
    f = W // n_dev
    RB = 64
    b_up, b_out, gain_a, shift_a, b_down, gain_f, shift_f = vec_ref[3:7], vec_ref[7:8], vec_ref[8:9], vec_ref[9:10], vec_ref[10:11], vec_ref[11:12], vec_ref[12:13]
    acc_s[...] = jnp.zeros_like(acc_s)

    def cast(rs):
        al_s[rs, :] = att_ref[rs, :].astype(BF16)

    rows_loop(S, RB, cast)
    r_s[...] = dot(al_s[...], ow_ref[...])

    def norm_one(rs):
        r = r_s[rs, :] + (x_ref[rs, :].astype(F32) + b_out)
        c = r - lane_mean(r)
        inv = lax.rsqrt(lane_mean(c * c) + EPS)
        n = c * inv
        n1_s[rs, :] = n
        i1_s[rs, :] = jnp.broadcast_to(inv, (RB, 128))
        h = n * gain_a + shift_a
        h1_s[rs, :] = h
        hl_s[rs, :] = h.astype(BF16)

    rows_loop(S, RB, norm_one)
    hlt_s[...] = hl_s[...].T
    CW = 512

    for j in range(FF_ // CW):
        cs = slice(j * CW, (j + 1) * CW)
        bias = vec_ref[3 + j * CW // W:4 + j * CW // W, j * CW % W:j * CW % W + CW] if j * CW % W + CW <= W else jnp.concatenate(
            [vec_ref[3 + j * CW // W:4 + j * CW // W, j * CW % W:], vec_ref[4 + j * CW // W:5 + j * CW // W, :j * CW % W + CW - W]], 1)
        inner = dot(hl_s[...], up_ref[:, cs]) + bias
        cdf, pdf = normal_cdf_pdf(inner)
        act_s[:, cs] = (inner * cdf).astype(BF16)
        dg_s[:, cs] = cdf + inner * pdf
    r_s[...] = dot(act_s[...], dw_ref[...])

    def norm_two(rs):
        r = r_s[rs, :] + (h1_s[rs, :] + b_down)
        c = r - lane_mean(r)
        inv = lax.rsqrt(lane_mean(c * c) + EPS)
        n = c * inv
        out_ref[rs, :] = (n * gain_f + shift_f).astype(BF16)
        ct = ct_ref[rs, :].astype(F32)
        acc_s[0] += fold8(ct * n)
        acc_s[1] += fold8(ct)
        gy = ct * gain_f
        g = inv * (gy - lane_mean(gy) - n * lane_mean(gy * n))
        r_s[rs, :] = g
        gl = g.astype(BF16)
        gl_s[rs, :] = gl
        acc_s[2] += fold8(gl.astype(F32))

    rows_loop(S, RB, norm_two)
    per = W // (4 * f)
    for j in range(FF_ // W):
        cs = slice(j * W, (j + 1) * W)
        gi = (dot(gl_s[...], dw_ref[cs, :], NT) * dg_s[:, cs]).astype(BF16)
        gi_s[:, cs] = gi
        vg_ref[3 + j:4 + j, :] = jnp.sum(gi.astype(F32), 0, keepdims=True)
        gd = dot(act_s[:, cs], gl_s[...], TN)
        P_ref[j * per:(j + 1) * per, :4 * f, :] = gd.reshape(per, 4 * f, W).astype(BF16)
    LW = 256
    for l in range(W // LW):
        parts = [dot(hlt_s[...], gi_s[:, k * W + l * LW:k * W + (l + 1) * LW]).reshape(n_dev, f, LW) for k in range(FF_ // W)]
        P_ref[:, 4 * f:8 * f, l * LW:(l + 1) * LW] = jnp.concatenate(parts, 1).astype(BF16)
    r_s[...] += dot(gi_s[...], up_ref[...], NT)

    def back_one(rs):
        g = r_s[rs, :]
        n = n1_s[rs, :]
        acc_s[3] += fold8(g * n)
        acc_s[4] += fold8(g)
        gy = g * gain_a
        inv = i1_s[rs, :1]
        go = inv * (gy - lane_mean(gy) - n * lane_mean(gy * n))
        g1_ref[rs, :] = go
        gl = go.astype(BF16)
        gl_s[rs, :] = gl
        acc_s[5] += fold8(gl.astype(F32))

    rows_loop(S, RB, back_one)
    go = dot(al_s[...], gl_s[...], TN).reshape(n_dev, f, W)
    P_ref[:, 8 * f:, :] = jnp.concatenate([go, jnp.zeros((n_dev, P_ref.shape[1] - 9 * f, W), F32)], 1).astype(BF16)
    ga_ref[...] = dot(gl_s[...], ow_ref[...], NT)
    vg_ref[0:3, :] = jnp.zeros((3, W), F32)
    vg_ref[13:, :] = jnp.zeros((VEC - 13, W), F32)
    for row, i in ((11, 0), (12, 1), (10, 2), (8, 3), (9, 4), (7, 5)):
        vg_ref[row:row + 1, :] = jnp.sum(acc_s[i], 0, keepdims=True)


def middle(x, ct, att, ow, up, dw, vec, n_dev):
    S, W = x.shape
    FF_ = up.shape[1]
    f = W // n_dev
    V = pltpu.VMEM
    vm = pl.BlockSpec(memory_space=pltpu.VMEM)
    sd = jax.ShapeDtypeStruct
    return pl.pallas_call(
        mid_kernel,
        out_shape=(sd((S, W), BF16), sd((S, W), F32), sd((S, W), F32), sd((n_dev, 8 * f + OUT_ROWS, W), BF16), sd((VEC, W), F32)),
        in_specs=[vm] * 7, out_specs=(vm,) * 5,
        scratch_shapes=[V((S, W), BF16), V((S, W), BF16), V((W, S), BF16), V((S, W), F32), V((S, W), F32), V((S, 128), F32),
                        V((S, FF_), BF16), V((S, FF_), F32), V((S, FF_), BF16), V((S, W), F32), V((S, W), BF16), V((6, 8, W), F32)],
        compiler_params=pltpu.CompilerParams(vmem_limit_bytes=60 << 20),
        name="middle",
    )(x, ct, att, ow, up, dw, vec)


OUT_ROWS = 32
QKV_ROWS = 80


class Scatter:
    def __init__(self, pl_, sib, own, R0, R1, R2, R3, out, snd, rcv, chunks):
        self.p, self.sib, self.own, self.R0, self.R1, self.R2, self.R3, self.out = pl_, sib, own, R0, R1, R2, R3, out
        self.snd, self.rcv, self.chunks = snd, rcv, chunks
        self.sent = []

    @staticmethod
    def sems(Z):
        return 6 * Z - 1

    def halves(self, k):
        r0, rows = self.chunks[k]
        h = rows // 32 * 16
        return pl.ds(r0, h), pl.ds(r0 + h, rows - h)

    def rows(self, k):
        return pl.ds(*self.chunks[k])

    def _go(self, src, dst, k, sem, dev, start):
        c = remote(src, dst, self.snd.at[k, sem], self.rcv.at[k, sem], dev)
        if start:
            c.start()
            self.sent.append(c)
        else:
            c.wait_recv()

    def order(self):
        return list(range(1, self.p.Z)) + [0]

    def _c0(self, k, dz, start):
        p = self.p
        zy = pl.ds(2 * p.zcol(dz), 2)
        self._go(self.sib(k, zy), self.R0.at[zy, :, self.rows(k)], k, dz, p.sibling(), start)

    def _c1(self, k, dz, start):
        p = self.p
        z = p.zcol(dz)
        a, b = self.halves(k)
        self._go(self.R0.at[pl.ds(2 * z, 2), 1 - p.x, a], self.R1.at[z, :, a], k, p.Z + dz, p.xpeer(), start)
        self._go(self.R0.at[2 * z + 1 - p.y, :, b], self.R1.at[z, :, b], k, 2 * p.Z + dz, p.ypeer(), start)

    def _c2(self, k, dz, start):
        p = self.p
        z = p.zcol(dz)
        a, b = self.halves(k)
        self._go(self.R1.at[z, 1 - p.y, a], self.R2.at[z, a], k, 3 * p.Z + dz, p.ypeer(), start)
        self._go(self.R1.at[z, 1 - p.x, b], self.R2.at[z, b], k, 4 * p.Z + dz, p.xpeer(), start)

    def _c3(self, k, dz, start):
        p = self.p
        self._go(self.R2.at[p.zcol(dz), self.rows(k)], self.R3.at[dz - 1, self.rows(k)], k, 5 * p.Z + dz - 1, p.zpeer(dz), start)

    def begin(self, k):
        for dz in self.order():
            self._c0(k, dz, True)

    @staticmethod
    def _add(dst, src):
        dst[...] = (dst[...].astype(F32) + src[...].astype(F32)).astype(BF16)

    def add_core(self, k):
        p, r = self.p, self.rows(k)
        for dz in self.order():
            self._c0(k, dz, False)
            z = p.zcol(dz)
            for y in range(2):
                for x in range(2):
                    self._add(self.R0.at[2 * z + y, x, r], self.own(k, 2 * z + y, x))
            self._c1(k, dz, True)

    def add_one(self, k):
        p = self.p
        a, b = self.halves(k)
        for dz in self.order():
            self._c1(k, dz, False)
            z = p.zcol(dz)
            for i in range(2):
                self._add(self.R1.at[z, i, a], self.R0.at[2 * z + i, p.x, a])
                self._add(self.R1.at[z, i, b], self.R0.at[2 * z + p.y, i, b])
            self._c2(k, dz, True)

    def add_two(self, k):
        p = self.p
        a, b = self.halves(k)
        for dz in self.order():
            self._c2(k, dz, False)
            z = p.zcol(dz)
            self._add(self.R2.at[z, a], self.R1.at[z, p.y, a])
            self._add(self.R2.at[z, b], self.R1.at[z, p.x, b])
            if dz:
                self._c3(k, dz, True)

    def finish(self, k):
        p, r = self.p, self.rows(k)
        total = self.R2[p.z, r].astype(F32)
        for dz in range(1, p.Z):
            self._c3(k, dz, False)
            total = total + self.R3[dz - 1, r].astype(F32)
        self.out[r, :] = total

    def drain(self):
        for c in self.sent:
            c.wait_send()
        self.sent = []


def back_attend(S, span, win, i, bias_ref, q_ref, k_ref, v_ref, att_s, inv_s, ga_s, mask_s, t_s, w_s, gs_s, p_s, vv_s, gkt_s, gvt_s,
                gq_s, gk_s, gv_s, bsum, HS):
    lanes = pl.ds(pl.multiple_of(i * 128, 128), 128)
    CH = span // 3
    half = win // 2
    rows = jnp.exp(bias_ref[pl.ds(pl.multiple_of(i * 8, 8), 8), :])
    for h in range(2):
        t_s[h * SB:(h + 1) * SB, :] = toep(rows[h:h + 1], span)
    vv_s[:, :128] = v_ref[:, lanes]
    gkt_s[...] = jnp.zeros_like(gkt_s)
    gvt_s[...] = jnp.zeros_like(gvt_s)
    lane = lax.broadcasted_iota(jnp.int32, (SB, 128), 1)

    def ext(x):
        hi, lo = split2(-jnp.sum(x, 1, keepdims=True))
        return jnp.where(lane == 0, hi, jnp.where(lane == 1, lo, jnp.zeros((SB, 128), BF16)))

    for a in range(S // SB):
        rs = slice(a * SB, (a + 1) * SB)
        qq = jnp.concatenate(halves(q_ref[rs, lanes]), 0)
        ga = ga_s[rs, lanes]
        inv = inv_s[rs, lanes]
        gwa, gwb = halves((ga * inv).astype(BF16))
        pa, pb = halves(ga * att_s[rs, lanes] * inv)
        gg = jnp.concatenate([jnp.concatenate([gwa, ext(pa)], 1), jnp.concatenate([gwb, ext(pb)], 1)], 0)
        for c in range(0, span, CH):
            s = dot(qq, k_ref[a * SB + c:a * SB + c + CH, lanes], NT)
            g = dot(gg, vv_s[a * SB + c:a * SB + c + CH, :], NT)
            m = mask_s[rs, c:c + CH]
            for h in range(2):
                hs = slice(h * SB, (h + 1) * SB)
                cm = t_s[hs, c:c + CH] * m
                w = s[hs] * cm
                w_s[hs, c:c + CH] = w.astype(BF16)
                gs_s[hs, c:c + CH] = (g[hs] * cm).astype(BF16)
                pw = g[hs] * w
                if a == 0:
                    p_s[hs, c:c + CH] = pw
                else:
                    p_s[hs, c:c + CH] += pw
        gq = dot(gs_s[...], k_ref[a * SB:a * SB + span, lanes])
        gq_s[rs, lanes] = pick(gq[:SB], gq[SB:])
        gkt_s[:, a * SB:a * SB + span] += dot(qq, gs_s[...], TN)
        gvt_s[:, a * SB:a * SB + span] += dot(jnp.concatenate([gwa, gwb], 0), w_s[...], TN)
    for t_ref, own, at in ((gkt_s, gk_s, 0), (gvt_s, gv_s, 128)):
        HS[0, i, :, at:at + 128] = t_ref[:, :half].T.astype(BF16)
        own[:, lanes] = t_ref[:, half:half + S].T
        HS[1, i, :, at:at + 128] = t_ref[:, half + S:].T.astype(BF16)
    bsum[pl.ds(pl.multiple_of(i * 8, 8), 8), :] = jnp.concatenate([unskew(p_s[:SB, :], win), unskew(p_s[SB:, :], win), jnp.zeros((6, win), F32)], 0)


def phi_back(g, feat, z, dh, dl, on, scale):
    t = g * feat.astype(F32)
    th, tl = split2(t)
    back = dot(th, dh, NT) + dot(tl, dh, NT) + dot(th, dl, NT)
    total = dot(jnp.concatenate([th, tl], 1), on)
    return scale * (back - (z * scale) * total)


def back_kernel(n_seq, chunks, scale, x_ref, dq_ref, dk_ref, pk_ref, bias_ref, dh_ref, dl_ref, w_ref, q_ref, k_ref, v_ref, vg_ref,
                att_h, inv_h, ga_h, zq_h, zk_h, g1_h, P_h,
                out_ref, gx_ref, vout_ref,
                big, U, R0, R1, R2, R3, mask_s, t_s, w_s, gs_s, p_s, vv_s, gkt_s, gvt_s, gq_s, gk_s, gv_s, bsum, HS, HR, gp_s, xt_s, cur, got,
                snd, rcv, hsnd, hrcv, vsnd, vrcv, lsem):
    S, W = x_ref.shape
    win = bias_ref.shape[1]
    span = win + SB
    n_pair = W // 128
    n_dev = 2 * n_seq
    f = W // n_dev
    p = Place(n_seq)

    def load(src, dst, i):
        return pltpu.make_async_copy(src, dst, lsem.at[i])

    early = [load(h, big.at[i], i) for i, h in enumerate((att_h, inv_h, ga_h))]
    halves_of = []
    for k in range(2):
        r0, n = chunks[k]
        halves_of.append(load(P_h.at[:, p.c, :, pl.ds(r0, n)], U.at[:, k, :, pl.ds(0, n)], 3 + k))
    for c in early + halves_of:
        c.start()
    p.greet()

    def sib(k, zy):
        r0, n = chunks[k]
        return P_h.at[zy, 1 - p.c, :, pl.ds(r0, n)] if k < 2 else U.at[zy, 1 - p.c, :, pl.ds(0, n)]

    def own(k, zy, x):
        n = chunks[k][1]
        return U.at[zy, k if k < 2 else p.c, x, pl.ds(0, n)]

    sc = Scatter(p, sib, own, R0, R1, R2, R3, out_ref, snd, rcv, chunks)
    sc.begin(0)
    sc.begin(1)
    fill_mask(mask_s, dq_ref, dk_ref, pk_ref, span, win // 2)
    vv_s[:, 128:] = jnp.ones((vv_s.shape[0], 128), BF16)
    xt_s[...] = x_ref[...].T
    for c in early:
        c.wait()

    def to_left(i):
        return remote(HS.at[0, i], HR.at[1, i], hsnd.at[0, i], hrcv.at[1, i], p.along(-1))

    def to_right(i):
        return remote(HS.at[1, i], HR.at[0, i], hsnd.at[1, i], hrcv.at[0, i], p.along(1))

    def pair(i, _):
        back_attend(S, span, win, i, bias_ref, q_ref, k_ref, v_ref, big.at[0], big.at[1], big.at[2], mask_s, t_s, w_s, gs_s, p_s, vv_s,
                    gkt_s, gvt_s, gq_s, gk_s, gv_s, bsum, HS)
        to_left(i).start()
        to_right(i).start()
        return 0

    lax.fori_loop(0, 1, pair, 0)
    halves_of[0].wait()
    sc.add_core(0)
    halves_of[1].wait()
    sc.add_core(1)
    lax.fori_loop(1, n_pair // 2 + 1, pair, 0)
    sc.add_one(0)
    lax.fori_loop(n_pair // 2 + 1, n_pair, pair, 0)
    late = [load(h, big.at[i], i) for i, h in enumerate((zq_h, zk_h, g1_h))]
    for c in late:
        c.start()
    sc.add_one(1)
    sc.add_two(0)
    for c in late:
        c.wait()
    lane = lax.broadcasted_iota(jnp.int32, (256, 128), 1) // 64
    row = lax.broadcasted_iota(jnp.int32, (256, 128), 0) // 64 % 2
    on = jnp.where(lane == row, 1.0, 0.0).astype(BF16)

    def project(i, _):
        def at(base):
            return pl.ds(pl.multiple_of(base + i * 128, 128), 128)

        lanes = at(0)
        own_lanes = pl.ds(pl.multiple_of(i * 128, 128), 128)
        gp_s[:, at(0)] = phi_back(gq_s[:, lanes], q_ref[:, lanes], big[0, :, lanes], dh_ref[i], dl_ref[i], on, scale).astype(BF16)
        to_left(i).wait_recv()
        to_right(i).wait_recv()
        gk = gk_s[:, own_lanes] + HR[0, i, :, :128].astype(F32) + HR[1, i, :, :128].astype(F32)
        gv = gv_s[:, own_lanes] + HR[0, i, :, 128:].astype(F32) + HR[1, i, :, 128:].astype(F32)
        gp_s[:, at(W)] = phi_back(gk, k_ref[win // 2:win // 2 + S, lanes], big[1, :, lanes], dh_ref[i], dl_ref[i], on, scale).astype(BF16)
        gp_s[:, at(2 * W)] = gv.astype(BF16)
        return 0

    lax.fori_loop(0, n_pair, project, 0)
    LW = 256
    n3 = chunks[2][1]
    for l in range(W // LW):
        parts = [dot(xt_s[...], gp_s[:, k * W + l * LW:k * W + (l + 1) * LW]).reshape(n_dev, f, LW) for k in range(3)]
        parts.append(jnp.zeros((n_dev, n3 - 3 * f, LW), F32))
        U[:, :, :, :n3, l * LW:(l + 1) * LW] = jnp.concatenate(parts, 1).astype(BF16).reshape(n_seq // 2, 2, 2, n3, LW)
    sc.begin(2)
    cur[0, :16, :] = jnp.concatenate([bsum[8 * (h // 2) + h % 2:8 * (h // 2) + h % 2 + 1, :] for h in range(2 * n_pair)] + [jnp.zeros((16 - 2 * n_pair, win), F32)], 0)
    cur[0, 16:, :W] = vg_ref[...]
    cur[0, 16:, W:] = jnp.zeros((VEC, win - W), F32)
    for k in range(3):
        cur[0, 16 + k:17 + k, :W] = jnp.sum(gp_s[:, k * W:(k + 1) * W].astype(F32), 0, keepdims=True)
    va = SumAll(p, cur, got, vsnd, vrcv)
    n = SumAll.steps(p.Z)
    va.start(0)
    sc.add_core(2)
    sc.add_two(1)
    va.step(0)
    va.start(1)
    gx_ref[...] = big[2] + dot(gp_s[...], w_ref[...], NT)
    va.step(1)
    va.start(2)
    sc.add_one(2)
    va.step(2)
    va.start(3)
    sc.finish(0)
    sc.add_two(2)
    va.step(3)
    for i in range(4, n):
        va.start(i)
        va.step(i)
    vout_ref[...] = cur[n]
    sc.finish(1)
    sc.finish(2)
    sc.drain()
    for i in range(n_pair):
        to_left(i).wait_send()
        to_right(i).wait_send()


def backward(n_seq, x, dq, dk, pk, bias8, dh, dl, w, q, k, v, vg, att, inv, ga, zq, zk, g1, P_, head_dim):
    S, W = x.shape
    KS = k.shape[0]
    win = bias8.shape[1]
    span = win + SB
    Z = n_seq // 4
    n_pair = W // 128
    f = W // (2 * n_seq)
    chunks = ((0, 4 * f), (4 * f, 4 * f + OUT_ROWS), (8 * f + OUT_ROWS, QKV_ROWS))
    R = 8 * f + OUT_ROWS + QKV_ROWS
    V = pltpu.VMEM
    vm = pl.BlockSpec(memory_space=pltpu.VMEM)
    hbm = pl.BlockSpec(memory_space=pl.ANY)
    M = Scatter.sems(Z)
    n = SumAll.steps(Z)
    D = pltpu.SemaphoreType.DMA
    sd = jax.ShapeDtypeStruct
    pw = 4 * f + OUT_ROWS
    return pl.pallas_call(
        functools.partial(back_kernel, n_seq, chunks, head_dim ** -0.25),
        out_shape=(sd((R, W), F32), sd((S, W), F32), sd((32, win), F32)),
        in_specs=[vm] * 12 + [hbm] * 7, out_specs=(vm,) * 3,
        scratch_shapes=[
            V((3, S, W), F32), V((2 * Z, 2, 2, pw, W), BF16), V((2 * Z, 2, R, W), BF16), V((Z, 2, R, W), BF16), V((Z, R, W), BF16), V((Z - 1, R, W), BF16),
            V((S, span), F32), V((2 * SB, span), F32), V((2 * SB, span), BF16), V((2 * SB, span), BF16), V((2 * SB, span), F32),
            V((KS, 256), BF16), V((128, KS), F32), V((128, KS), F32), V((S, W), F32), V((S, W), F32), V((S, W), F32), V((8 * n_pair, win), F32),
            V((2, n_pair, S, 256), BF16), V((2, n_pair, S, 256), BF16), V((S, 3 * W), BF16), V((W, S), BF16), V((n + 1, 32, win), F32), V((n, 32, win), F32),
            D((3, M)), D((3, M)), D((2, n_pair)), D((2, n_pair)), D((n,)), D((n,)), D((5,))],
        compiler_params=pltpu.CompilerParams(collective_id=2, has_side_effects=True, vmem_limit_bytes=64 << 20),
        name="backward",
    )(x, dq, dk, pk, bias8, dh, dl, w, q, k, v, vg, att, inv, ga, zq, zk, g1, P_)


EPS = 1e-06
EXACT_MATMUL = lax.Precision.HIGHEST


def padded_2(cells, sides, width):
    for axis, dim in sides:
        count = lax.axis_size(axis)
        ends = count - 1
        head = lax.slice_in_dim(cells, 0, width, axis=dim)
        tail = lax.slice_in_dim(cells, cells.shape[dim] - width, cells.shape[dim], axis=dim)
        cells = jnp.concatenate(
            [
                lax.ppermute(tail, axis, [(i, (i + 1) % count) for i in range(ends)]),
                cells,
                lax.ppermute(head, axis, [((i + 1) % count, i) for i in range(ends)]),
            ],
            axis=dim,
        )
    return cells


def passed_along(block, axis, distance):
    devices = range(lax.axis_size(axis))
    route = [(i - distance, i) for i in devices if i - distance in devices]
    return lax.ppermute(block, axis, route)


def layer_norm(values, gain, shift):
    center = values - jnp.mean(values, -1, keepdims=True)
    spread = jnp.mean(center * center, -1, keepdims=True)
    return center * lax.rsqrt(spread + EPS) * gain + shift


def feature_map(heads_in, random_features):
    scaled_input = heads_in * heads_in.shape[-1] ** (-0.25)
    projected_rows = jnp.einsum(
        "ykb,kib->yki", scaled_input, random_features, precision=EXACT_MATMUL
    )
    half_square = 0.5 * jnp.sum(scaled_input * scaled_input, -1, keepdims=True)
    return jnp.exp(projected_rows - half_square) * random_features.shape[1] ** (-0.5)


def document_numbers(positions, lengths_row):
    ends = jnp.cumsum(lengths_row)
    counted = jnp.sum((positions[:, None] >= ends[None, :]).astype(jnp.int32), -1)
    return jnp.where(positions < 0, -1, counted)


def fits(n_seq, n_row, f):
    return n_row == 2 and n_seq in (8, 16) and f % 8 == 0


def own_slab(weights, n_seq):
    w_qkv, b_qkv, w_out, b_out, gain_a, shift_a, w_up, b_up, w_down, b_down, gain_f, shift_f = weights
    W = w_out.shape[1]
    n_dev = 2 * n_seq
    me = lax.axis_index("seq") * 2 + lax.axis_index("row")

    def placed(v):
        n = v.shape[0]
        lanes = jnp.arange(n * n_dev, dtype=jnp.int32) // n
        return jnp.where(lanes == me, jnp.tile(v, n_dev), jnp.zeros((), v.dtype)).reshape(-1, W)

    def blocks(w):
        return [w[:, j * W : (j + 1) * W] for j in range(w.shape[1] // W)]

    vecs = [placed(v) for v in (b_qkv, b_up, b_out, gain_a, shift_a, b_down, gain_f, shift_f)]
    rows = sum(v.shape[0] for v in vecs)
    pad = jnp.zeros((VEC - rows, W), BF16)
    return jnp.concatenate(vecs + [pad] + blocks(w_qkv) + [w_out] + blocks(w_up) + [w_down], 0)


def feature_blocks(draws):
    h, m, d = draws.shape
    t = draws.transpose(0, 2, 1).reshape(h // 2, 2, d, m)
    z = jnp.zeros((h // 2, d, m), F32)
    full = jnp.concatenate([jnp.concatenate([t[:, 0], z], 2), jnp.concatenate([z, t[:, 1]], 2)], 1)
    hi = lax.reduce_precision(full, 8, 7)
    return hi.astype(BF16), (full - hi).astype(BF16)


def with_kernels(tokens, cotangent, lengths, padding, feature_draws, rel_bias, *weights):
    local = tokens[0]
    seq_len, model_width = local.shape
    head_count, window_len = rel_bias.shape
    half_win = window_len // 2
    head_dim = model_width // head_count
    n_seq = lax.axis_size("seq")
    f = weights[2].shape[0]
    start_pos = lax.axis_index("seq") * seq_len
    positions = start_pos + jnp.arange(seq_len, dtype=jnp.int32)
    ext_pos = start_pos - half_win + jnp.arange(seq_len + window_len, dtype=jnp.int32)
    dq = document_numbers(positions, lengths[0])[:, None]
    dk = document_numbers(ext_pos, lengths[0])[None, :]
    pad8 = jnp.broadcast_to(padding, (8, seq_len))
    bias8 = bias_rows(rel_bias)
    dh, dl = feature_blocks(feature_draws)
    (qkv_w, out_w, up_w, down_w, vec, zq, zk, q_low, keys_x, vals_x, attended, inv_tot, pk) = forward(
        n_seq, own_slab(weights, n_seq), local, pad8, dq, dk, bias8, dh, dl, f, head_dim)
    out, g1, ga, P_, vg = middle(local, cotangent[0], attended, out_w, up_w, down_w, vec, 2 * n_seq)
    P_ = P_.reshape(n_seq // 2, 2, 2, P_.shape[1], model_width)
    o, gx, vo = backward(n_seq, local, dq, dk, pk, bias8, dh, dl, qkv_w, q_low, keys_x, vals_x, vg, attended, inv_tot, ga, zq, zk, g1, P_, head_dim)
    me = lax.axis_index("seq") * 2 + lax.axis_index("row")

    def cols(r0, k):
        return o[r0 : r0 + k * f].reshape(k, f, model_width).transpose(1, 0, 2).reshape(f, k * model_width)

    def mine(r0, k):
        return lax.dynamic_slice(vo[16 + r0 : 16 + r0 + k, :model_width].reshape(-1), (me * k * f,), (k * f,))

    q0 = 8 * f + OUT_ROWS
    return (
        out[None], gx[None], vo[:head_count], cols(q0, 3), mine(0, 3), o[8 * f : 9 * f], mine(7, 1), mine(8, 1), mine(9, 1),
        cols(4 * f, 4), mine(3, 4), o[: 4 * f], mine(10, 1), mine(11, 1), mine(12, 1),
    )


def on_device(
    tokens,
    cotangent,
    lengths,
    padding,
    feature_draws,
    rel_bias,
    w_qkv,
    b_qkv,
    w_out,
    b_out,
    gain_attn,
    shift_attn,
    w_up,
    b_up,
    w_down,
    b_down,
    gain_ffn,
    shift_ffn,
):
    if fits(lax.axis_size("seq"), lax.axis_size("row"), w_out.shape[0]):
        return with_kernels(
            tokens, cotangent, lengths, padding, feature_draws, rel_bias, w_qkv, b_qkv, w_out, b_out, gain_attn, shift_attn,
            w_up, b_up, w_down, b_down, gain_ffn, shift_ffn,
        )
    local = tokens[0]
    seq_len = local.shape[0]
    model_width = local.shape[1]
    head_count = rel_bias.shape[0]
    window_len = rel_bias.shape[1]
    half_win = window_len // 2
    feat_count = feature_draws.shape[1]
    head_dim = model_width // head_count
    feat_cols = head_count * feat_count
    params = (
        lax.all_gather(w_qkv, ("seq", "row"), axis=0, tiled=True),
        lax.all_gather(b_qkv, ("seq", "row"), axis=0, tiled=True),
        lax.all_gather(w_out, ("seq", "row"), axis=0, tiled=True),
        lax.all_gather(b_out, ("seq", "row"), axis=0, tiled=True),
        lax.all_gather(gain_attn, ("seq", "row"), axis=0, tiled=True),
        lax.all_gather(shift_attn, ("seq", "row"), axis=0, tiled=True),
        lax.all_gather(w_up, ("seq", "row"), axis=0, tiled=True),
        lax.all_gather(b_up, ("seq", "row"), axis=0, tiled=True),
        lax.all_gather(w_down, ("seq", "row"), axis=0, tiled=True),
        lax.all_gather(b_down, ("seq", "row"), axis=0, tiled=True),
        lax.all_gather(gain_ffn, ("seq", "row"), axis=0, tiled=True),
        lax.all_gather(shift_ffn, ("seq", "row"), axis=0, tiled=True),
    )
    (
        qkv_w,
        qkv_b,
        out_w,
        out_b,
        first_norm_gain,
        shift_one,
        up_w,
        up_b,
        down_w,
        down_b,
        gain_two,
        shift_two,
    ) = params
    seq_pos = lax.axis_index("seq")
    start_pos = seq_pos * seq_len
    positions = start_pos + jnp.arange(seq_len, dtype=jnp.int32)
    ext_pos = start_pos - half_win + jnp.arange(seq_len + window_len, dtype=jnp.int32)
    doc_query = document_numbers(positions, lengths[0])
    doc_keys = document_numbers(ext_pos, lengths[0])
    pad_local = padding[0]
    pad_ones = jnp.ones((half_win,), jnp.int32)
    pad_keys = jnp.concatenate([pad_ones, pad_local, pad_ones])
    proj_qkv = jnp.dot(local, qkv_w, preferred_element_type=jnp.float32) + qkv_b
    queries = proj_qkv[:, :model_width].reshape(seq_len, head_count, head_dim)
    keys_in = proj_qkv[:, model_width : 2 * model_width].reshape(seq_len, head_count, head_dim)
    q_full, query_back = jax.vjp(partial(feature_map, random_features=feature_draws), queries)
    k_full, key_back = jax.vjp(partial(feature_map, random_features=feature_draws), keys_in)
    q_feat = q_full.astype(jnp.bfloat16)
    k_flat = k_full.astype(jnp.bfloat16).reshape(seq_len, feat_cols)
    values_low = proj_qkv[:, 2 * model_width :].astype(jnp.bfloat16)
    own_keys = jnp.concatenate([k_flat, values_low], 1)
    masked_keys = jnp.concatenate([k_flat * pad_local.astype(jnp.bfloat16)[:, None], values_low], 1)
    rims = padded_2(masked_keys, (("seq", 0),), half_win)
    key_ext = jnp.concatenate([rims[:half_win], own_keys, rims[half_win + seq_len :]], 0)

    dq, dk, pk = doc_query[:, None], doc_keys[None, :], pad_keys[None, :]
    bias8 = bias_rows(rel_bias)
    q_low = q_feat.reshape(seq_len, feat_cols)
    keys_x, vals_x = key_ext[:, :feat_cols], key_ext[:, feat_cols:]
    attended, inv_tot = attn_fwd(dq, dk, pk, bias8, q_low, keys_x, vals_x)
    att_low = attended.astype(jnp.bfloat16)
    branch = jnp.dot(att_low, out_w, preferred_element_type=jnp.float32) + out_b
    resid_one = local.astype(jnp.float32) + branch
    hidden_one, ln_one_back = jax.vjp(
        layer_norm, resid_one, first_norm_gain.astype(jnp.float32), shift_one.astype(jnp.float32)
    )
    hidden_low = hidden_one.astype(jnp.bfloat16)
    inner = jnp.dot(hidden_low, up_w, preferred_element_type=jnp.float32) + up_b
    active, gelu_back = jax.vjp(partial(jax.nn.gelu, approximate=False), inner)
    active_low = active.astype(jnp.bfloat16)
    ffn_out = jnp.dot(active_low, down_w, preferred_element_type=jnp.float32) + down_b
    result, ln_two_back = jax.vjp(
        layer_norm,
        hidden_one + ffn_out,
        gain_two.astype(jnp.float32),
        shift_two.astype(jnp.float32),
    )
    params = (
        lax.all_gather(w_qkv, ("seq", "row"), axis=0, tiled=True),
        lax.all_gather(b_qkv, ("seq", "row"), axis=0, tiled=True),
        lax.all_gather(w_out, ("seq", "row"), axis=0, tiled=True),
        lax.all_gather(b_out, ("seq", "row"), axis=0, tiled=True),
        lax.all_gather(gain_attn, ("seq", "row"), axis=0, tiled=True),
        lax.all_gather(shift_attn, ("seq", "row"), axis=0, tiled=True),
        lax.all_gather(w_up, ("seq", "row"), axis=0, tiled=True),
        lax.all_gather(b_up, ("seq", "row"), axis=0, tiled=True),
        lax.all_gather(w_down, ("seq", "row"), axis=0, tiled=True),
        lax.all_gather(b_down, ("seq", "row"), axis=0, tiled=True),
        lax.all_gather(gain_ffn, ("seq", "row"), axis=0, tiled=True),
        lax.all_gather(shift_ffn, ("seq", "row"), axis=0, tiled=True),
    )
    (
        qkv_w,
        qkv_b,
        out_w,
        out_b,
        first_norm_gain,
        shift_one,
        up_w,
        up_b,
        down_w,
        down_b,
        gain_two,
        shift_two,
    ) = params
    grad_two, grad_gain_two, grad_shift_two = ln_two_back(cotangent[0].astype(jnp.float32))
    grad_two_low = grad_two.astype(jnp.bfloat16)
    grad_down_w = jnp.einsum(
        "ti,tj->ij", active_low, grad_two_low, preferred_element_type=jnp.float32
    )
    grad_down_b = jnp.sum(grad_two_low, 0, dtype=jnp.float32)
    grad_active = jnp.dot(grad_two_low, down_w.T, preferred_element_type=jnp.float32)
    grad_inner_low = gelu_back(grad_active)[0].astype(jnp.bfloat16)
    grad_up_w = jnp.einsum(
        "ti,tj->ij", hidden_low, grad_inner_low, preferred_element_type=jnp.float32
    )
    grad_up_b = jnp.sum(grad_inner_low, 0, dtype=jnp.float32)
    grad_hidden = grad_two + jnp.dot(grad_inner_low, up_w.T, preferred_element_type=jnp.float32)
    grad_one, grad_gain_one, grad_shift_one = ln_one_back(grad_hidden)
    grad_one_low = grad_one.astype(jnp.bfloat16)
    grad_out_w = jnp.einsum("ti,tj->ij", att_low, grad_one_low, preferred_element_type=jnp.float32)
    grad_out_b = jnp.sum(grad_one_low, 0, dtype=jnp.float32)
    grad_att = jnp.dot(grad_one_low, out_w.T, preferred_element_type=jnp.float32)
    grad_fq_all, grad_kf, grad_vv, grad_b8 = attn_bwd(
        dq, dk, pk, bias8, q_low, keys_x, vals_x, attended, inv_tot, grad_att
    )
    grad_bias = grad_b8.reshape(head_count // 2, 8, window_len)[:, :2].reshape(head_count, window_len)
    lower_rim = jnp.concatenate([grad_kf[:half_win], grad_vv[:half_win]], 1)
    upper_rim = jnp.concatenate([grad_kf[half_win + seq_len :], grad_vv[half_win + seq_len :]], 1)
    from_right = passed_along(lower_rim.astype(jnp.bfloat16), "seq", -1).astype(lower_rim.dtype)
    from_left = passed_along(upper_rim.astype(jnp.bfloat16), "seq", 1).astype(upper_rim.dtype)
    returned = from_left + from_right
    pad_float = pad_local.astype(jnp.float32)[:, None]
    grad_kfeat = grad_kf[half_win : half_win + seq_len] + returned[:, :feat_cols] * pad_float
    value_gradient = grad_vv[half_win : half_win + seq_len] + returned[:, feat_cols:]
    grad_queries = query_back(grad_fq_all.reshape(seq_len, head_count, feat_count))[0]
    grad_keys_in = key_back(grad_kfeat.reshape(seq_len, head_count, feat_count))[0]
    grad_proj_low = jnp.concatenate(
        [
            grad_queries.reshape(seq_len, model_width),
            grad_keys_in.reshape(seq_len, model_width),
            value_gradient,
        ],
        1,
    ).astype(jnp.bfloat16)
    grad_qkv_w = jnp.einsum("ti,tj->ij", local, grad_proj_low, preferred_element_type=jnp.float32)
    grad_qkv_b = jnp.sum(grad_proj_low, 0, dtype=jnp.float32)
    grad_input = grad_one + jnp.dot(grad_proj_low, qkv_w.T, preferred_element_type=jnp.float32)
    grad_rel = lax.psum(grad_bias, ("seq", "row"))
    summed = (
        lax.psum_scatter(grad_qkv_w, ("seq", "row"), scatter_dimension=0, tiled=True),
        lax.psum_scatter(grad_qkv_b, ("seq", "row"), scatter_dimension=0, tiled=True),
        lax.psum_scatter(grad_out_w, ("seq", "row"), scatter_dimension=0, tiled=True),
        lax.psum_scatter(grad_out_b, ("seq", "row"), scatter_dimension=0, tiled=True),
        lax.psum_scatter(grad_gain_one, ("seq", "row"), scatter_dimension=0, tiled=True),
        lax.psum_scatter(grad_shift_one, ("seq", "row"), scatter_dimension=0, tiled=True),
        lax.psum_scatter(grad_up_w, ("seq", "row"), scatter_dimension=0, tiled=True),
        lax.psum_scatter(grad_up_b, ("seq", "row"), scatter_dimension=0, tiled=True),
        lax.psum_scatter(grad_down_w, ("seq", "row"), scatter_dimension=0, tiled=True),
        lax.psum_scatter(grad_down_b, ("seq", "row"), scatter_dimension=0, tiled=True),
        lax.psum_scatter(grad_gain_two, ("seq", "row"), scatter_dimension=0, tiled=True),
        lax.psum_scatter(grad_shift_two, ("seq", "row"), scatter_dimension=0, tiled=True),
    )
    return (
        result[None].astype(jnp.bfloat16),
        grad_input[None],
        grad_rel,
        summed[0],
        summed[1],
        summed[2],
        summed[3],
        summed[4],
        summed[5],
        summed[6],
        summed[7],
        summed[8],
        summed[9],
        summed[10],
        summed[11],
    )


def solution(mesh):
    in_specs = (
        P("row", "seq", None),
        P("row", "seq", None),
        P("row", None),
        P("row", "seq"),
        P(),
        P(),
        P(("seq", "row"), None),
        P(("seq", "row")),
        P(("seq", "row"), None),
        P(("seq", "row")),
        P(("seq", "row")),
        P(("seq", "row")),
        P(("seq", "row"), None),
        P(("seq", "row")),
        P(("seq", "row"), None),
        P(("seq", "row")),
        P(("seq", "row")),
        P(("seq", "row")),
    )
    out_specs = (
        P("row", "seq", None),
        P("row", "seq", None),
        P(),
        P(("seq", "row"), None),
        P(("seq", "row")),
        P(("seq", "row"), None),
        P(("seq", "row")),
        P(("seq", "row")),
        P(("seq", "row")),
        P(("seq", "row"), None),
        P(("seq", "row")),
        P(("seq", "row"), None),
        P(("seq", "row")),
        P(("seq", "row")),
        P(("seq", "row")),
    )
    return jax.shard_map(
        on_device, mesh=mesh, in_specs=in_specs, out_specs=out_specs, check_vma=False
    )
```

```python
from functools import partial

import functools
import jax
import jax.numpy as jnp
from jax import lax
from jax.experimental import pallas as pl
from jax.experimental.pallas import tpu as pltpu
from jax.sharding import PartitionSpec as P

F32, BF16 = jnp.float32, jnp.bfloat16
NT = (((1,), (1,)), ((), ()))
TN = (((0,), (0,)), ((), ()))
SB = 128

def dot(a, b, dims=None):
    if dims is None:
        return jnp.dot(a, b, preferred_element_type=F32)
    return lax.dot_general(a, b, dims, preferred_element_type=F32)

def toep(row, width):
    win = row.shape[1]
    wide = jnp.concatenate([row, jnp.zeros((1, width - win), F32)], 1)
    return pltpu.roll(jnp.broadcast_to(wide, (SB, width)), 0, 1, stride=1, stride_axis=0)

def unskew(p, win):
    rows = p.shape[0]; width = p.shape[1]
    while rows > 8:
        rows //= 2
        p = p[:rows] + pltpu.roll(p[rows:], width - rows, 1)
    r = lax.broadcasted_iota(jnp.int32, (8, 1), 0)
    for s in (1, 2, 4):
        p = jnp.where((r & s) != 0, pltpu.roll(p, width - s, 1), p)
    return jnp.sum(p, 0, keepdims=True)[:, :win]

def fill_mask(mask_s, dq_ref, dk_ref, pk_ref, span, half):
    S = mask_s.shape[0]
    for a in range(S // SB):
        dq = dq_ref[a*SB:(a+1)*SB, :]
        dk = dk_ref[:, a*SB:a*SB+span]
        pk = pk_ref[:, a*SB:a*SB+span]
        r = lax.broadcasted_iota(jnp.int32, (SB, span), 0)
        c = lax.broadcasted_iota(jnp.int32, (SB, span), 1)
        ok = (dq == dk) & ((pk == 1) | (c == r + half))
        mask_s[a*SB:(a+1)*SB, :] = jnp.where(ok, 1.0, 0.0)

def halves(x):
    lane = lax.broadcasted_iota(jnp.int32, x.shape, 1)
    z = jnp.zeros_like(x)
    return jnp.where(lane < 64, x, z), jnp.where(lane >= 64, x, z)

def pick(a, b):
    lane = lax.broadcasted_iota(jnp.int32, a.shape, 1)
    return jnp.where(lane < 64, a, b)

def fwd_kernel(CH, dq_ref, dk_ref, pk_ref, bias_ref, q_ref, k_ref, v_ref, att_ref, inv_ref, mask_s, t_s, w_s, v_s):
    S = q_ref.shape[0]; win = bias_ref.shape[1]; span = win + SB
    p = pl.program_id(0)
    @pl.when(p == 0)
    def _():
        fill_mask(mask_s, dq_ref, dk_ref, pk_ref, span, win // 2)
        v_s[:, 128:] = jnp.ones((v_s.shape[0], 128), BF16)
    rows = jnp.exp(bias_ref[pl.ds(pl.multiple_of(p * 8, 8), 8), :])
    for i in range(2):
        t_s[i*SB:(i+1)*SB, :] = toep(rows[i:i+1], span)
    v_s[:, :128] = v_ref[...]
    for a in range(S // SB):
        qa, qb = halves(q_ref[a*SB:(a+1)*SB, :])
        qq = jnp.concatenate([qa, qb], 0)
        for c in range(0, span, CH):
            s = dot(qq, k_ref[a*SB+c:a*SB+c+CH, :], NT)
            m = mask_s[a*SB:(a+1)*SB, c:c+CH]
            t = t_s[:, c:c+CH]
            w_s[:SB, c:c+CH] = (s[:SB] * (t[:SB] * m)).astype(BF16)
            w_s[SB:, c:c+CH] = (s[SB:] * (t[SB:] * m)).astype(BF16)
        o = dot(w_s[...], v_s[a*SB:a*SB+span, :])
        inv = 1.0 / pick(o[:SB, 128:], o[SB:, 128:])
        att_ref[a*SB:(a+1)*SB, :] = pick(o[:SB, :128], o[SB:, :128]) * inv
        inv_ref[a*SB:(a+1)*SB, :] = inv

def bias_rows(rel_bias):
    h, w = rel_bias.shape
    x = rel_bias.reshape(h // 2, 2, w)
    return jnp.pad(x, ((0, 0), (0, 6), (0, 0))).reshape(h // 2 * 8, w)

def attn_fwd(dq, dk, pk, bias8, q, k, v, CH=384):
    S, D = q.shape; KS = k.shape[0]; win = bias8.shape[1]; span = win + SB
    full = lambda *s: pl.BlockSpec(s, lambda p: (0,) * len(s))
    col = lambda n: pl.BlockSpec((n, 128), lambda p: (0, p))
    return pl.pallas_call(
        functools.partial(fwd_kernel, CH),
        grid=(D // 128,),
        out_shape=(jax.ShapeDtypeStruct((S, D), F32), jax.ShapeDtypeStruct((S, D), F32)),
        in_specs=[full(S, 1), full(1, KS), full(1, KS), full(*bias8.shape), col(S), col(KS), col(KS)],
        out_specs=(col(S), col(S)),
        scratch_shapes=[pltpu.VMEM((S, span), F32), pltpu.VMEM((2*SB, span), F32), pltpu.VMEM((2*SB, span), BF16), pltpu.VMEM((KS, 256), BF16)],
        compiler_params=pltpu.CompilerParams(vmem_limit_bytes=48 << 20),
        name="attn_fwd",
    )(dq, dk, pk, bias8, q, k, v)

def bwd_kernel(CH, dq_ref, dk_ref, pk_ref, bias_ref, q_ref, k_ref, v_ref, att_ref, inv_ref, ga_ref,
               gq_ref, gk_ref, gv_ref, gb_ref, mask_s, t_s, w_s, gs_s, p_s, v_s, gk_s, gv_s):
    S = q_ref.shape[0]; win = bias_ref.shape[1]; span = win + SB
    p = pl.program_id(0)
    @pl.when(p == 0)
    def _():
        fill_mask(mask_s, dq_ref, dk_ref, pk_ref, span, win // 2)
        v_s[:, 128:] = jnp.ones((v_s.shape[0], 128), BF16)
    rows = jnp.exp(bias_ref[pl.ds(pl.multiple_of(p * 8, 8), 8), :])
    for i in range(2):
        t_s[i*SB:(i+1)*SB, :] = toep(rows[i:i+1], span)
    v_s[:, :128] = v_ref[...]
    gk_s[...] = jnp.zeros_like(gk_s)
    gv_s[...] = jnp.zeros_like(gv_s)
    for a in range(S // SB):
        rs = slice(a*SB, (a+1)*SB)
        qa, qb = halves(q_ref[rs, :])
        qq = jnp.concatenate([qa, qb], 0)
        ga = ga_ref[rs, :]
        inv = inv_ref[rs, :]
        gw = (ga * inv).astype(BF16)
        gwa, gwb = halves(gw)
        pr = ga * att_ref[rs, :] * inv
        pa, pb = halves(pr)
        lane = lax.broadcasted_iota(jnp.int32, (SB, 128), 1)
        def ext(x):
            g = -jnp.sum(x, 1, keepdims=True)
            hi = g.astype(BF16)
            lo = (g - hi.astype(F32)).astype(BF16)
            z = jnp.zeros((SB, 128), BF16)
            return jnp.where(lane == 0, hi, jnp.where(lane == 1, lo, z))
        gg = jnp.concatenate([jnp.concatenate([gwa, ext(pa)], 1), jnp.concatenate([gwb, ext(pb)], 1)], 0)
        for c in range(0, span, CH):
            s = dot(qq, k_ref[a*SB+c:a*SB+c+CH, :], NT)
            g = dot(gg, v_s[a*SB+c:a*SB+c+CH, :], NT)
            m = mask_s[rs, c:c+CH]
            for h in range(2):
                hs = slice(h*SB, (h+1)*SB)
                cm = t_s[hs, c:c+CH] * m
                w = s[hs] * cm
                w_s[hs, c:c+CH] = w.astype(BF16)
                gs_s[hs, c:c+CH] = (g[hs] * cm).astype(BF16)
                pw = g[hs] * w
                if a == 0:
                    p_s[hs, c:c+CH] = pw
                else:
                    p_s[hs, c:c+CH] += pw
        gq = dot(gs_s[...], k_ref[a*SB:a*SB+span, :])
        gq_ref[rs, :] = pick(gq[:SB], gq[SB:])
        gk_s[:, a*SB:a*SB+span] += dot(qq, gs_s[...], TN)
        gwq = jnp.concatenate([gwa, gwb], 0)
        gv_s[:, a*SB:a*SB+span] += dot(gwq, w_s[...], TN)
    gk_ref[...] = gk_s[...].T
    gv_ref[...] = gv_s[...].T
    gb_ref[...] = jnp.concatenate([unskew(p_s[:SB, :], win), unskew(p_s[SB:, :], win), jnp.zeros((6, win), F32)], 0)

def attn_bwd(dq, dk, pk, bias8, q, k, v, att, inv, ga, CH=384):
    S, D = q.shape; KS = k.shape[0]; win = bias8.shape[1]; span = win + SB
    full = lambda *s: pl.BlockSpec(s, lambda p: (0,) * len(s))
    col = lambda n: pl.BlockSpec((n, 128), lambda p: (0, p))
    V = pltpu.VMEM
    return pl.pallas_call(
        functools.partial(bwd_kernel, CH),
        grid=(D // 128,),
        out_shape=(jax.ShapeDtypeStruct((S, D), F32), jax.ShapeDtypeStruct((KS, D), F32), jax.ShapeDtypeStruct((KS, D), F32),
                   jax.ShapeDtypeStruct(bias8.shape, F32)),
        in_specs=[full(S, 1), full(1, KS), full(1, KS), full(*bias8.shape), col(S), col(KS), col(KS), col(S), col(S), col(S)],
        out_specs=(col(S), col(KS), col(KS), pl.BlockSpec((8, win), lambda p: (p, 0))),
        scratch_shapes=[V((S, span), F32), V((2*SB, span), F32), V((2*SB, span), BF16), V((2*SB, span), BF16), V((2*SB, span), F32),
                        V((KS, 256), BF16), V((128, KS), F32), V((128, KS), F32)],
        compiler_params=pltpu.CompilerParams(vmem_limit_bytes=56 << 20),
        name="attn_bwd",
    )(dq, dk, pk, bias8, q, k, v, att, inv, ga)


MESH = pl.DeviceIdType.MESH
SLAB = 32


class Place:
    def __init__(self, n_seq):
        self.Z = n_seq // 4
        s, self.x = lax.axis_index("seq"), lax.axis_index("row")
        self.s = s
        self.c, self.y, self.z = lax.rem(s, 2), lax.rem(s // 2, 2), s // 4
        self.me = s * 2 + self.x

    def seq(self, z, y, c):
        return (z * 2 + y) * 2 + c

    def zx(self, k):
        z, d = self.z, 1
        while d <= k:
            if k // d % 2:
                z = z + d - 2 * d * lax.rem(self.z // d, 2)
            d *= 2
        return z

    def sibling(self):
        return (self.seq(self.z, self.y, 1 - self.c), self.x)

    def xpeer(self):
        return (self.s, 1 - self.x)

    def ypeer(self):
        return (self.seq(self.z, 1 - self.y, self.c), self.x)

    def zpeer(self, k):
        return (self.seq(self.zx(k), self.y, self.c), self.x)

    def partner(self):
        t, n = self.s - 1 + 2 * self.c, 4 * self.Z
        return (lax.rem(t + n, n), self.x), jnp.logical_and(t >= 0, t < n)

    def greet(self, partner):
        b = pltpu.get_barrier_semaphore()
        peers = [self.sibling(), self.xpeer(), self.ypeer()] + [self.zpeer(k) for k in range(1, self.Z)]
        if partner:
            peers.append(self.partner()[0])
        for p in peers:
            pl.semaphore_signal(b, inc=1, device_id=p, device_id_type=MESH)
        pl.semaphore_wait(b, len(peers))


def remote(src, dst, snd, rcv, dev):
    return pltpu.make_async_remote_copy(src_ref=src, dst_ref=dst, send_sem=snd, recv_sem=rcv, device_id=dev, device_id_type=MESH)


class Gather:
    def __init__(self, place, own, G, snd, rcv, chunks):
        self.p, self.own, self.G, self.snd, self.rcv, self.chunks = place, own, G, snd, rcv, chunks
        self.sent = []

    @staticmethod
    def sems(Z):
        return 5 * Z + 3

    def _copy(self, k, sem, at, dev, part=None, own=False):
        lo, n = part or self.chunks[k][:2]
        dst = self.G.at[at + (pl.ds(lo, n),)]
        src = self.own.at[pl.ds(lo, n)] if own else dst
        return remote(src, dst, self.snd.at[k, sem], self.rcv.at[k, sem], dev)

    def _send(self, *a, **kw):
        c = self._copy(*a, **kw)
        c.start()
        self.sent.append(c)

    def parts(self, k):
        r0, rows, h = self.chunks[k]
        return (r0, h), (r0 + h, rows - h)

    def at(self, j, fy=0, fx=0):
        p = self.p
        return (p.zx(j), p.y if not fy else 1 - p.y, p.c, p.x if not fx else 1 - p.x)

    def column(self, k, t, other=False):
        p = self.p
        y, x = (1 - p.y if t > 1 else p.y), (1 - p.x if t % 2 else p.x)
        return self._copy(k, 5 * p.Z - 1 + t, (slice(None), y, 1 - p.c if other else p.c, x), p.sibling())

    def give(self, k, t):
        c = self.column(k, t)
        c.start()
        self.sent.append(c)

    def bz(self, k):
        for j in range(1, self.p.Z):
            self._send(k, j - 1, self.at(0), self.p.zpeer(j), own=True)

    def bx(self, k):
        self._send(k, self.p.Z - 1, self.at(0), self.p.xpeer(), own=True)

    def by(self, k):
        self._send(k, 2 * self.p.Z - 1, self.at(0), self.p.ypeer(), own=True)

    def direct(self, k, j):
        p, (lo, n) = self.p, self.chunks[k][:2]
        for sem, dev in ((p.Z - 1 + j, p.xpeer()), (2 * p.Z - 1 + j, p.ypeer())):
            at = self.at(j) + (pl.ds(lo, n),)
            c = remote(self.own.at[p.zx(j), pl.ds(lo, n)], self.G.at[at], self.snd.at[k, sem], self.rcv.at[k, sem], dev)
            c.start()
            self.sent.append(c)

    def pzx(self, k):
        p, Z = self.p, self.p.Z
        for j in range(1, Z):
            self._copy(k, j - 1, self.at(j), p.zpeer(j)).wait_recv()
            self._send(k, Z - 1 + j, self.at(j), p.xpeer())
        self.give(k, 0)

    def pzy(self, k):
        for j in range(1, self.p.Z):
            self._send(k, 2 * self.p.Z - 1 + j, self.at(j), self.p.ypeer())

    def px(self, k):
        p, Z = self.p, self.p.Z
        a, b = self.parts(k)
        for j in range(Z):
            self._copy(k, Z - 1 + j, self.at(j, 0, 1), p.xpeer()).wait_recv()
            if a[1]:
                self._send(k, 3 * Z - 1 + j, self.at(j, 0, 1), p.ypeer(), a)
            self._copy(k, 2 * Z - 1 + j, self.at(j, 1, 0), p.ypeer()).wait_recv()
            if b[1]:
                self._send(k, 4 * Z - 1 + j, self.at(j, 1, 0), p.xpeer(), b)
        self.give(k, 1)
        self.give(k, 2)

    def pd(self, k):
        p, Z = self.p, self.p.Z
        a, b = self.parts(k)
        for j in range(Z):
            if a[1]:
                self._copy(k, 3 * Z - 1 + j, self.at(j, 1, 1), p.ypeer(), a).wait_recv()
            if b[1]:
                self._copy(k, 4 * Z - 1 + j, self.at(j, 1, 1), p.xpeer(), b).wait_recv()
        self.give(k, 3)

    def fin(self, k):
        for t in range(4):
            self.column(k, t, True).wait_recv()

    def drain(self):
        for c in self.sent:
            c.wait_send()
        self.sent = []


def play(steps, table):
    for step in steps:
        name = step.rstrip("0123456789")
        table[name](int(step[len(name):]))


class Scatter:
    def __init__(self, place, sib, own, R0, R1, R2, R3, snd, rcv, chunks):
        self.p, self.sib, self.own, self.R0, self.R1, self.R2, self.R3 = place, sib, own, R0, R1, R2, R3
        self.snd, self.rcv, self.chunks = snd, rcv, chunks
        self.sent = []

    @staticmethod
    def sems(Z):
        return 6 * Z - 1

    @staticmethod
    def buffers(Z, R, W):
        return [pltpu.VMEM((2 * Z, 2, R, W), BF16), pltpu.VMEM((Z, 2, R, W), BF16), pltpu.VMEM((Z, R, W), BF16), pltpu.VMEM((Z - 1, R, W), BF16)]

    def rows(self, k):
        return pl.ds(*self.chunks[k][:2])

    def parts(self, k):
        r0, n, h = self.chunks[k]
        return pl.ds(r0, h) if h else None, pl.ds(r0 + h, n - h) if h < n else None

    def _go(self, src, dst, k, sem, dev, start):
        c = remote(src, dst, self.snd.at[k, sem], self.rcv.at[k, sem], dev)
        if start:
            c.start()
            self.sent.append(c)
        else:
            c.wait_recv()

    def order(self):
        return list(range(self.p.Z - 1, -1, -1))

    def _c0(self, k, j, start):
        zy = pl.ds(2 * self.p.zx(j), 2)
        self._go(self.sib(k, zy), self.R0.at[zy, :, self.rows(k)], k, j, self.p.sibling(), start)

    def _c1(self, k, j, start):
        p = self.p
        z = p.zx(j)
        a, b = self.parts(k)
        if a is not None:
            self._go(self.R0.at[pl.ds(2 * z, 2), 1 - p.x, a], self.R1.at[z, :, a], k, p.Z + j, p.xpeer(), start)
        if b is not None:
            self._go(self.R0.at[2 * z + 1 - p.y, :, b], self.R1.at[z, :, b], k, 2 * p.Z + j, p.ypeer(), start)

    def _c2(self, k, j, start):
        p = self.p
        z = p.zx(j)
        a, b = self.parts(k)
        if a is not None:
            self._go(self.R1.at[z, 1 - p.y, a], self.R2.at[z, a], k, 3 * p.Z + j, p.ypeer(), start)
        if b is not None:
            self._go(self.R1.at[z, 1 - p.x, b], self.R2.at[z, b], k, 4 * p.Z + j, p.xpeer(), start)

    def _c3(self, k, j, start):
        r = self.rows(k)
        self._go(self.R2.at[self.p.zx(j), r], self.R3.at[j - 1, r], k, 5 * self.p.Z + j - 1, self.p.zpeer(j), start)

    def begin(self, k):
        for j in self.order():
            self._c0(k, j, True)

    @staticmethod
    def _add(dst, src):
        dst[...] = (dst[...].astype(F32) + src[...].astype(F32)).astype(BF16)

    def core(self, k, js=None):
        p = self.p
        for j in js or self.order():
            self._c0(k, j, False)
            z = p.zx(j)
            for y in range(2):
                for x in range(2):
                    self._add(self.R0.at[2 * z + y, x, self.rows(k)], self.own(k, 2 * z + y, x))
            self._c1(k, j, True)

    def one(self, k, js=None):
        p = self.p
        a, b = self.parts(k)
        for j in js or self.order():
            self._c1(k, j, False)
            z = p.zx(j)
            for i in range(2):
                if a is not None:
                    self._add(self.R1.at[z, i, a], self.R0.at[2 * z + i, p.x, a])
                if b is not None:
                    self._add(self.R1.at[z, i, b], self.R0.at[2 * z + p.y, i, b])
            self._c2(k, j, True)

    def two(self, k, js=None):
        p = self.p
        a, b = self.parts(k)
        for j in js or self.order():
            self._c2(k, j, False)
            z = p.zx(j)
            if a is not None:
                self._add(self.R2.at[z, a], self.R1.at[z, p.y, a])
            if b is not None:
                self._add(self.R2.at[z, b], self.R1.at[z, p.x, b])
            if j:
                self._c3(k, j, True)

    def finish(self, k):
        p, r = self.p, self.rows(k)
        total = self.R2[p.z, r].astype(F32)
        for j in range(1, p.Z):
            self._c3(k, j, False)
            total = total + self.R3[j - 1, r].astype(F32)
        return total

    def drain(self):
        for c in self.sent:
            c.wait_send()
        self.sent = []


class SumAll:
    def __init__(self, place, cur, got, snd, rcv):
        self.p, self.cur, self.got, self.snd, self.rcv = place, cur, got, snd, rcv
        p = place
        self.peers = [p.sibling(), p.xpeer(), p.ypeer()]
        d = 1
        while d < p.Z:
            self.peers.append(p.zpeer(d))
            d *= 2

    @staticmethod
    def steps(Z):
        return 3 + (Z - 1).bit_length()

    def _copy(self, i):
        return remote(self.cur.at[i], self.got.at[i], self.snd.at[i], self.rcv.at[i], self.peers[i])

    def start(self, i):
        self._copy(i).start()

    def step(self, i):
        self._copy(i).wait()
        self.cur[i + 1] = self.cur[i] + self.got[i]


def dma(*shape):
    return pltpu.SemaphoreType.DMA(shape)


def vmem(*n):
    return [pl.BlockSpec(memory_space=pltpu.VMEM)] * (n[0] if n else 1)


def doc_numbers(len_ref, pos):
    ends, count = jnp.int32(0), jnp.zeros(pos.shape, jnp.int32)
    for i in range(len_ref.shape[1]):
        ends = ends + len_ref[0, i]
        count = count + jnp.where(pos >= ends, 1, 0)
    return jnp.where(pos < 0, -1, count)


def fill_band(mask_s, len_ref, pk, start, half):
    S, span = mask_s.shape
    KS = pk.shape[1]
    dk = doc_numbers(len_ref, start - half + lax.broadcasted_iota(jnp.int32, (1, KS), 1))
    for a in range(S // SB):
        dq = doc_numbers(len_ref, start + a * SB + lax.broadcasted_iota(jnp.int32, (SB, 1), 0))
        r = lax.broadcasted_iota(jnp.int32, (SB, span), 0)
        c = lax.broadcasted_iota(jnp.int32, (SB, span), 1)
        ok = (dq == dk[:, a * SB:a * SB + span]) & ((pk[:, a * SB:a * SB + span] == 1) | (c == r + half))
        mask_s[a * SB:(a + 1) * SB, :] = jnp.where(ok, 1.0, 0.0)


def fill_features(dm_s, draws_ref):
    m, d = draws_ref.shape[1:]
    z = jnp.zeros((m, d), F32)
    for i in range(draws_ref.shape[0] // 2):
        full = jnp.concatenate([jnp.concatenate([draws_ref[2 * i], z], 1), jnp.concatenate([z, draws_ref[2 * i + 1]], 1)], 0)
        dm_s[0, i], dm_s[1, i] = split2(full)


def ones_per_head():
    lane = lax.broadcasted_iota(jnp.int32, (256, 128), 1) // 64
    row = lax.rem(lax.broadcasted_iota(jnp.int32, (256, 128), 0) // 64, 2)
    return jnp.where(lane == row, 1.0, 0.0).astype(BF16)


def split2(x):
    hi = x.astype(BF16)
    return hi, (x - hi.astype(F32)).astype(BF16)


def coefs(bias_ref, i, t_s, span):
    for h in range(2):
        t_s[h * SB:(h + 1) * SB, :] = toep(jnp.exp(bias_ref[pl.ds(2 * i + h, 1), :]), span)


FORWARD = (
    "bx1", "by0", "bx2", "bx0", "bz0", "bz1", "by1", "by2", "bz2", "bz3", "pzx0", "pzy0", "px0", "bz4", "pzx1", "pzy1", "by3",
    "pd0", "H0", "px1", "pzx2", "pzy2", "pd1", "fin0", "pre0", "bx5", "bx4", "bx3", "po0", "bz5", "px2", "fin1", "po1", "pzx4",
    "pzx3", "pzy3", "pd2", "fin2", "pzx5", "po2", "KV0", "dz0", "hw0", "px3", "mask0", "by4", "kvw0", "pzy4", "by5", "rim0", "pr0",
    "px4", "pzy5", "rim1", "pr1", "pd3", "px5", "pd4", "rim2", "pr2", "pd5", "fin4", "fin3", "fin5", "uo0", "uu0", "uu1", "dw0",
)
CUT_FORWARD = (0, 0, 0, 0, 0, 0)


def phi(z, dh, dl, on, scale):
    s = z * scale
    sh, sl = split2(s)
    rows = dot(jnp.concatenate([sh, sl], 1), jnp.concatenate([dh, dh], 1), NT) + dot(sh, dl, NT)
    half = dot(jnp.concatenate(split2(s * s * 0.5), 1), on)
    return jnp.exp(rows - half) * (dh.shape[0] // 2) ** -0.5


def fwd_attend(S, span, i, bias_ref, q_s, k_s, v_s, mask_s, t_s, w_s, vv_s, att_ref, inv_ref):
    lanes = pl.ds(pl.multiple_of(i * 128, 128), 128)
    CH = span // 3
    coefs(bias_ref, i, t_s, span)
    vv_s[:, :128] = v_s[:, lanes]
    for a in range(S // SB):
        rs = slice(a * SB, (a + 1) * SB)
        qq = jnp.concatenate(halves(q_s[S + a * SB:S + (a + 1) * SB, lanes]), 0)
        for c in range(0, span, CH):
            s = dot(qq, k_s[a * SB + c:a * SB + c + CH, lanes], NT)
            m = mask_s[rs, c:c + CH]
            for h in range(2):
                hs = slice(h * SB, (h + 1) * SB)
                w_s[hs, c:c + CH] = (s[hs] * (t_s[hs, c:c + CH] * m)).astype(BF16)
        o = dot(w_s[...], vv_s[a * SB:a * SB + span, :])
        inv = 1.0 / pick(o[:SB, 128:], o[SB:, 128:])
        att_ref[rs, lanes] = pick(o[:SB, :128], o[SB:, :128]) * inv
        inv_ref[rs, lanes] = inv


def forward_kernel(n_seq, chunks, scale, wq_ref, wo_ref, wu_ref, wd_ref, b3_ref, b4_ref, b1_ref, x_ref, pad_ref, bias_ref, draws_ref, len_ref,
                   qkv_h, out_h, up_h, zq_h, zk_h, q_h, k_h, v_h, att_h, inv_h, vec_ref, pk_ref, col_ref,
                   qkv_ref, out_ref, up_ref, zq_ref, zk_ref, q_ref, k_ref, v_ref, att_ref, inv_ref,
                   own_s, G, XR, P3, pad_s, mask_s, t_s, w_s, vv_s, dm_s, snd, rcv, hsnd, hrcv, dsnd, drcv, osem):
    S, W = x_ref.shape
    f = wo_ref.shape[0]
    win = bias_ref.shape[1]
    span = win + SB
    wide = 256
    p = Place(n_seq)
    g = Gather(p, own_s, G, snd, rcv, chunks)

    def placed(v, n):
        return pltpu.roll(jnp.broadcast_to(v, (8, v.shape[1])), p.me * n, 1)[:1]

    def thirds(v, j):
        return jnp.concatenate([v[:, t * W + j * wide:t * W + (j + 1) * wide] for t in range(3)], 1)

    wq = wq_ref[...].astype(F32)
    b3 = placed(b3_ref[...], 3 * f)
    b4 = placed(b4_ref[...], 4 * f)
    singles = pltpu.roll(b1_ref[...], p.me * f, 1)
    rest = [[b4[:, j * W:(j + 1) * W] for j in range(4)] + [singles[0:3]], [singles[3:6], jnp.zeros((4, W), F32)], [jnp.zeros((7, W), F32)]]
    for j in range(3):
        own_s[j * SLAB:(j + 1) * SLAB, :] = jnp.concatenate([thirds(wq, j), thirds(b3, j)] + rest[j], 0).astype(BF16)
    wide_up = [wu_ref[:, j * W:(j + 1) * W].astype(F32) for j in range(4)]
    own_s[3 * SLAB:4 * SLAB, :] = jnp.concatenate([wo_ref[...].astype(F32), jnp.zeros((SLAB - f, W), F32)], 0).astype(BF16)
    own_s[4 * SLAB:, :] = jnp.concatenate(wide_up, 0).astype(BF16)
    pad_s[...] = jnp.broadcast_to(pad_ref[...], pad_s.shape)
    p.greet(True)
    partner, has = p.partner()
    mine, theirs = 2 * p.c, 2 - 2 * p.c
    leaving = []

    def leave(src, dst):
        c = pltpu.make_async_copy(src, dst, osem.at[len(leaving)])
        c.start()
        leaving.append(c)

    halo = (remote(x_ref, XR, hsnd.at[0], hrcv.at[0], partner), remote(pad_s, P3.at[theirs], hsnd.at[1], hrcv.at[1], partner))
    halo_in = remote(pad_s, P3.at[mine], hsnd.at[1], hrcv.at[1], partner)
    pads = remote(pad_s, P3.at[mine], hsnd.at[2], hrcv.at[2], p.sibling())
    pads_in = remote(pad_s, P3.at[theirs], hsnd.at[2], hrcv.at[2], p.sibling())
    own_rows, far, near = pl.ds(S, S), pl.ds(pl.multiple_of(mine * S, S), S), pl.ds(pl.multiple_of(theirs * S, S), S)
    given = [remote(r.at[own_rows], r.at[far], hsnd.at[3 + i], hrcv.at[3 + i], p.sibling()) for i, r in enumerate((k_ref, v_ref, q_ref))]
    taken = [remote(r.at[own_rows], r.at[near], hsnd.at[3 + i], hrcv.at[3 + i], p.sibling()) for i, r in enumerate((k_ref, v_ref, q_ref))]
    pads.start()

    def send_halo(_):
        @pl.when(has)
        def _():
            for h in halo:
                h.start()

    def take_halo(_):
        @pl.when(has)
        def _():
            halo[0].wait_recv()
            halo_in.wait_recv()

        @pl.when(jnp.logical_not(has))
        def _():
            XR[...] = jnp.zeros_like(XR)
            P3[mine] = jnp.zeros(pad_s.shape, jnp.int32)

    G[p.z, p.y, p.c, p.x] = own_s[...]
    P3[1] = pad_s[...]

    def down(j):
        return remote(wd_ref, col_ref.at[p.z], dsnd.at[j - 1], drcv.at[j - 1], p.zpeer(j))

    def down_in(j):
        return remote(wd_ref, col_ref.at[p.zx(j)], dsnd.at[j - 1], drcv.at[j - 1], p.zpeer(j))

    def send_down(_):
        for j in range(1, p.Z):
            down(j).start()

    def take_down(_):
        for j in range(1, p.Z):
            down_in(j).wait_recv()

    col_ref[p.z] = wd_ref[...]

    def early(_):
        fill_features(dm_s, draws_ref)
        vv_s[:, 128:] = jnp.ones((vv_s.shape[0], 128), BF16)

    on = ones_per_head()

    def features(z, i):
        return phi(z, dm_s[0, i], dm_s[1, i], on, scale).astype(BF16)

    def project(j):
        cs = slice(j * wide, (j + 1) * wide)
        unpack_qkv(g, j, qkv_ref, vec_ref)
        bias = vec_ref[8 * j:8 * j + 1, :]
        x = x_ref[...]
        zq = dot(x, qkv_ref[j, :, :wide]) + bias[:, :wide]
        zk = dot(x, qkv_ref[j, :, wide:2 * wide]) + bias[:, wide:2 * wide]
        zq_ref[:, cs] = zq
        zk_ref[:, cs] = zk
        for i in range(wide // 128):
            pp, at = wide // 128 * j + i, slice(i * 128, (i + 1) * 128)
            lanes = slice(pp * 128, (pp + 1) * 128)
            q_ref[S:2 * S, lanes] = features(zq[:, at], pp)
            k_ref[S:2 * S, lanes] = features(zk[:, at], pp)
        v_ref[S:2 * S, cs] = (dot(x, qkv_ref[j, :, 2 * wide:]) + bias[:, 2 * wide:]).astype(BF16)
        leave(qkv_ref.at[j], qkv_h.at[j])
        for a, b in ((zq_ref, zq_h), (zk_ref, zk_h)):
            leave(a.at[:, cs], b.at[:, cs])

    def give(_):
        for c in given:
            c.start()

    def band(_):
        pads_in.wait_recv()
        pk_ref[...] = jnp.concatenate([P3[0, :1], P3[1, :1], P3[2, :1]], 1)
        fill_band(mask_s, len_ref, pk_ref[...], p.s * S, win // 2)

    def rim(j):
        cs = slice(j * wide, (j + 1) * wide)
        bias = vec_ref[8 * j:8 * j + 1, :]
        x = XR[...]
        zq = dot(x, qkv_ref[j, :, :wide]) + bias[:, :wide]
        zk = dot(x, qkv_ref[j, :, wide:2 * wide]) + bias[:, wide:2 * wide]
        for i in range(wide // 128):
            pp = wide // 128 * j + i
            q_ref[far, pp * 128:(pp + 1) * 128] = features(zq[:, i * 128:(i + 1) * 128], pp)
            k_ref[far, pp * 128:(pp + 1) * 128] = features(zk[:, i * 128:(i + 1) * 128], pp)
        v_ref[far, cs] = (dot(x, qkv_ref[j, :, 2 * wide:]) + bias[:, 2 * wide:]).astype(BF16)
        if j == 2:
            for a, b in ((q_ref, q_h), (k_ref, k_h), (v_ref, v_h)):
                leave(a, b)

    def take(_):
        for c in taken:
            c.wait_recv()

    def pairs(j):
        def pair(i, _):
            fwd_attend(S, span, i, bias_ref, q_ref, k_ref, v_ref, mask_s, t_s, w_s, vv_s, att_ref, inv_ref)
            return 0

        lax.fori_loop(2 * j, 2 * j + 2, pair, 0)
        cs = slice(j * wide, (j + 1) * wide)
        for a, b in ((att_ref, att_h), (inv_ref, inv_h)):
            leave(a.at[:, cs], b.at[:, cs])

    def unpack_up(i):
        k = 4 + i
        lo, n, _ = chunks[k]
        first = (lo - 4 * SLAB) // f

        def put(at, j, v):
            up_ref[at, (first + j) * W:(first + j + 1) * W] = v

        shard_pairs(G, lo, n, f, put)
        cs = slice(first * W, first * W + n // f * W)
        leave(up_ref.at[:, cs], up_h.at[:, cs])

    def unpack_out(_):
        def put(at, j, v):
            out_ref[at, :] = v

        shard_pairs(G, 3 * SLAB, f, f, put)
        leave(out_ref, out_h)

    play(FORWARD, dict(
        bx=g.bx, by=g.by, bz=g.bz, pzx=g.pzx, pzy=g.pzy, px=g.px, pd=g.pd, fin=g.fin, H=send_halo, hw=take_halo, pre=early, po=project,
        KV=give, kvw=take, mask=band, rim=rim, pr=pairs, uo=unpack_out, uu=unpack_up, dz=send_down, dw=take_down))

    @pl.when(has)
    def _():
        for h in halo:
            h.wait_send()
    for c in given + [pads] + [down(j) for j in range(1, p.Z)]:
        c.wait_send()
    g.drain()
    for c in leaving:
        c.wait()


def shard_pairs(G, lo, n, f, put):
    def one(s, _):
        full = pl.ds(lo, (n + 15) // 16 * 16)
        at = (s // 4, lax.rem(s // 2, 2), lax.rem(s, 2))
        a, b = (G[at + (x, full)].astype(F32) for x in range(2))
        rows = pl.ds(pl.multiple_of(s * 2 * f, 2 * f), 2 * f)
        for j in range(n // f):
            put(rows, j, jnp.concatenate([a[j * f:(j + 1) * f], b[j * f:(j + 1) * f]], 0).astype(BF16))
        return 0

    lax.fori_loop(0, 4 * G.shape[0], one, 0)


def unpack_qkv(g, j, qkv_ref, vec_ref):
    G = g.G
    f = qkv_ref.shape[1] // (8 * G.shape[0])
    lo = j * SLAB

    def one(s, t):
        at = (s // 4, lax.rem(s // 2, 2), lax.rem(s, 2))
        a, b = (G[at + (x, pl.ds(lo, SLAB))].astype(F32) for x in range(2))
        qkv_ref[j, pl.ds(pl.multiple_of(s * 2 * f, 2 * f), 2 * f), :] = jnp.concatenate([a[:f], b[:f]], 0).astype(BF16)
        return t + a[f:] + b[f:]

    vec_ref[8 * j:8 * j + 8, :] = lax.fori_loop(0, 4 * G.shape[0], one, jnp.zeros((SLAB - f, G.shape[-1]), F32))


def forward(n_seq, wq, wo, wu, wd, b3, b4, b1, x, pad, bias, draws, lens):
    S, W = x.shape
    f = wo.shape[0]
    win = bias.shape[1]
    span = win + SB
    KS = S + win
    Z = n_seq // 4
    R = 4 * SLAB + 4 * f
    chunks = tuple((SLAB * k, SLAB, CUT_FORWARD[k]) for k in range(4)) + tuple((4 * SLAB + 2 * f * k, 2 * f, CUT_FORWARD[4 + k]) for k in range(2))
    V = pltpu.VMEM
    M = Gather.sems(Z)
    D = f * 2 * n_seq
    sd = jax.ShapeDtypeStruct
    heads, feats, dims = draws.shape
    K = len(chunks)
    large = (sd((3, D, W), BF16), sd((D, W), BF16), sd((D, 4 * W), BF16), sd((S, W), F32), sd((S, W), F32),
             sd((KS, W), BF16), sd((KS, W), BF16), sd((KS, W), BF16), sd((S, W), F32), sd((S, W), F32))
    return pl.pallas_call(
        functools.partial(forward_kernel, n_seq, chunks, dims ** -0.25),
        out_shape=large + (sd((24, W), F32), sd((1, KS), jnp.int32), sd((Z, 4 * f, W), BF16)),
        in_specs=vmem(11) + [pl.BlockSpec(memory_space=pltpu.SMEM)], out_specs=(pl.BlockSpec(memory_space=pl.ANY),) * len(large) + tuple(vmem(3)),
        scratch_shapes=[V(s.shape, s.dtype) for s in large] + [
            V((R, W), BF16), V((Z, 2, 2, 2, R, W), BF16), V((S, W), BF16), V((3, 8, S), jnp.int32), V((8, S), jnp.int32),
            V((S, span), F32), V((2 * SB, span), F32), V((2 * SB, span), BF16), V((KS, 256), BF16),
            V((2, heads // 2, 2 * feats, 2 * dims), BF16), dma(K, M), dma(K, M), dma(6), dma(6), dma(Z - 1), dma(Z - 1), dma(24)],
        compiler_params=pltpu.CompilerParams(collective_id=1, has_side_effects=True, vmem_limit_bytes=60 << 20),
        name="forward",
    )(wq, wo, wu, wd, b3, b4, b1, x, pad, bias, draws, lens)


DOWN_PARTS = 3
CUT_DOWN = 16


def lane_mean(v):
    return jnp.mean(v, 1, keepdims=True)


def rows_loop(total, step, body):
    def one(i, c):
        body(pl.ds(pl.multiple_of(i * step, step), step))
        return c

    lax.fori_loop(0, total // step, one, 0)


def fold8(v):
    return jnp.sum(v.reshape(v.shape[0] // 8, 8, v.shape[1]), 0)


def normal_cdf_pdf(x):
    u = jnp.abs(x) * 0.7071067811865476
    t = 1.0 / (1.0 + 0.3275911 * u)
    e = jnp.exp(-0.5 * x * x)
    poly = t * (0.254829592 + t * (-0.284496736 + t * (1.421413741 + t * (-1.453152027 + t * 1.061405429))))
    tail = 0.5 * poly * e
    return jnp.where(x >= 0, 1.0 - tail, tail), e * 0.3989422804014327


def middle_kernel(n_seq, heads, col_ref, x_ref, vec_ref, ct_h, att_h, inv_h, ow_h, up_h, out_ref, g1_ref, gw_ref, gt_ref, vg_ref, P_h,
                  ct_ref, att_ref, inv_ref, ow_ref, up_ref, P_ref,
                  al_s, hl_s, hlt_s, h1_s, n1_s, i1_s, act_s, dg_s, gi_s, r_s, gl_s, acc_s, G, snd, rcv, lsem, osem):
    S, W = x_ref.shape
    FF_ = up_ref.shape[1]
    n_dev = P_ref.shape[0]
    f = W // n_dev
    RB = 64
    p = Place(n_seq)
    loads = [pltpu.make_async_copy(a, b, lsem.at[i]) for i, (a, b) in enumerate(
        ((att_h, att_ref), (ow_h, ow_ref), (up_h, up_ref), (ct_h, ct_ref), (inv_h, inv_ref)))]
    for c in loads:
        c.start()
    part = 4 * f // DOWN_PARTS
    g = Gather(p, col_ref, G, snd, rcv, tuple((part * k, part, CUT_DOWN) for k in range(DOWN_PARTS)))
    p.greet(False)
    G[:, p.y, p.c, p.x] = col_ref[...]
    for k in range(DOWN_PARTS):
        for j in range(p.Z):
            g.direct(k, j)
    for k in range(DOWN_PARTS):
        g.give(k, 0)
    b_out, gain_a, shift_a, b_down, gain_f, shift_f = (vec_ref[i:i + 1] for i in (5, 6, 7, 9, 10, 11))
    acc_s[...] = jnp.zeros_like(acc_s)

    def cast(rs):
        al_s[rs, :] = att_ref[rs, :].astype(BF16)

    loads[0].wait()
    rows_loop(S, RB, cast)
    loads[1].wait()
    r_s[...] = dot(al_s[...], ow_ref[...])

    def norm_one(rs):
        r = r_s[rs, :] + (x_ref[rs, :].astype(F32) + b_out)
        c = r - lane_mean(r)
        inv = lax.rsqrt(lane_mean(c * c) + EPS)
        n = c * inv
        n1_s[rs, :] = n
        i1_s[rs, :] = jnp.broadcast_to(inv, (RB, 128))
        h = n * gain_a + shift_a
        h1_s[rs, :] = h
        hl_s[rs, :] = h.astype(BF16)

    rows_loop(S, RB, norm_one)
    loads[2].wait()
    hlt_s[...] = hl_s[...].T
    CW = W // 2
    between = {1: ((g.px, 0),), 2: ((g.px, 1),), 3: ((g.px, 2),), 5: ((g.pd, 0),), 6: ((g.pd, 1),), 7: ((g.pd, 2),)}
    for j in range(FF_ // CW):
        cs = slice(j * CW, (j + 1) * CW)
        inner = dot(hl_s[...], up_ref[:, cs]) + vec_ref[1 + j // 2:2 + j // 2, j % 2 * CW:(j % 2 + 1) * CW]
        cdf, pdf = normal_cdf_pdf(inner)
        act_s[:, cs] = (inner * cdf).astype(BF16)
        dg_s[:, cs] = cdf + inner * pdf
        for step, k in between.get(j, ()):
            step(k)
    for k in range(DOWN_PARTS):
        g.fin(k)
    r_s[...] = dot(act_s[...], G[...].reshape(FF_, W))

    def norm_two(rs):
        r = r_s[rs, :] + (h1_s[rs, :] + b_down)
        c = r - lane_mean(r)
        inv = lax.rsqrt(lane_mean(c * c) + EPS)
        n = c * inv
        out_ref[rs, :] = (n * gain_f + shift_f).astype(BF16)
        ct = ct_ref[rs, :].astype(F32)
        acc_s[0] += fold8(ct * n)
        acc_s[1] += fold8(ct)
        gy = ct * gain_f
        gr = inv * (gy - lane_mean(gy) - n * lane_mean(gy * n))
        r_s[rs, :] = gr
        gl = gr.astype(BF16)
        gl_s[rs, :] = gl
        acc_s[2] += fold8(gl.astype(F32))

    loads[3].wait()
    rows_loop(S, RB, norm_two)
    block = FF_ // p.Z

    def leave(i, lo, n):
        rows = pl.ds(lo, n)
        c = pltpu.make_async_copy(P_ref.at[:, rows], P_h.at[:, rows], osem.at[i])
        c.start()
        leaving.append(c)

    leaving = []
    per = n_dev // p.Z
    for j in range(p.Z):
        gd = dot(act_s[:, j * block:(j + 1) * block], gl_s[...], TN)
        P_ref[j * per:(j + 1) * per, :4 * f, :] = gd.reshape(per, 4 * f, W).astype(BF16)
    leave(0, 0, 4 * f)
    vg_ref[...] = jnp.zeros_like(vg_ref)
    for j in range(p.Z):
        cs = slice(j * block, (j + 1) * block)
        gi = (dot(gl_s[...], G[j].reshape(block, W), NT) * dg_s[:, cs]).astype(BF16)
        gi_s[:, cs] = gi
    for j in range(FF_ // W):
        vg_ref[1 + j:2 + j, :] = jnp.sum(gi_s[:, j * W:(j + 1) * W].astype(F32), 0, keepdims=True)
    for i in range(2):
        parts = [dot(hlt_s[...], gi_s[:, k * W:(k + 1) * W]).reshape(n_dev, f, W) for k in (2 * i, 2 * i + 1)]
        P_ref[:, 4 * f + 2 * f * i:4 * f + 2 * f * (i + 1), :] = jnp.concatenate(parts, 1).astype(BF16)
        leave(1 + i, 4 * f + 2 * f * i, 2 * f)
    r_s[...] += dot(gi_s[...], up_ref[...], NT)

    def back_one(rs):
        gr = r_s[rs, :]
        n = n1_s[rs, :]
        acc_s[3] += fold8(gr * n)
        acc_s[4] += fold8(gr)
        gy = gr * gain_a
        inv = i1_s[rs, :1]
        go = inv * (gy - lane_mean(gy) - n * lane_mean(gy * n))
        g1_ref[rs, :] = go
        gl = go.astype(BF16)
        gl_s[rs, :] = gl
        acc_s[5] += fold8(gl.astype(F32))

    rows_loop(S, RB, back_one)
    for row, i in ((10, 0), (11, 1), (9, 2), (6, 3), (7, 4), (5, 5)):
        vg_ref[row:row + 1, :] = jnp.sum(acc_s[i], 0, keepdims=True)
    go = dot(al_s[...], gl_s[...], TN).reshape(n_dev, f, W)
    P_ref[:, 8 * f:, :] = jnp.concatenate([go, jnp.zeros((n_dev, SLAB - f, W), F32)], 1).astype(BF16)
    leave(3, 8 * f, SLAB)
    r_s[...] = dot(gl_s[...], ow_ref[...], NT)
    of_head = lax.broadcasted_iota(jnp.int32, (W, 128), 0) // (W // heads) == lax.broadcasted_iota(jnp.int32, (W, 128), 1)
    of_head = jnp.where(of_head, 1.0, 0.0).astype(BF16)

    def weighted(rs):
        g = r_s[rs, :] * inv_ref[rs, :]
        gw_ref[rs, :] = g.astype(BF16)
        hi, lo = split2(g * att_ref[rs, :])
        total = -(dot(hi, of_head) + dot(lo, of_head))
        hi = total.astype(BF16).astype(F32)
        gt_ref[rs, :] = (hi + pltpu.roll(total - hi, heads, 1)).astype(BF16)

    loads[4].wait()
    rows_loop(S, 2 * RB, weighted)
    g.drain()
    for c in leaving:
        c.wait()


def middle(n_seq, heads, col, x, ct, att, inv, ow, up, vec):
    S, W = x.shape
    FF_ = up.shape[1]
    n_dev = 2 * n_seq
    f = W // n_dev
    Z = n_seq // 4
    V = pltpu.VMEM
    sd = jax.ShapeDtypeStruct
    return pl.pallas_call(
        functools.partial(middle_kernel, n_seq, heads),
        out_shape=(sd((S, W), BF16), sd((S, W), F32), sd((S, W), BF16), sd((S, 128), BF16), sd((24, W), F32), sd((n_dev, 8 * f + SLAB, W), BF16)),
        in_specs=vmem(3) + [pl.BlockSpec(memory_space=pl.ANY)] * 5, out_specs=tuple(vmem(5)) + (pl.BlockSpec(memory_space=pl.ANY),),
        scratch_shapes=[V((S, W), BF16), V((S, W), F32), V((S, W), F32), V((W, W), BF16), V((W, FF_), BF16), V((n_dev, 8 * f + SLAB, W), BF16),
                        V((S, W), BF16), V((S, W), BF16), V((W, S), BF16), V((S, W), F32), V((S, W), F32), V((S, 128), F32),
                        V((S, FF_), BF16), V((S, FF_), F32), V((S, FF_), BF16), V((S, W), F32), V((S, W), BF16), V((6, 8, W), F32),
                        V((Z, 2, 2, 2, 4 * f, W), BF16), dma(DOWN_PARTS, Gather.sems(Z)), dma(DOWN_PARTS, Gather.sems(Z)), dma(5), dma(4)],
        compiler_params=pltpu.CompilerParams(collective_id=2, has_side_effects=True, vmem_limit_bytes=60 << 20),
        name="middle",
    )(col, x, vec, ct, att, inv, ow, up)


BACKWARD = (
    "H0", "b3", "b0", "b1", "pre0", "c0", "b4", "pr2", "c1", "o0", "b2", "c2", "pr1", "pr0", "hw0", "o1", "v0", "c3", "ri0",
    "t0", "o2", "t1", "pj0", "c4", "b5", "o3", "ri1", "t2", "c5", "pj1", "v1", "b6", "o4", "f1", "t3", "o5", "c6", "f0", "ri2",
    "t4", "pj2", "b7", "v2", "t5", "o6", "c7", "t6", "v3", "f3", "o7", "t7", "f5", "v4", "f6", "f2", "f4", "gx0", "f7", "v5",
)
CUT_BACKWARD = (32, 32, 32, 32, 16, 16, 16, 16)


def head_rows(gw, gt, i, heads):
    lane = lax.broadcasted_iota(jnp.int32, gt.shape, 1)
    rows = []
    for h, g in enumerate(halves(gw)):
        mine = jnp.logical_or(lane == 2 * i + h, lane == 2 * i + h + heads)
        rows.append(jnp.concatenate([g, jnp.where(mine, gt, jnp.zeros_like(gt))], 1))
    return jnp.concatenate(rows, 0)


def back_own(S, span, win, heads, i, bias_ref, q_ref, k_ref, v_ref, gw_s, gt_s, mask_s, t_s, w_s, gs_s, p_s, vv_s, gkt_s, gvt_s, gq_s, bsum):
    lanes = pl.ds(pl.multiple_of(i * 128, 128), 128)
    CH = span // 3
    half = win // 2
    coefs(bias_ref, i, t_s, span)
    vv_s[:, :128] = v_ref[:, lanes]
    for a in range(S // SB):
        rs, qs = slice(a * SB, (a + 1) * SB), slice(S + a * SB, S + (a + 1) * SB)
        qq = jnp.concatenate(halves(q_ref[qs, lanes]), 0)
        gg = head_rows(gw_s[qs, lanes], gt_s[qs, :], i, heads)
        for c in range(0, span, CH):
            s = dot(qq, k_ref[a * SB + c:a * SB + c + CH, lanes], NT)
            g = dot(gg, vv_s[a * SB + c:a * SB + c + CH, :], NT)
            m = mask_s[rs, c:c + CH]
            for h in range(2):
                hs = slice(h * SB, (h + 1) * SB)
                cm = t_s[hs, c:c + CH] * m
                w = s[hs] * cm
                w_s[hs, c:c + CH] = w.astype(BF16)
                gs_s[hs, c:c + CH] = (g[hs] * cm).astype(BF16)
                pw = g[hs] * w
                if a == 0:
                    p_s[hs, c:c + CH] = pw
                else:
                    p_s[hs, c:c + CH] += pw
        gq = dot(gs_s[...], k_ref[a * SB:a * SB + span, lanes])
        gq_s[rs, lanes] = pick(gq[:SB], gq[SB:])
        cols = slice(half - a * SB, half - a * SB + S)
        gk, gv = dot(qq, gs_s[:, cols], TN), dot(gg[:, :128], w_s[:, cols], TN)
        if a == 0:
            gkt_s[i], gvt_s[i] = gk, gv
        else:
            gkt_s[i] += gk
            gvt_s[i] += gv
    for h in range(2):
        bsum[pl.ds(2 * i + h, 1), :] = unskew(p_s[h * SB:(h + 1) * SB, :], win)


def back_rim(S, span, heads, i, bias_ref, q_ref, k_ref, v_ref, gw_s, gt_s, maskr_s, t_s, w_s, gs_s, vv_s, gkt_s, gvt_s):
    lanes = pl.ds(pl.multiple_of(i * 128, 128), 128)
    coefs(bias_ref, i, t_s, span)
    vv_s[S:2 * S, :128] = v_ref[S:2 * S, lanes]
    for a in range(S // SB):
        for side, (k0, k1, t0) in enumerate(((0, (a + 1) * SB, span - (a + 1) * SB), (a * SB, S, 0))):
            n = k1 - k0
            qs = slice(2 * S * side + a * SB, 2 * S * side + (a + 1) * SB)
            qq = jnp.concatenate(halves(q_ref[qs, lanes]), 0)
            gg = head_rows(gw_s[qs, lanes], gt_s[qs, :], i, heads)
            s = dot(qq, k_ref[S + k0:S + k1, lanes], NT)
            g = dot(gg, vv_s[S + k0:S + k1, :], NT)
            m = maskr_s[side, a * SB:(a + 1) * SB, k0:k1]
            for h in range(2):
                hs = slice(h * SB, (h + 1) * SB)
                cm = t_s[hs, t0:t0 + n] * m
                w_s[hs, :n] = (s[hs] * cm).astype(BF16)
                gs_s[hs, :n] = (g[hs] * cm).astype(BF16)
            gkt_s[i, :, k0:k1] += dot(qq, gs_s[:, :n], TN)
            gvt_s[i, :, k0:k1] += dot(gg[:, :128], w_s[:, :n], TN)


def phi_back(g, feat, z, dh, dl, on, scale):
    t = g * feat.astype(F32)
    th, tl = split2(t)
    back = dot(th, dh) + dot(tl, dh) + dot(th, dl)
    total = dot(jnp.concatenate([th, tl], 1), on)
    return scale * (back - (z * scale) * total)


def backward_kernel(n_seq, chunks, scale, x_ref, pk_ref, bias_ref, draws_ref, len_ref, vg_ref, gw_ref, gt_ref,
                    w_h, q_h, k_h, v_h, zq_h, zk_h, g1_h, P_h,
                    gx_ref, rel_ref, gqkv_ref, gup_ref, gdown_ref, gout_ref, small_ref,
                    w_ref, q_ref, k_ref, v_ref, zq_ref, zk_ref,
                    U, PQ, R0, R1, R2, R3, mask_s, maskr_s, t_s, w_s, gs_s, p_s, vv_s, gkt_s, gvt_s, gq_s, gw_s, gt_s, gp_s, xt_s, dm_s, ex_s,
                    cur, got, snd, rcv, hsnd, hrcv, vsnd, vrcv, lsem):
    S, W = x_ref.shape
    heads, win = bias_ref.shape
    span = win + SB
    n_pair = W // 128
    n_dev = 2 * n_seq
    f = W // n_dev
    wide = 256
    p = Place(n_seq)
    partner, has = p.partner()
    mine, theirs = 2 * p.c, 2 - 2 * p.c
    far, near = pl.ds(pl.multiple_of(mine * S, S), S), pl.ds(pl.multiple_of(theirs * S, S), S)

    def load(src, dst, i):
        return pltpu.make_async_copy(src, dst, lsem.at[i])

    def own_half(k):
        r0, n = chunks[k][:2]
        return load(P_h.at[:, p.c, :, pl.ds(r0, n)], U.at[k % 2, :, :, pl.ds(0, n)], 1 + k % 2)

    residual = load(g1_h, gx_ref, 0)
    early = [load(h, r, 3 + i) for i, (h, r) in enumerate(((q_h, q_ref), (k_h, k_ref), (v_h, v_ref)))]
    late = [load(h, r, 6 + i) for i, (h, r) in enumerate(((zq_h, zq_ref), (zk_h, zk_ref), (w_h, w_ref)))]
    own_half(0).start()
    for c in early:
        c.start()
    own_half(1).start()
    for c in late:
        c.start()
    residual.start()
    p.greet(True)
    sides = ((gw_ref, gw_s), (gt_ref, gt_s))
    out_far = [remote(a, b.at[near], hsnd.at[i], hrcv.at[i], partner) for i, (a, b) in enumerate(sides)]
    in_far = [remote(a, b.at[far], hsnd.at[i], hrcv.at[i], partner) for i, (a, b) in enumerate(sides)]
    out_near = [remote(a, b.at[far], hsnd.at[2 + i], hrcv.at[2 + i], p.sibling()) for i, (a, b) in enumerate(sides)]
    in_near = [remote(a, b.at[near], hsnd.at[2 + i], hrcv.at[2 + i], p.sibling()) for i, (a, b) in enumerate(sides)]

    def send_halo(_):
        for c in out_near:
            c.start()

        @pl.when(has)
        def _():
            for c in out_far:
                c.start()

    def take_halo(_):
        for c in in_near:
            c.wait_recv()

        @pl.when(has)
        def _():
            for c in in_far:
                c.wait_recv()

    def sib(k, zy):
        return P_h.at[zy, 1 - p.c, :, pl.ds(*chunks[k][:2])] if k < 5 else PQ.at[k - 5, zy, 1 - p.c]

    def own(k, zy, x):
        return U.at[k % 2, zy, x, pl.ds(0, chunks[k][1])] if k < 5 else PQ.at[k - 5, zy, p.c, x]

    sc = Scatter(p, sib, own, R0, R1, R2, R3, snd, rcv, chunks)
    on = ones_per_head()

    def prepare(_):
        start = p.s * S
        fill_band(mask_s, len_ref, pk_ref[...], start, win // 2)
        dk = doc_numbers(len_ref, start + lax.broadcasted_iota(jnp.int32, (1, S), 1))
        real = pk_ref[:, S:2 * S] == 1
        for side in range(2):
            dq = doc_numbers(len_ref, start + (2 * side - 1) * S + lax.broadcasted_iota(jnp.int32, (S, 1), 0))
            maskr_s[side] = jnp.where((dq == dk) & real, 1.0, 0.0)
        fill_features(dm_s, draws_ref)
        vv_s[:, 128:] = jnp.ones((vv_s.shape[0], 128), BF16)
        gw_s[S:2 * S, :] = gw_ref[...]
        gt_s[S:2 * S, :] = gt_ref[...]
        xt_s[...] = x_ref[...].T
        cur[0] = jnp.zeros(cur.shape[1:], F32)

        @pl.when(jnp.logical_not(has))
        def _():
            gw_s[far, :] = jnp.zeros((S, W), BF16)
            gt_s[far, :] = jnp.zeros((S, 128), BF16)
        for c in early:
            c.wait()

    def core(k):
        if k < 5:
            own_half(k).wait()
        sc.core(k)
        if k + 2 < 5:
            own_half(k + 2).start()

    def own_pairs(j):
        def one(i, _):
            back_own(S, span, win, heads, i, bias_ref, q_ref, k_ref, v_ref, gw_s, gt_s, mask_s, t_s, w_s, gs_s, p_s, vv_s, gkt_s, gvt_s, gq_s, cur.at[0])
            return 0

        lax.fori_loop(2 * j, 2 * j + 2, one, 0)

    def rim_pairs(j):
        def one(i, _):
            back_rim(S, span, heads, i, bias_ref, q_ref, k_ref, v_ref, gw_s, gt_s, maskr_s, t_s, w_s, gs_s, vv_s, gkt_s, gvt_s)
            return 0

        lax.fori_loop(2 * j, 2 * j + 2, one, 0)

    def project(l):
        if l == 0:
            for c in late[:2]:
                c.wait()

        def one(i, _):
            def at(t):
                return pl.ds(pl.multiple_of(l * W + t * wide + (i - wide // 128 * l) * 128, 128), 128)

            lanes = pl.ds(pl.multiple_of(i * 128, 128), 128)
            gp_s[:, at(0)] = phi_back(gq_s[:, lanes], q_ref[S:2 * S, lanes], zq_ref[:, lanes], dm_s[0, i], dm_s[1, i], on, scale).astype(BF16)
            gp_s[:, at(1)] = phi_back(gkt_s[i].T, k_ref[S:2 * S, lanes], zk_ref[:, lanes], dm_s[0, i], dm_s[1, i], on, scale).astype(BF16)
            gp_s[:, at(2)] = gvt_s[i].T.astype(BF16)
            return 0

        lax.fori_loop(wide // 128 * l, wide // 128 * (l + 1), one, 0)
        cs = slice(l * W, (l + 1) * W)
        sums = jnp.sum(gp_s[:, cs].astype(F32), 0, keepdims=True)
        extra = jnp.concatenate([sums, vg_ref[8 * l + 1:8 * l + 8, :]], 0)
        part = dot(xt_s[...], gp_s[:, cs]).reshape(n_dev, f, W)
        part = jnp.concatenate([part, jnp.broadcast_to(extra[None], (n_dev,) + extra.shape)], 1)
        PQ[l] = part.astype(BF16).reshape(n_seq // 2, 2, 2, SLAB, W)

    def tokens_back(_):
        residual.wait()
        late[2].wait()
        gx_ref[...] += dot(gp_s[:, :W], w_ref[0], NT) + dot(gp_s[:, W:2 * W], w_ref[1], NT) + dot(gp_s[:, 2 * W:], w_ref[2], NT)

    def done(k):
        total = sc.finish(k)
        if k < 2:
            gdown_ref[2 * f * k:2 * f * (k + 1), :] = total
        elif k < 4:
            for j in range(2):
                gup_ref[:, (2 * (k - 2) + j) * W:(2 * (k - 2) + j + 1) * W] = total[j * f:(j + 1) * f]
        elif k == 4:
            gout_ref[...] = total[:f]
        else:
            l = k - 5
            for t in range(3):
                gqkv_ref[:, t * W + l * wide:t * W + (l + 1) * wide] = total[:f, t * wide:(t + 1) * wide]
            ex_s[8 * l:8 * l + 8, :] = total[f:]

    va = SumAll(p, cur, got, vsnd, vrcv)
    n = SumAll.steps(p.Z)

    def sum_step(i):
        if i:
            va.step(i - 1)
        if i < n:
            va.start(i)

    play(BACKWARD, dict(b=sc.begin, c=core, o=sc.one, t=sc.two, f=done, pre=prepare, pr=own_pairs, ri=rim_pairs, H=send_halo, hw=take_halo, pj=project, gx=tokens_back, v=sum_step))
    rel_ref[...] = cur[n][:rel_ref.shape[0]]

    def mine(row, share):
        width = row.shape[1]
        return pltpu.roll(jnp.broadcast_to(row, (8, width)), lax.rem(width - share * p.me, width), 1)[:1, :128]

    ex = ex_s[...]
    small_ref[0:1, :] = mine(jnp.concatenate([ex[8 * l:8 * l + 1, t * wide:(t + 1) * wide] for t in range(3) for l in range(3)], 1), 3 * f)
    small_ref[1:2, :] = mine(jnp.concatenate([ex[k:k + 1] for k in range(1, 5)], 1), 4 * f)
    singles = jnp.concatenate([ex[5:8], ex[9:12], jnp.zeros((2, W), F32)], 0)
    small_ref[2:8, :] = pltpu.roll(singles, lax.rem(W - f * p.me, W), 1)[:6, :128]
    sc.drain()
    for c in out_near:
        c.wait_send()

    @pl.when(has)
    def _():
        for c in out_far:
            c.wait_send()


def backward(n_seq, x, pk, bias, draws, lens, w, q, k, v, vg, zq, zk, gw, gt, g1, P_):
    S, W = x.shape
    KS = k.shape[0]
    heads, win = bias.shape
    feats, dims = draws.shape[1:]
    span = win + SB
    Z = n_seq // 4
    n_pair = W // 128
    f = W // (2 * n_seq)
    first = 8 * f + SLAB
    R = first + 3 * SLAB
    where = tuple((2 * f * k, 2 * f) for k in range(4)) + ((8 * f, SLAB),) + tuple((first + SLAB * l, SLAB) for l in range(3))
    chunks = tuple(w + (h,) for w, h in zip(where, CUT_BACKWARD))
    V = pltpu.VMEM
    hbm = pl.BlockSpec(memory_space=pl.ANY)
    n = SumAll.steps(Z)
    K = len(chunks)
    sd = jax.ShapeDtypeStruct
    return pl.pallas_call(
        functools.partial(backward_kernel, n_seq, chunks, dims ** -0.25),
        out_shape=(sd((S, W), F32), sd((heads, win), F32), sd((f, 3 * W), F32), sd((f, 4 * W), F32), sd((4 * f, W), F32), sd((f, W), F32), sd((8, 128), F32)),
        in_specs=vmem(4) + [pl.BlockSpec(memory_space=pltpu.SMEM)] + vmem(3) + [hbm] * 8, out_specs=tuple(vmem(7)),
        scratch_shapes=[V(a.shape, a.dtype) for a in (w, q, k, v, zq, zk)] + [
            V((2, 2 * Z, 2, 2 * f, W), BF16), V((3, 2 * Z, 2, 2, SLAB, W), BF16)] + Scatter.buffers(Z, R, W) + [
            V((S, span), F32), V((2, S, S), F32), V((2 * SB, span), F32), V((2 * SB, span), BF16), V((2 * SB, span), BF16), V((2 * SB, span), F32),
            V((KS, 256), BF16), V((n_pair, 128, S), F32), V((n_pair, 128, S), F32), V((S, W), F32), V((KS, W), BF16), V((KS, 128), BF16),
            V((S, 3 * W), BF16), V((W, S), BF16),
            V((2, heads // 2, 2 * feats, 2 * dims), BF16), V((24, W), F32), V((n + 1, 16, win), F32), V((n, 16, win), F32),
            dma(K, Scatter.sems(Z)), dma(K, Scatter.sems(Z)), dma(4), dma(4), dma(n), dma(n), dma(9)],
        compiler_params=pltpu.CompilerParams(collective_id=3, has_side_effects=True, vmem_limit_bytes=64 << 20),
        name="backward",
    )(x, pk, bias, draws, lens, vg, gw, gt, w, q, k, v, zq, zk, g1, P_)

EPS = 1e-06
EXACT_MATMUL = lax.Precision.HIGHEST


def padded_2(cells, sides, width):
    for axis, dim in sides:
        count = lax.axis_size(axis)
        ends = count - 1
        head = lax.slice_in_dim(cells, 0, width, axis=dim)
        tail = lax.slice_in_dim(cells, cells.shape[dim] - width, cells.shape[dim], axis=dim)
        cells = jnp.concatenate(
            [
                lax.ppermute(tail, axis, [(i, (i + 1) % count) for i in range(ends)]),
                cells,
                lax.ppermute(head, axis, [((i + 1) % count, i) for i in range(ends)]),
            ],
            axis=dim,
        )
    return cells


def passed_along(block, axis, distance):
    devices = range(lax.axis_size(axis))
    route = [(i - distance, i) for i in devices if i - distance in devices]
    return lax.ppermute(block, axis, route)


def layer_norm(values, gain, shift):
    center = values - jnp.mean(values, -1, keepdims=True)
    spread = jnp.mean(center * center, -1, keepdims=True)
    return center * lax.rsqrt(spread + EPS) * gain + shift


def feature_map(heads_in, random_features):
    scaled_input = heads_in * heads_in.shape[-1] ** (-0.25)
    projected_rows = jnp.einsum(
        "ykb,kib->yki", scaled_input, random_features, precision=EXACT_MATMUL
    )
    half_square = 0.5 * jnp.sum(scaled_input * scaled_input, -1, keepdims=True)
    return jnp.exp(projected_rows - half_square) * random_features.shape[1] ** (-0.5)


def document_numbers(positions, lengths_row):
    ends = jnp.cumsum(lengths_row)
    counted = jnp.sum((positions[:, None] >= ends[None, :]).astype(jnp.int32), -1)
    return jnp.where(positions < 0, -1, counted)


def fits(n_seq, n_row, f, tokens_here, half_win):
    return n_row == 2 and n_seq == 4 * 4 and f + 8 == SLAB and tokens_here == half_win


def with_kernels(tokens, cotangent, lengths, padding, feature_draws, rel_bias, *weights):
    w_qkv, b_qkv, w_out, b_out, gain_a, shift_a, w_up, b_up, w_down, b_down, gain_f, shift_f = weights
    local = tokens[0]
    W = local.shape[1]
    n_seq = lax.axis_size("seq")
    f = w_out.shape[0]
    b3 = jnp.pad(b_qkv.astype(F32), (0, 3 * W - 3 * f))[None]
    b4 = jnp.pad(b_up.astype(F32), (0, 4 * W - 4 * f))[None]
    b1 = jnp.pad(jnp.stack([b_out, gain_a, shift_a, b_down, gain_f, shift_f]).astype(F32), ((0, 2), (0, W - f)))
    (qkv_w, out_w, up_w, zq, zk, q, k, v, att, inv, vec, pk, col) = forward(
        n_seq, w_qkv, w_out, w_up, w_down, b3, b4, b1, local, padding, rel_bias, feature_draws, lengths)
    out, g1, gw, gt, vg, P_ = middle(n_seq, rel_bias.shape[0], col, local, cotangent[0], att, inv, out_w, up_w, vec)
    P_ = P_.reshape(n_seq // 2, 2, 2, P_.shape[1], W)
    gx, rel, g_qkv, g_up, g_down, g_out, small = backward(
        n_seq, local, pk, rel_bias, feature_draws, lengths, qkv_w, q, k, v, vg, zq, zk, gw, gt, g1, P_)
    one = [small[i, :f] for i in range(2, 8)]
    return (
        out[None], gx[None], rel, g_qkv, small[0, : 3 * f], g_out, one[0], one[1], one[2], g_up, small[1, : 4 * f],
        g_down, one[3], one[4], one[5],
    )


def on_device(
    tokens,
    cotangent,
    lengths,
    padding,
    feature_draws,
    rel_bias,
    w_qkv,
    b_qkv,
    w_out,
    b_out,
    gain_attn,
    shift_attn,
    w_up,
    b_up,
    w_down,
    b_down,
    gain_ffn,
    shift_ffn,
):
    if fits(lax.axis_size("seq"), lax.axis_size("row"), w_out.shape[0], tokens.shape[1], rel_bias.shape[1] // 2):
        return with_kernels(
            tokens, cotangent, lengths, padding, feature_draws, rel_bias, w_qkv, b_qkv, w_out, b_out, gain_attn, shift_attn,
            w_up, b_up, w_down, b_down, gain_ffn, shift_ffn,
        )
    local = tokens[0]
    seq_len = local.shape[0]
    model_width = local.shape[1]
    head_count = rel_bias.shape[0]
    window_len = rel_bias.shape[1]
    half_win = window_len // 2
    feat_count = feature_draws.shape[1]
    head_dim = model_width // head_count
    feat_cols = head_count * feat_count
    params = (
        lax.all_gather(w_qkv, ("seq", "row"), axis=0, tiled=True),
        lax.all_gather(b_qkv, ("seq", "row"), axis=0, tiled=True),
        lax.all_gather(w_out, ("seq", "row"), axis=0, tiled=True),
        lax.all_gather(b_out, ("seq", "row"), axis=0, tiled=True),
        lax.all_gather(gain_attn, ("seq", "row"), axis=0, tiled=True),
        lax.all_gather(shift_attn, ("seq", "row"), axis=0, tiled=True),
        lax.all_gather(w_up, ("seq", "row"), axis=0, tiled=True),
        lax.all_gather(b_up, ("seq", "row"), axis=0, tiled=True),
        lax.all_gather(w_down, ("seq", "row"), axis=0, tiled=True),
        lax.all_gather(b_down, ("seq", "row"), axis=0, tiled=True),
        lax.all_gather(gain_ffn, ("seq", "row"), axis=0, tiled=True),
        lax.all_gather(shift_ffn, ("seq", "row"), axis=0, tiled=True),
    )
    (
        qkv_w,
        qkv_b,
        out_w,
        out_b,
        first_norm_gain,
        shift_one,
        up_w,
        up_b,
        down_w,
        down_b,
        gain_two,
        shift_two,
    ) = params
    seq_pos = lax.axis_index("seq")
    start_pos = seq_pos * seq_len
    positions = start_pos + jnp.arange(seq_len, dtype=jnp.int32)
    ext_pos = start_pos - half_win + jnp.arange(seq_len + window_len, dtype=jnp.int32)
    doc_query = document_numbers(positions, lengths[0])
    doc_keys = document_numbers(ext_pos, lengths[0])
    pad_local = padding[0]
    pad_ones = jnp.ones((half_win,), jnp.int32)
    pad_keys = jnp.concatenate([pad_ones, pad_local, pad_ones])
    proj_qkv = jnp.dot(local, qkv_w, preferred_element_type=jnp.float32) + qkv_b
    queries = proj_qkv[:, :model_width].reshape(seq_len, head_count, head_dim)
    keys_in = proj_qkv[:, model_width : 2 * model_width].reshape(seq_len, head_count, head_dim)
    q_full, query_back = jax.vjp(partial(feature_map, random_features=feature_draws), queries)
    k_full, key_back = jax.vjp(partial(feature_map, random_features=feature_draws), keys_in)
    q_feat = q_full.astype(jnp.bfloat16)
    k_flat = k_full.astype(jnp.bfloat16).reshape(seq_len, feat_cols)
    values_low = proj_qkv[:, 2 * model_width :].astype(jnp.bfloat16)
    own_keys = jnp.concatenate([k_flat, values_low], 1)
    masked_keys = jnp.concatenate([k_flat * pad_local.astype(jnp.bfloat16)[:, None], values_low], 1)
    rims = padded_2(masked_keys, (("seq", 0),), half_win)
    key_ext = jnp.concatenate([rims[:half_win], own_keys, rims[half_win + seq_len :]], 0)

    dq, dk, pk = doc_query[:, None], doc_keys[None, :], pad_keys[None, :]
    bias8 = bias_rows(rel_bias)
    q_low = q_feat.reshape(seq_len, feat_cols)
    keys_x, vals_x = key_ext[:, :feat_cols], key_ext[:, feat_cols:]
    attended, inv_tot = attn_fwd(dq, dk, pk, bias8, q_low, keys_x, vals_x)
    att_low = attended.astype(jnp.bfloat16)
    branch = jnp.dot(att_low, out_w, preferred_element_type=jnp.float32) + out_b
    resid_one = local.astype(jnp.float32) + branch
    hidden_one, ln_one_back = jax.vjp(
        layer_norm, resid_one, first_norm_gain.astype(jnp.float32), shift_one.astype(jnp.float32)
    )
    hidden_low = hidden_one.astype(jnp.bfloat16)
    inner = jnp.dot(hidden_low, up_w, preferred_element_type=jnp.float32) + up_b
    active, gelu_back = jax.vjp(partial(jax.nn.gelu, approximate=False), inner)
    active_low = active.astype(jnp.bfloat16)
    ffn_out = jnp.dot(active_low, down_w, preferred_element_type=jnp.float32) + down_b
    result, ln_two_back = jax.vjp(
        layer_norm,
        hidden_one + ffn_out,
        gain_two.astype(jnp.float32),
        shift_two.astype(jnp.float32),
    )
    params = (
        lax.all_gather(w_qkv, ("seq", "row"), axis=0, tiled=True),
        lax.all_gather(b_qkv, ("seq", "row"), axis=0, tiled=True),
        lax.all_gather(w_out, ("seq", "row"), axis=0, tiled=True),
        lax.all_gather(b_out, ("seq", "row"), axis=0, tiled=True),
        lax.all_gather(gain_attn, ("seq", "row"), axis=0, tiled=True),
        lax.all_gather(shift_attn, ("seq", "row"), axis=0, tiled=True),
        lax.all_gather(w_up, ("seq", "row"), axis=0, tiled=True),
        lax.all_gather(b_up, ("seq", "row"), axis=0, tiled=True),
        lax.all_gather(w_down, ("seq", "row"), axis=0, tiled=True),
        lax.all_gather(b_down, ("seq", "row"), axis=0, tiled=True),
        lax.all_gather(gain_ffn, ("seq", "row"), axis=0, tiled=True),
        lax.all_gather(shift_ffn, ("seq", "row"), axis=0, tiled=True),
    )
    (
        qkv_w,
        qkv_b,
        out_w,
        out_b,
        first_norm_gain,
        shift_one,
        up_w,
        up_b,
        down_w,
        down_b,
        gain_two,
        shift_two,
    ) = params
    grad_two, grad_gain_two, grad_shift_two = ln_two_back(cotangent[0].astype(jnp.float32))
    grad_two_low = grad_two.astype(jnp.bfloat16)
    grad_down_w = jnp.einsum(
        "ti,tj->ij", active_low, grad_two_low, preferred_element_type=jnp.float32
    )
    grad_down_b = jnp.sum(grad_two_low, 0, dtype=jnp.float32)
    grad_active = jnp.dot(grad_two_low, down_w.T, preferred_element_type=jnp.float32)
    grad_inner_low = gelu_back(grad_active)[0].astype(jnp.bfloat16)
    grad_up_w = jnp.einsum(
        "ti,tj->ij", hidden_low, grad_inner_low, preferred_element_type=jnp.float32
    )
    grad_up_b = jnp.sum(grad_inner_low, 0, dtype=jnp.float32)
    grad_hidden = grad_two + jnp.dot(grad_inner_low, up_w.T, preferred_element_type=jnp.float32)
    grad_one, grad_gain_one, grad_shift_one = ln_one_back(grad_hidden)
    grad_one_low = grad_one.astype(jnp.bfloat16)
    grad_out_w = jnp.einsum("ti,tj->ij", att_low, grad_one_low, preferred_element_type=jnp.float32)
    grad_out_b = jnp.sum(grad_one_low, 0, dtype=jnp.float32)
    grad_att = jnp.dot(grad_one_low, out_w.T, preferred_element_type=jnp.float32)
    grad_fq_all, grad_kf, grad_vv, grad_b8 = attn_bwd(
        dq, dk, pk, bias8, q_low, keys_x, vals_x, attended, inv_tot, grad_att
    )
    grad_bias = grad_b8.reshape(head_count // 2, 8, window_len)[:, :2].reshape(head_count, window_len)
    lower_rim = jnp.concatenate([grad_kf[:half_win], grad_vv[:half_win]], 1)
    upper_rim = jnp.concatenate([grad_kf[half_win + seq_len :], grad_vv[half_win + seq_len :]], 1)
    from_right = passed_along(lower_rim.astype(jnp.bfloat16), "seq", -1).astype(lower_rim.dtype)
    from_left = passed_along(upper_rim.astype(jnp.bfloat16), "seq", 1).astype(upper_rim.dtype)
    returned = from_left + from_right
    pad_float = pad_local.astype(jnp.float32)[:, None]
    grad_kfeat = grad_kf[half_win : half_win + seq_len] + returned[:, :feat_cols] * pad_float
    value_gradient = grad_vv[half_win : half_win + seq_len] + returned[:, feat_cols:]
    grad_queries = query_back(grad_fq_all.reshape(seq_len, head_count, feat_count))[0]
    grad_keys_in = key_back(grad_kfeat.reshape(seq_len, head_count, feat_count))[0]
    grad_proj_low = jnp.concatenate(
        [
            grad_queries.reshape(seq_len, model_width),
            grad_keys_in.reshape(seq_len, model_width),
            value_gradient,
        ],
        1,
    ).astype(jnp.bfloat16)
    grad_qkv_w = jnp.einsum("ti,tj->ij", local, grad_proj_low, preferred_element_type=jnp.float32)
    grad_qkv_b = jnp.sum(grad_proj_low, 0, dtype=jnp.float32)
    grad_input = grad_one + jnp.dot(grad_proj_low, qkv_w.T, preferred_element_type=jnp.float32)
    grad_rel = lax.psum(grad_bias, ("seq", "row"))
    summed = (
        lax.psum_scatter(grad_qkv_w, ("seq", "row"), scatter_dimension=0, tiled=True),
        lax.psum_scatter(grad_qkv_b, ("seq", "row"), scatter_dimension=0, tiled=True),
        lax.psum_scatter(grad_out_w, ("seq", "row"), scatter_dimension=0, tiled=True),
        lax.psum_scatter(grad_out_b, ("seq", "row"), scatter_dimension=0, tiled=True),
        lax.psum_scatter(grad_gain_one, ("seq", "row"), scatter_dimension=0, tiled=True),
        lax.psum_scatter(grad_shift_one, ("seq", "row"), scatter_dimension=0, tiled=True),
        lax.psum_scatter(grad_up_w, ("seq", "row"), scatter_dimension=0, tiled=True),
        lax.psum_scatter(grad_up_b, ("seq", "row"), scatter_dimension=0, tiled=True),
        lax.psum_scatter(grad_down_w, ("seq", "row"), scatter_dimension=0, tiled=True),
        lax.psum_scatter(grad_down_b, ("seq", "row"), scatter_dimension=0, tiled=True),
        lax.psum_scatter(grad_gain_two, ("seq", "row"), scatter_dimension=0, tiled=True),
        lax.psum_scatter(grad_shift_two, ("seq", "row"), scatter_dimension=0, tiled=True),
    )
    return (
        result[None].astype(jnp.bfloat16),
        grad_input[None],
        grad_rel,
        summed[0],
        summed[1],
        summed[2],
        summed[3],
        summed[4],
        summed[5],
        summed[6],
        summed[7],
        summed[8],
        summed[9],
        summed[10],
        summed[11],
    )


def solution(mesh):
    in_specs = (
        P("row", "seq", None),
        P("row", "seq", None),
        P("row", None),
        P("row", "seq"),
        P(),
        P(),
        P(("seq", "row"), None),
        P(("seq", "row")),
        P(("seq", "row"), None),
        P(("seq", "row")),
        P(("seq", "row")),
        P(("seq", "row")),
        P(("seq", "row"), None),
        P(("seq", "row")),
        P(("seq", "row"), None),
        P(("seq", "row")),
        P(("seq", "row")),
        P(("seq", "row")),
    )
    out_specs = (
        P("row", "seq", None),
        P("row", "seq", None),
        P(),
        P(("seq", "row"), None),
        P(("seq", "row")),
        P(("seq", "row"), None),
        P(("seq", "row")),
        P(("seq", "row")),
        P(("seq", "row")),
        P(("seq", "row"), None),
        P(("seq", "row")),
        P(("seq", "row"), None),
        P(("seq", "row")),
        P(("seq", "row")),
        P(("seq", "row")),
    )
    return jax.shard_map(
        on_device, mesh=mesh, in_specs=in_specs, out_specs=out_specs, check_vma=False
    )
```

```python
from functools import partial

import functools
import jax
import jax.numpy as jnp
from jax import lax
from jax.experimental import pallas as pl
from jax.experimental.pallas import tpu as pltpu
from jax.sharding import PartitionSpec as P

F32, BF16 = jnp.float32, jnp.bfloat16
NT = (((1,), (1,)), ((), ()))
TN = (((0,), (0,)), ((), ()))
SB = 128

def dot(a, b, dims=None):
    if dims is None:
        return jnp.dot(a, b, preferred_element_type=F32)
    return lax.dot_general(a, b, dims, preferred_element_type=F32)

def toep(row, width):
    win = row.shape[1]
    wide = jnp.concatenate([row, jnp.zeros((1, width - win), F32)], 1)
    return pltpu.roll(jnp.broadcast_to(wide, (SB, width)), 0, 1, stride=1, stride_axis=0)

def unskew(p, win):
    rows = p.shape[0]; width = p.shape[1]
    while rows > 8:
        rows //= 2
        p = p[:rows] + pltpu.roll(p[rows:], width - rows, 1)
    r = lax.broadcasted_iota(jnp.int32, (8, 1), 0)
    for s in (1, 2, 4):
        p = jnp.where((r & s) != 0, pltpu.roll(p, width - s, 1), p)
    return jnp.sum(p, 0, keepdims=True)[:, :win]

def fill_mask(mask_s, dq_ref, dk_ref, pk_ref, span, half):
    S = mask_s.shape[0]
    for a in range(S // SB):
        dq = dq_ref[a*SB:(a+1)*SB, :]
        dk = dk_ref[:, a*SB:a*SB+span]
        pk = pk_ref[:, a*SB:a*SB+span]
        r = lax.broadcasted_iota(jnp.int32, (SB, span), 0)
        c = lax.broadcasted_iota(jnp.int32, (SB, span), 1)
        ok = (dq == dk) & ((pk == 1) | (c == r + half))
        mask_s[a*SB:(a+1)*SB, :] = jnp.where(ok, 1.0, 0.0)

def halves(x):
    lane = lax.broadcasted_iota(jnp.int32, x.shape, 1)
    z = jnp.zeros_like(x)
    return jnp.where(lane < 64, x, z), jnp.where(lane >= 64, x, z)

def pick(a, b):
    lane = lax.broadcasted_iota(jnp.int32, a.shape, 1)
    return jnp.where(lane < 64, a, b)

def fwd_kernel(CH, dq_ref, dk_ref, pk_ref, bias_ref, q_ref, k_ref, v_ref, att_ref, inv_ref, mask_s, t_s, w_s, v_s):
    S = q_ref.shape[0]; win = bias_ref.shape[1]; span = win + SB
    p = pl.program_id(0)
    @pl.when(p == 0)
    def _():
        fill_mask(mask_s, dq_ref, dk_ref, pk_ref, span, win // 2)
        v_s[:, 128:] = jnp.ones((v_s.shape[0], 128), BF16)
    rows = jnp.exp(bias_ref[pl.ds(pl.multiple_of(p * 8, 8), 8), :])
    for i in range(2):
        t_s[i*SB:(i+1)*SB, :] = toep(rows[i:i+1], span)
    v_s[:, :128] = v_ref[...]
    for a in range(S // SB):
        qa, qb = halves(q_ref[a*SB:(a+1)*SB, :])
        qq = jnp.concatenate([qa, qb], 0)
        for c in range(0, span, CH):
            s = dot(qq, k_ref[a*SB+c:a*SB+c+CH, :], NT)
            m = mask_s[a*SB:(a+1)*SB, c:c+CH]
            t = t_s[:, c:c+CH]
            w_s[:SB, c:c+CH] = (s[:SB] * (t[:SB] * m)).astype(BF16)
            w_s[SB:, c:c+CH] = (s[SB:] * (t[SB:] * m)).astype(BF16)
        o = dot(w_s[...], v_s[a*SB:a*SB+span, :])
        inv = 1.0 / pick(o[:SB, 128:], o[SB:, 128:])
        att_ref[a*SB:(a+1)*SB, :] = pick(o[:SB, :128], o[SB:, :128]) * inv
        inv_ref[a*SB:(a+1)*SB, :] = inv

def bias_rows(rel_bias):
    h, w = rel_bias.shape
    x = rel_bias.reshape(h // 2, 2, w)
    return jnp.pad(x, ((0, 0), (0, 6), (0, 0))).reshape(h // 2 * 8, w)

def attn_fwd(dq, dk, pk, bias8, q, k, v, CH=384):
    S, D = q.shape; KS = k.shape[0]; win = bias8.shape[1]; span = win + SB
    full = lambda *s: pl.BlockSpec(s, lambda p: (0,) * len(s))
    col = lambda n: pl.BlockSpec((n, 128), lambda p: (0, p))
    return pl.pallas_call(
        functools.partial(fwd_kernel, CH),
        grid=(D // 128,),
        out_shape=(jax.ShapeDtypeStruct((S, D), F32), jax.ShapeDtypeStruct((S, D), F32)),
        in_specs=[full(S, 1), full(1, KS), full(1, KS), full(*bias8.shape), col(S), col(KS), col(KS)],
        out_specs=(col(S), col(S)),
        scratch_shapes=[pltpu.VMEM((S, span), F32), pltpu.VMEM((2*SB, span), F32), pltpu.VMEM((2*SB, span), BF16), pltpu.VMEM((KS, 256), BF16)],
        compiler_params=pltpu.CompilerParams(vmem_limit_bytes=48 << 20),
        name="attn_fwd",
    )(dq, dk, pk, bias8, q, k, v)

def bwd_kernel(CH, dq_ref, dk_ref, pk_ref, bias_ref, q_ref, k_ref, v_ref, att_ref, inv_ref, ga_ref,
               gq_ref, gk_ref, gv_ref, gb_ref, mask_s, t_s, w_s, gs_s, p_s, v_s, gk_s, gv_s):
    S = q_ref.shape[0]; win = bias_ref.shape[1]; span = win + SB
    p = pl.program_id(0)
    @pl.when(p == 0)
    def _():
        fill_mask(mask_s, dq_ref, dk_ref, pk_ref, span, win // 2)
        v_s[:, 128:] = jnp.ones((v_s.shape[0], 128), BF16)
    rows = jnp.exp(bias_ref[pl.ds(pl.multiple_of(p * 8, 8), 8), :])
    for i in range(2):
        t_s[i*SB:(i+1)*SB, :] = toep(rows[i:i+1], span)
    v_s[:, :128] = v_ref[...]
    gk_s[...] = jnp.zeros_like(gk_s)
    gv_s[...] = jnp.zeros_like(gv_s)
    for a in range(S // SB):
        rs = slice(a*SB, (a+1)*SB)
        qa, qb = halves(q_ref[rs, :])
        qq = jnp.concatenate([qa, qb], 0)
        ga = ga_ref[rs, :]
        inv = inv_ref[rs, :]
        gw = (ga * inv).astype(BF16)
        gwa, gwb = halves(gw)
        pr = ga * att_ref[rs, :] * inv
        pa, pb = halves(pr)
        lane = lax.broadcasted_iota(jnp.int32, (SB, 128), 1)
        def ext(x):
            g = -jnp.sum(x, 1, keepdims=True)
            hi = g.astype(BF16)
            lo = (g - hi.astype(F32)).astype(BF16)
            z = jnp.zeros((SB, 128), BF16)
            return jnp.where(lane == 0, hi, jnp.where(lane == 1, lo, z))
        gg = jnp.concatenate([jnp.concatenate([gwa, ext(pa)], 1), jnp.concatenate([gwb, ext(pb)], 1)], 0)
        for c in range(0, span, CH):
            s = dot(qq, k_ref[a*SB+c:a*SB+c+CH, :], NT)
            g = dot(gg, v_s[a*SB+c:a*SB+c+CH, :], NT)
            m = mask_s[rs, c:c+CH]
            for h in range(2):
                hs = slice(h*SB, (h+1)*SB)
                cm = t_s[hs, c:c+CH] * m
                w = s[hs] * cm
                w_s[hs, c:c+CH] = w.astype(BF16)
                gs_s[hs, c:c+CH] = (g[hs] * cm).astype(BF16)
                pw = g[hs] * w
                if a == 0:
                    p_s[hs, c:c+CH] = pw
                else:
                    p_s[hs, c:c+CH] += pw
        gq = dot(gs_s[...], k_ref[a*SB:a*SB+span, :])
        gq_ref[rs, :] = pick(gq[:SB], gq[SB:])
        gk_s[:, a*SB:a*SB+span] += dot(qq, gs_s[...], TN)
        gwq = jnp.concatenate([gwa, gwb], 0)
        gv_s[:, a*SB:a*SB+span] += dot(gwq, w_s[...], TN)
    gk_ref[...] = gk_s[...].T
    gv_ref[...] = gv_s[...].T
    gb_ref[...] = jnp.concatenate([unskew(p_s[:SB, :], win), unskew(p_s[SB:, :], win), jnp.zeros((6, win), F32)], 0)

def attn_bwd(dq, dk, pk, bias8, q, k, v, att, inv, ga, CH=384):
    S, D = q.shape; KS = k.shape[0]; win = bias8.shape[1]; span = win + SB
    full = lambda *s: pl.BlockSpec(s, lambda p: (0,) * len(s))
    col = lambda n: pl.BlockSpec((n, 128), lambda p: (0, p))
    V = pltpu.VMEM
    return pl.pallas_call(
        functools.partial(bwd_kernel, CH),
        grid=(D // 128,),
        out_shape=(jax.ShapeDtypeStruct((S, D), F32), jax.ShapeDtypeStruct((KS, D), F32), jax.ShapeDtypeStruct((KS, D), F32),
                   jax.ShapeDtypeStruct(bias8.shape, F32)),
        in_specs=[full(S, 1), full(1, KS), full(1, KS), full(*bias8.shape), col(S), col(KS), col(KS), col(S), col(S), col(S)],
        out_specs=(col(S), col(KS), col(KS), pl.BlockSpec((8, win), lambda p: (p, 0))),
        scratch_shapes=[V((S, span), F32), V((2*SB, span), F32), V((2*SB, span), BF16), V((2*SB, span), BF16), V((2*SB, span), F32),
                        V((KS, 256), BF16), V((128, KS), F32), V((128, KS), F32)],
        compiler_params=pltpu.CompilerParams(vmem_limit_bytes=56 << 20),
        name="attn_bwd",
    )(dq, dk, pk, bias8, q, k, v, att, inv, ga)


MESH = pl.DeviceIdType.MESH
SLAB = 32


class Place:
    def __init__(self, n_seq):
        self.Z = n_seq // 4
        s, self.x = lax.axis_index("seq"), lax.axis_index("row")
        self.s = s
        self.c, self.y, self.z = lax.rem(s, 2), lax.rem(s // 2, 2), s // 4
        self.me = s * 2 + self.x

    def seq(self, z, y, c):
        return (z * 2 + y) * 2 + c

    def zx(self, k):
        z, d = self.z, 1
        while d <= k:
            if k // d % 2:
                z = z + d - 2 * d * lax.rem(self.z // d, 2)
            d *= 2
        return z

    def sibling(self):
        return (self.seq(self.z, self.y, 1 - self.c), self.x)

    def xpeer(self):
        return (self.s, 1 - self.x)

    def ypeer(self):
        return (self.seq(self.z, 1 - self.y, self.c), self.x)

    def zpeer(self, k):
        return (self.seq(self.zx(k), self.y, self.c), self.x)

    def partner(self):
        t, n = self.s - 1 + 2 * self.c, 4 * self.Z
        return (lax.rem(t + n, n), self.x), jnp.logical_and(t >= 0, t < n)

    def greet(self, partner):
        b = pltpu.get_barrier_semaphore()
        peers = [self.sibling(), self.xpeer(), self.ypeer()] + [self.zpeer(k) for k in range(1, self.Z)]
        if partner:
            peers.append(self.partner()[0])
        for p in peers:
            pl.semaphore_signal(b, inc=1, device_id=p, device_id_type=MESH)
        pl.semaphore_wait(b, len(peers))


def remote(src, dst, snd, rcv, dev):
    return pltpu.make_async_remote_copy(src_ref=src, dst_ref=dst, send_sem=snd, recv_sem=rcv, device_id=dev, device_id_type=MESH)


class Gather:
    def __init__(self, place, own, G, snd, rcv, chunks):
        self.p, self.own, self.G, self.snd, self.rcv, self.chunks = place, own, G, snd, rcv, chunks
        self.sent = []

    @staticmethod
    def sems(Z):
        return 5 * Z + 3

    def _copy(self, k, sem, at, dev, part=None, own=False):
        lo, n = part or self.chunks[k][:2]
        dst = self.G.at[at + (pl.ds(lo, n),)]
        src = self.own.at[pl.ds(lo, n)] if own else dst
        return remote(src, dst, self.snd.at[k, sem], self.rcv.at[k, sem], dev)

    def _send(self, *a, **kw):
        c = self._copy(*a, **kw)
        c.start()
        self.sent.append(c)

    def parts(self, k):
        r0, rows, h = self.chunks[k]
        return (r0, h), (r0 + h, rows - h)

    def at(self, j, fy=0, fx=0):
        p = self.p
        return (p.zx(j), p.y if not fy else 1 - p.y, p.c, p.x if not fx else 1 - p.x)

    def column(self, k, t, other=False):
        p = self.p
        y, x = (1 - p.y if t > 1 else p.y), (1 - p.x if t % 2 else p.x)
        return self._copy(k, 5 * p.Z - 1 + t, (slice(None), y, 1 - p.c if other else p.c, x), p.sibling())

    def give(self, k, t):
        c = self.column(k, t)
        c.start()
        self.sent.append(c)

    def bz(self, k):
        for j in range(1, self.p.Z):
            self._send(k, j - 1, self.at(0), self.p.zpeer(j), own=True)

    def bx(self, k):
        self._send(k, self.p.Z - 1, self.at(0), self.p.xpeer(), own=True)

    def by(self, k):
        self._send(k, 2 * self.p.Z - 1, self.at(0), self.p.ypeer(), own=True)

    def direct(self, k, j):
        p, (lo, n) = self.p, self.chunks[k][:2]
        for sem, dev in ((p.Z - 1 + j, p.xpeer()), (2 * p.Z - 1 + j, p.ypeer())):
            at = self.at(j) + (pl.ds(lo, n),)
            c = remote(self.own.at[p.zx(j), pl.ds(lo, n)], self.G.at[at], self.snd.at[k, sem], self.rcv.at[k, sem], dev)
            c.start()
            self.sent.append(c)

    def pzx(self, k):
        p, Z = self.p, self.p.Z
        for j in range(1, Z):
            self._copy(k, j - 1, self.at(j), p.zpeer(j)).wait_recv()
            self._send(k, Z - 1 + j, self.at(j), p.xpeer())
        self.give(k, 0)

    def pzy(self, k):
        for j in range(1, self.p.Z):
            self._send(k, 2 * self.p.Z - 1 + j, self.at(j), self.p.ypeer())

    def px(self, k):
        p, Z = self.p, self.p.Z
        a, b = self.parts(k)
        for j in range(Z):
            self._copy(k, Z - 1 + j, self.at(j, 0, 1), p.xpeer()).wait_recv()
            if a[1]:
                self._send(k, 3 * Z - 1 + j, self.at(j, 0, 1), p.ypeer(), a)
            self._copy(k, 2 * Z - 1 + j, self.at(j, 1, 0), p.ypeer()).wait_recv()
            if b[1]:
                self._send(k, 4 * Z - 1 + j, self.at(j, 1, 0), p.xpeer(), b)
        self.give(k, 1)
        self.give(k, 2)

    def pd(self, k):
        p, Z = self.p, self.p.Z
        a, b = self.parts(k)
        for j in range(Z):
            if a[1]:
                self._copy(k, 3 * Z - 1 + j, self.at(j, 1, 1), p.ypeer(), a).wait_recv()
            if b[1]:
                self._copy(k, 4 * Z - 1 + j, self.at(j, 1, 1), p.xpeer(), b).wait_recv()
        self.give(k, 3)

    def fin(self, k):
        for t in range(4):
            self.column(k, t, True).wait_recv()

    def drain(self):
        for c in self.sent:
            c.wait_send()
        self.sent = []


def play(steps, table):
    for step in steps:
        name = step.rstrip("0123456789")
        table[name](int(step[len(name):]))


class Scatter:
    def __init__(self, place, sib, own, R0, R1, R2, R3, snd, rcv, chunks):
        self.p, self.sib, self.own, self.R0, self.R1, self.R2, self.R3 = place, sib, own, R0, R1, R2, R3
        self.snd, self.rcv, self.chunks = snd, rcv, chunks
        self.sent = []

    @staticmethod
    def sems(Z):
        return 6 * Z - 1

    @staticmethod
    def buffers(Z, R, W):
        return [pltpu.VMEM((2 * Z, 2, R, W), BF16), pltpu.VMEM((Z, 2, R, W), BF16), pltpu.VMEM((Z, R, W), BF16), pltpu.VMEM((Z - 1, R, W), BF16)]

    def rows(self, k):
        return pl.ds(*self.chunks[k][:2])

    def parts(self, k):
        r0, n, h = self.chunks[k]
        return pl.ds(r0, h) if h else None, pl.ds(r0 + h, n - h) if h < n else None

    def _go(self, src, dst, k, sem, dev, start):
        c = remote(src, dst, self.snd.at[k, sem], self.rcv.at[k, sem], dev)
        if start:
            c.start()
            self.sent.append(c)
        else:
            c.wait_recv()

    def order(self):
        return list(range(self.p.Z - 1, -1, -1))

    def _c0(self, k, j, start):
        zy = pl.ds(2 * self.p.zx(j), 2)
        self._go(self.sib(k, zy), self.R0.at[zy, :, self.rows(k)], k, j, self.p.sibling(), start)

    def _c1(self, k, j, start):
        p = self.p
        z = p.zx(j)
        a, b = self.parts(k)
        if a is not None:
            self._go(self.R0.at[pl.ds(2 * z, 2), 1 - p.x, a], self.R1.at[z, :, a], k, p.Z + j, p.xpeer(), start)
        if b is not None:
            self._go(self.R0.at[2 * z + 1 - p.y, :, b], self.R1.at[z, :, b], k, 2 * p.Z + j, p.ypeer(), start)

    def _c2(self, k, j, start):
        p = self.p
        z = p.zx(j)
        a, b = self.parts(k)
        if a is not None:
            self._go(self.R1.at[z, 1 - p.y, a], self.R2.at[z, a], k, 3 * p.Z + j, p.ypeer(), start)
        if b is not None:
            self._go(self.R1.at[z, 1 - p.x, b], self.R2.at[z, b], k, 4 * p.Z + j, p.xpeer(), start)

    def _c3(self, k, j, start):
        r = self.rows(k)
        self._go(self.R2.at[self.p.zx(j), r], self.R3.at[j - 1, r], k, 5 * self.p.Z + j - 1, self.p.zpeer(j), start)

    def begin(self, k):
        for j in self.order():
            self._c0(k, j, True)

    @staticmethod
    def _add(dst, src):
        dst[...] = (dst[...].astype(F32) + src[...].astype(F32)).astype(BF16)

    def core(self, k, js=None):
        p = self.p
        for j in js or self.order():
            self._c0(k, j, False)
            z = p.zx(j)
            for y in range(2):
                for x in range(2):
                    self._add(self.R0.at[2 * z + y, x, self.rows(k)], self.own(k, 2 * z + y, x))
            self._c1(k, j, True)

    def one(self, k, js=None):
        p = self.p
        a, b = self.parts(k)
        for j in js or self.order():
            self._c1(k, j, False)
            z = p.zx(j)
            for i in range(2):
                if a is not None:
                    self._add(self.R1.at[z, i, a], self.R0.at[2 * z + i, p.x, a])
                if b is not None:
                    self._add(self.R1.at[z, i, b], self.R0.at[2 * z + p.y, i, b])
            self._c2(k, j, True)

    def two(self, k, js=None):
        p = self.p
        a, b = self.parts(k)
        for j in js or self.order():
            self._c2(k, j, False)
            z = p.zx(j)
            if a is not None:
                self._add(self.R2.at[z, a], self.R1.at[z, p.y, a])
            if b is not None:
                self._add(self.R2.at[z, b], self.R1.at[z, p.x, b])
            if j:
                self._c3(k, j, True)

    def finish(self, k):
        p, r = self.p, self.rows(k)
        total = self.R2[p.z, r].astype(F32)
        for j in range(1, p.Z):
            self._c3(k, j, False)
            total = total + self.R3[j - 1, r].astype(F32)
        return total

    def drain(self):
        for c in self.sent:
            c.wait_send()
        self.sent = []


class SumAll:
    def __init__(self, place, cur, got, snd, rcv):
        self.p, self.cur, self.got, self.snd, self.rcv = place, cur, got, snd, rcv
        p = place
        self.peers = [p.sibling(), p.xpeer(), p.ypeer()]
        d = 1
        while d < p.Z:
            self.peers.append(p.zpeer(d))
            d *= 2

    @staticmethod
    def steps(Z):
        return 3 + (Z - 1).bit_length()

    def _copy(self, i):
        return remote(self.cur.at[i], self.got.at[i], self.snd.at[i], self.rcv.at[i], self.peers[i])

    def start(self, i):
        self._copy(i).start()

    def step(self, i):
        self._copy(i).wait()
        self.cur[i + 1] = self.cur[i] + self.got[i]


def dma(*shape):
    return pltpu.SemaphoreType.DMA(shape)


def vmem(*n):
    return [pl.BlockSpec(memory_space=pltpu.VMEM)] * (n[0] if n else 1)


def doc_numbers(len_ref, pos):
    ends, count = jnp.int32(0), jnp.zeros(pos.shape, jnp.int32)
    for i in range(len_ref.shape[1]):
        ends = ends + len_ref[0, i]
        count = count + jnp.where(pos >= ends, 1, 0)
    return jnp.where(pos < 0, -1, count)


def fill_band(mask_s, len_ref, pk, start, half):
    S, span = mask_s.shape
    KS = pk.shape[1]
    dk = doc_numbers(len_ref, start - half + lax.broadcasted_iota(jnp.int32, (1, KS), 1))
    for a in range(S // SB):
        dq = doc_numbers(len_ref, start + a * SB + lax.broadcasted_iota(jnp.int32, (SB, 1), 0))
        r = lax.broadcasted_iota(jnp.int32, (SB, span), 0)
        c = lax.broadcasted_iota(jnp.int32, (SB, span), 1)
        ok = (dq == dk[:, a * SB:a * SB + span]) & ((pk[:, a * SB:a * SB + span] == 1) | (c == r + half))
        mask_s[a * SB:(a + 1) * SB, :] = jnp.where(ok, 1.0, 0.0)


def fill_features(dm_s, draws_ref):
    m, d = draws_ref.shape[1:]
    z = jnp.zeros((m, d), F32)
    for i in range(draws_ref.shape[0] // 2):
        full = jnp.concatenate([jnp.concatenate([draws_ref[2 * i], z], 1), jnp.concatenate([z, draws_ref[2 * i + 1]], 1)], 0)
        dm_s[0, i], dm_s[1, i] = split2(full)


def ones_per_head():
    lane = lax.broadcasted_iota(jnp.int32, (256, 128), 1) // 64
    row = lax.rem(lax.broadcasted_iota(jnp.int32, (256, 128), 0) // 64, 2)
    return jnp.where(lane == row, 1.0, 0.0).astype(BF16)


def split2(x):
    hi = x.astype(BF16)
    return hi, (x - hi.astype(F32)).astype(BF16)


def coefs(bias_ref, i, t_s, span):
    for h in range(2):
        t_s[h * SB:(h + 1) * SB, :] = toep(jnp.exp(bias_ref[pl.ds(2 * i + h, 1), :]), span)


FORWARD = (
    "bx4", "by2", "bz0", "bz1", "pre0", "bx2", "by3", "by0", "bx0", "pzx0", "by1", "bx1", "bz2", "bz3", "pzy0", "by4", "pzx1",
    "pzy1", "pzx2", "bz5", "pzy2", "bz4", "bx5", "H0", "bx3", "px1", "px0", "px2", "pd0", "pzx5", "pd1", "fin0", "fin1", "po0",
    "pd2", "fin2", "pzx4", "po1", "pzx3", "po2", "dz0", "KV0", "pzy3", "pzy4", "hw0", "mask0", "by5", "px3", "kvw0", "rim0",
    "pzy5", "rim1", "px4", "rim2", "pr0", "px5", "pr1", "pd3", "pd4", "pr2", "pd5", "dw0", "fin3", "fin4", "uo0", "uu0", "fin5",
    "uu1",
)
CUT_FORWARD = (0, 0, 0, 0, 0, 0)


def phi(z, dh, dl, on, scale):
    s = z * scale
    sh, sl = split2(s)
    rows = dot(jnp.concatenate([sh, sl], 1), jnp.concatenate([dh, dh], 1), NT) + dot(sh, dl, NT)
    half = dot(jnp.concatenate(split2(s * s * 0.5), 1), on)
    return jnp.exp(rows - half) * (dh.shape[0] // 2) ** -0.5


def fwd_attend(S, span, i, bias_ref, q_s, k_s, v_s, mask_s, t_s, w_s, vv_s, att_ref, inv_ref):
    lanes = pl.ds(pl.multiple_of(i * 128, 128), 128)
    CH = span
    coefs(bias_ref, i, t_s, span)
    vv_s[:, :128] = v_s[:, lanes]
    for a in range(S // SB):
        rs = slice(a * SB, (a + 1) * SB)
        qq = jnp.concatenate(halves(q_s[S + a * SB:S + (a + 1) * SB, lanes]), 0)
        for c in range(0, span, CH):
            s = dot(qq, k_s[a * SB + c:a * SB + c + CH, lanes], NT)
            m = mask_s[rs, c:c + CH]
            for h in range(2):
                hs = slice(h * SB, (h + 1) * SB)
                w_s[a % 2, hs, c:c + CH] = (s[hs] * (t_s[hs, c:c + CH] * m)).astype(BF16)
        o = dot(w_s[a % 2], vv_s[a * SB:a * SB + span, :])
        inv = 1.0 / pick(o[:SB, 128:], o[SB:, 128:])
        att_ref[rs, lanes] = pick(o[:SB, :128], o[SB:, :128]) * inv
        inv_ref[rs, lanes] = inv


def forward_kernel(n_seq, chunks, scale, wq_ref, wo_ref, wu_ref, wd_ref, vq_ref, vu_ref, v1_ref, v2_ref, v3_ref, v4_ref, v5_ref, v6_ref, x_ref, pad_ref, bias_ref, draws_ref, len_ref,
                   qkv_h, out_h, up_h, zq_h, zk_h, q_h, k_h, v_h, att_h, inv_h, vec_ref, pk_ref, col_ref,
                   qkv_ref, out_ref, up_ref, zq_ref, zk_ref, q_ref, k_ref, v_ref, att_ref, inv_ref,
                   own_s, G, XR, P3, pad_s, mask_s, t_s, w_s, vv_s, dm_s, snd, rcv, hsnd, hrcv, dsnd, drcv, osem, vb_s):
    S, W = x_ref.shape
    f = wo_ref.shape[0]
    win = bias_ref.shape[1]
    span = win + SB
    wide = 256
    p = Place(n_seq)
    g = Gather(p, own_s, G, snd, rcv, chunks)

    def placed(v, n):
        return pltpu.roll(jnp.broadcast_to(v, (8, v.shape[1])), p.me * n, 1)[:1]

    def thirds(v, j):
        return jnp.concatenate([v[:, t * W + j * wide:t * W + (j + 1) * wide] for t in range(3)], 1)

    wq = wq_ref[...].astype(F32)
    vb_s[...] = jnp.zeros_like(vb_s)
    for i, r in enumerate((vq_ref, vu_ref, v1_ref, v2_ref, v3_ref, v4_ref, v5_ref, v6_ref)):
        vb_s[i:i + 1, :r.shape[1]] = r[...].astype(F32)
    b3 = placed(vb_s[0:1, :3 * W], 3 * f)
    b4 = placed(vb_s[1:2, :], 4 * f)
    singles = pltpu.roll(vb_s[:, :W], p.me * f, 1)[2:8]
    rest = [[b4[:, j * W:(j + 1) * W] for j in range(4)] + [singles[0:3]], [singles[3:6], jnp.zeros((4, W), F32)], [jnp.zeros((7, W), F32)]]
    for j in range(3):
        own_s[j * SLAB:(j + 1) * SLAB, :] = jnp.concatenate([thirds(wq, j), thirds(b3, j)] + rest[j], 0).astype(BF16)
    wide_up = [wu_ref[:, j * W:(j + 1) * W].astype(F32) for j in range(4)]
    own_s[3 * SLAB:4 * SLAB, :] = jnp.concatenate([wo_ref[...].astype(F32), jnp.zeros((SLAB - f, W), F32)], 0).astype(BF16)
    own_s[4 * SLAB:, :] = jnp.concatenate(wide_up, 0).astype(BF16)
    pad_s[...] = jnp.broadcast_to(pad_ref[...], pad_s.shape)
    p.greet(True)
    partner, has = p.partner()
    mine, theirs = 2 * p.c, 2 - 2 * p.c
    leaving = []

    def leave(src, dst):
        c = pltpu.make_async_copy(src, dst, osem.at[len(leaving)])
        c.start()
        leaving.append(c)

    halo = (remote(x_ref, XR, hsnd.at[0], hrcv.at[0], partner), remote(pad_s, P3.at[theirs], hsnd.at[1], hrcv.at[1], partner))
    halo_in = remote(pad_s, P3.at[mine], hsnd.at[1], hrcv.at[1], partner)
    pads = remote(pad_s, P3.at[mine], hsnd.at[2], hrcv.at[2], p.sibling())
    pads_in = remote(pad_s, P3.at[theirs], hsnd.at[2], hrcv.at[2], p.sibling())
    own_rows, far, near = pl.ds(S, S), pl.ds(pl.multiple_of(mine * S, S), S), pl.ds(pl.multiple_of(theirs * S, S), S)
    given = [remote(r.at[own_rows], r.at[far], hsnd.at[3 + i], hrcv.at[3 + i], p.sibling()) for i, r in enumerate((k_ref, v_ref, q_ref))]
    taken = [remote(r.at[own_rows], r.at[near], hsnd.at[3 + i], hrcv.at[3 + i], p.sibling()) for i, r in enumerate((k_ref, v_ref, q_ref))]
    pads.start()

    def send_halo(_):
        @pl.when(has)
        def _():
            for h in halo:
                h.start()

    def take_halo(_):
        @pl.when(has)
        def _():
            halo[0].wait_recv()
            halo_in.wait_recv()

        @pl.when(jnp.logical_not(has))
        def _():
            XR[...] = jnp.zeros_like(XR)
            P3[mine] = jnp.zeros(pad_s.shape, jnp.int32)

    G[p.z, p.y, p.c, p.x] = own_s[...]
    P3[1] = pad_s[...]

    def down(j):
        return remote(wd_ref, col_ref.at[p.z], dsnd.at[j - 1], drcv.at[j - 1], p.zpeer(j))

    def down_in(j):
        return remote(wd_ref, col_ref.at[p.zx(j)], dsnd.at[j - 1], drcv.at[j - 1], p.zpeer(j))

    def send_down(_):
        for j in range(1, p.Z):
            down(j).start()

    def take_down(_):
        for j in range(1, p.Z):
            down_in(j).wait_recv()

    col_ref[p.z] = wd_ref[...]

    def early(_):
        fill_features(dm_s, draws_ref)
        vv_s[:, 128:] = jnp.ones((vv_s.shape[0], 128), BF16)

    on = ones_per_head()

    def features(z, i):
        return phi(z, dm_s[0, i], dm_s[1, i], on, scale).astype(BF16)

    def project(j):
        cs = slice(j * wide, (j + 1) * wide)
        unpack_qkv(g, j, qkv_ref, vec_ref)
        bias = vec_ref[8 * j:8 * j + 1, :]
        x = x_ref[...]
        zq = dot(x, qkv_ref[j, :, :wide]) + bias[:, :wide]
        zk = dot(x, qkv_ref[j, :, wide:2 * wide]) + bias[:, wide:2 * wide]
        zq_ref[:, cs] = zq
        zk_ref[:, cs] = zk
        for i in range(wide // 128):
            pp, at = wide // 128 * j + i, slice(i * 128, (i + 1) * 128)
            lanes = slice(pp * 128, (pp + 1) * 128)
            q_ref[S:2 * S, lanes] = features(zq[:, at], pp)
            k_ref[S:2 * S, lanes] = features(zk[:, at], pp)
        v_ref[S:2 * S, cs] = (dot(x, qkv_ref[j, :, 2 * wide:]) + bias[:, 2 * wide:]).astype(BF16)
        leave(qkv_ref.at[j], qkv_h.at[j])
        for a, b in ((zq_ref, zq_h), (zk_ref, zk_h)):
            leave(a.at[:, cs], b.at[:, cs])

    def give(_):
        for c in given:
            c.start()

    def band(_):
        pads_in.wait_recv()
        pk_ref[...] = jnp.concatenate([P3[0, :1], P3[1, :1], P3[2, :1]], 1)
        fill_band(mask_s, len_ref, pk_ref[...], p.s * S, win // 2)

    def rim(j):
        cs = slice(j * wide, (j + 1) * wide)
        bias = vec_ref[8 * j:8 * j + 1, :]
        x = XR[...]
        zq = dot(x, qkv_ref[j, :, :wide]) + bias[:, :wide]
        zk = dot(x, qkv_ref[j, :, wide:2 * wide]) + bias[:, wide:2 * wide]
        for i in range(wide // 128):
            pp = wide // 128 * j + i
            q_ref[far, pp * 128:(pp + 1) * 128] = features(zq[:, i * 128:(i + 1) * 128], pp)
            k_ref[far, pp * 128:(pp + 1) * 128] = features(zk[:, i * 128:(i + 1) * 128], pp)
        v_ref[far, cs] = (dot(x, qkv_ref[j, :, 2 * wide:]) + bias[:, 2 * wide:]).astype(BF16)
        if j == 2:
            for a, b in ((q_ref, q_h), (k_ref, k_h), (v_ref, v_h)):
                leave(a, b)

    def take(_):
        for c in taken:
            c.wait_recv()

    def pairs(j):
        def pair(i, _):
            fwd_attend(S, span, i, bias_ref, q_ref, k_ref, v_ref, mask_s, t_s, w_s, vv_s, att_ref, inv_ref)
            return 0

        lax.fori_loop(2 * j, 2 * j + 2, pair, 0)
        cs = slice(j * wide, (j + 1) * wide)
        for a, b in ((att_ref, att_h), (inv_ref, inv_h)):
            leave(a.at[:, cs], b.at[:, cs])

    def unpack_up(i):
        k = 4 + i
        lo, n, _ = chunks[k]
        first = (lo - 4 * SLAB) // f

        def put(at, j, v):
            up_ref[at, (first + j) * W:(first + j + 1) * W] = v

        shard_pairs(G, lo, n, f, put)
        cs = slice(first * W, first * W + n // f * W)
        leave(up_ref.at[:, cs], up_h.at[:, cs])

    def unpack_out(_):
        def put(at, j, v):
            out_ref[at, :] = v

        shard_pairs(G, 3 * SLAB, f, f, put)
        leave(out_ref, out_h)

    play(FORWARD, dict(
        bx=g.bx, by=g.by, bz=g.bz, pzx=g.pzx, pzy=g.pzy, px=g.px, pd=g.pd, fin=g.fin, H=send_halo, hw=take_halo, pre=early, po=project,
        KV=give, kvw=take, mask=band, rim=rim, pr=pairs, uo=unpack_out, uu=unpack_up, dz=send_down, dw=take_down))

    @pl.when(has)
    def _():
        for h in halo:
            h.wait_send()
    for c in given + [pads] + [down(j) for j in range(1, p.Z)]:
        c.wait_send()
    g.drain()
    for c in leaving:
        c.wait()


def shard_pairs(G, lo, n, f, put):
    def one(s, _):
        full = pl.ds(lo, (n + 15) // 16 * 16)
        at = (s // 4, lax.rem(s // 2, 2), lax.rem(s, 2))
        a, b = (G[at + (x, full)].astype(F32) for x in range(2))
        rows = pl.ds(pl.multiple_of(s * 2 * f, 2 * f), 2 * f)
        for j in range(n // f):
            put(rows, j, jnp.concatenate([a[j * f:(j + 1) * f], b[j * f:(j + 1) * f]], 0).astype(BF16))
        return 0

    lax.fori_loop(0, 4 * G.shape[0], one, 0)


def unpack_qkv(g, j, qkv_ref, vec_ref):
    G = g.G
    f = qkv_ref.shape[1] // (8 * G.shape[0])
    lo = j * SLAB

    def one(s, t):
        at = (s // 4, lax.rem(s // 2, 2), lax.rem(s, 2))
        a, b = (G[at + (x, pl.ds(lo, SLAB))].astype(F32) for x in range(2))
        qkv_ref[j, pl.ds(pl.multiple_of(s * 2 * f, 2 * f), 2 * f), :] = jnp.concatenate([a[:f], b[:f]], 0).astype(BF16)
        return t + a[f:] + b[f:]

    vec_ref[8 * j:8 * j + 8, :] = lax.fori_loop(0, 4 * G.shape[0], one, jnp.zeros((SLAB - f, G.shape[-1]), F32))


def forward(n_seq, wq, wo, wu, wd, vectors, x, pad, bias, draws, lens):
    S, W = x.shape
    f = wo.shape[0]
    win = bias.shape[1]
    span = win + SB
    KS = S + win
    Z = n_seq // 4
    R = 4 * SLAB + 4 * f
    chunks = tuple((SLAB * k, SLAB, CUT_FORWARD[k]) for k in range(4)) + tuple((4 * SLAB + 2 * f * k, 2 * f, CUT_FORWARD[4 + k]) for k in range(2))
    V = pltpu.VMEM
    M = Gather.sems(Z)
    D = f * 2 * n_seq
    sd = jax.ShapeDtypeStruct
    heads, feats, dims = draws.shape
    K = len(chunks)
    large = (sd((3, D, W), BF16), sd((D, W), BF16), sd((D, 4 * W), BF16), sd((S, W), F32), sd((S, W), F32),
             sd((KS, W), BF16), sd((KS, W), BF16), sd((KS, W), BF16), sd((S, W), F32), sd((S, W), F32))
    return pl.pallas_call(
        functools.partial(forward_kernel, n_seq, chunks, dims ** -0.25),
        out_shape=large + (sd((24, W), F32), sd((1, KS), jnp.int32), sd((Z, 4 * f, W), BF16)),
        in_specs=vmem(16) + [pl.BlockSpec(memory_space=pltpu.SMEM)], out_specs=(pl.BlockSpec(memory_space=pl.ANY),) * len(large) + tuple(vmem(3)),
        scratch_shapes=[V(s.shape, s.dtype) for s in large] + [
            V((R, W), BF16), V((Z, 2, 2, 2, R, W), BF16), V((S, W), BF16), V((3, 8, S), jnp.int32), V((8, S), jnp.int32),
            V((S, span), F32), V((2 * SB, span), F32), V((2, 2 * SB, span), BF16), V((KS, 256), BF16),
            V((2, heads // 2, 2 * feats, 2 * dims), BF16), dma(K, M), dma(K, M), dma(6), dma(6), dma(Z - 1), dma(Z - 1), dma(24), V((8, 4 * W), F32)],
        compiler_params=pltpu.CompilerParams(collective_id=1, has_side_effects=True, vmem_limit_bytes=60 << 20),
        name="forward",
    )(wq, wo, wu, wd, *vectors, x, pad, bias, draws, lens)


DOWN_PARTS = 3
CUT_DOWN = 16


def lane_mean(v):
    return jnp.mean(v, 1, keepdims=True)


def rows_loop(total, step, body):
    def one(i, c):
        body(pl.ds(pl.multiple_of(i * step, step), step))
        return c

    lax.fori_loop(0, total // step, one, 0)


def fold8(v):
    return jnp.sum(v.reshape(v.shape[0] // 8, 8, v.shape[1]), 0)


def normal_cdf_pdf(x):
    u = jnp.abs(x) * 0.7071067811865476
    t = 1.0 / (1.0 + 0.3275911 * u)
    e = jnp.exp(-0.5 * x * x)
    poly = t * (0.254829592 + t * (-0.284496736 + t * (1.421413741 + t * (-1.453152027 + t * 1.061405429))))
    tail = 0.5 * poly * e
    return jnp.where(x >= 0, 1.0 - tail, tail), e * 0.3989422804014327


def middle_kernel(n_seq, heads, col_ref, x_ref, vec_ref, ct_h, att_h, inv_h, ow_h, up_h, out_ref, g1_ref, gw_ref, gt_ref, vg_ref, P_h,
                  ct_ref, att_ref, inv_ref, ow_ref, up_ref, P_ref,
                  al_s, hl_s, hlt_s, h1_s, n1_s, i1_s, act_s, dg_s, gi_s, r_s, gl_s, acc_s, G, snd, rcv, lsem, osem):
    S, W = x_ref.shape
    FF_ = up_ref.shape[1]
    n_dev = P_ref.shape[0]
    f = W // n_dev
    RB = 256
    p = Place(n_seq)
    loads = [pltpu.make_async_copy(a, b, lsem.at[i]) for i, (a, b) in enumerate(
        ((att_h, att_ref), (ow_h, ow_ref), (up_h, up_ref), (ct_h, ct_ref), (inv_h, inv_ref)))]
    for c in loads:
        c.start()
    part = 4 * f // DOWN_PARTS
    g = Gather(p, col_ref, G, snd, rcv, tuple((part * k, part, CUT_DOWN) for k in range(DOWN_PARTS)))
    p.greet(False)
    G[:, p.y, p.c, p.x] = col_ref[...]
    for k in range(DOWN_PARTS):
        for j in range(p.Z):
            g.direct(k, j)
    for k in range(DOWN_PARTS):
        g.give(k, 0)
    b_out, gain_a, shift_a, b_down, gain_f, shift_f = (vec_ref[i:i + 1] for i in (5, 6, 7, 9, 10, 11))
    acc_s[...] = jnp.zeros_like(acc_s)

    def cast(rs):
        al_s[rs, :] = att_ref[rs, :].astype(BF16)

    loads[0].wait()
    rows_loop(S, RB, cast)
    loads[1].wait()
    r_s[...] = dot(al_s[...], ow_ref[...])

    def norm_one(rs):
        r = r_s[rs, :] + (x_ref[rs, :].astype(F32) + b_out)
        c = r - lane_mean(r)
        inv = lax.rsqrt(lane_mean(c * c) + EPS)
        n = c * inv
        n1_s[rs, :] = n
        i1_s[rs, :] = jnp.broadcast_to(inv, (RB, 128))
        h = n * gain_a + shift_a
        h1_s[rs, :] = h
        hl_s[rs, :] = h.astype(BF16)

    rows_loop(S, RB, norm_one)
    loads[2].wait()
    hlt_s[...] = hl_s[...].T
    CW = W // 2
    between = {1: ((g.px, 0),), 2: ((g.px, 1),), 3: ((g.px, 2),), 5: ((g.pd, 0),), 6: ((g.pd, 1),), 7: ((g.pd, 2),)}
    for j in range(FF_ // CW):
        cs = slice(j * CW, (j + 1) * CW)
        inner = dot(hl_s[...], up_ref[:, cs]) + vec_ref[1 + j // 2:2 + j // 2, j % 2 * CW:(j % 2 + 1) * CW]
        cdf, pdf = normal_cdf_pdf(inner)
        act_s[:, cs] = (inner * cdf).astype(BF16)
        dg_s[:, cs] = cdf + inner * pdf
        for step, k in between.get(j, ()):
            step(k)
    for k in range(DOWN_PARTS):
        g.fin(k)
    r_s[...] = dot(act_s[...], G[...].reshape(FF_, W))

    def norm_two(rs):
        r = r_s[rs, :] + (h1_s[rs, :] + b_down)
        c = r - lane_mean(r)
        inv = lax.rsqrt(lane_mean(c * c) + EPS)
        n = c * inv
        out_ref[rs, :] = (n * gain_f + shift_f).astype(BF16)
        ct = ct_ref[rs, :].astype(F32)
        acc_s[0] += fold8(ct * n)
        acc_s[1] += fold8(ct)
        gy = ct * gain_f
        gr = inv * (gy - lane_mean(gy) - n * lane_mean(gy * n))
        r_s[rs, :] = gr
        gl = gr.astype(BF16)
        gl_s[rs, :] = gl
        acc_s[2] += fold8(gl.astype(F32))

    loads[3].wait()
    rows_loop(S, RB, norm_two)
    block = FF_ // p.Z

    def leave(i, lo, n):
        rows = pl.ds(lo, n)
        c = pltpu.make_async_copy(P_ref.at[:, rows], P_h.at[:, rows], osem.at[i])
        c.start()
        leaving.append(c)

    leaving = []
    per = n_dev // p.Z
    for j in range(p.Z):
        gd = dot(act_s[:, j * block:(j + 1) * block], gl_s[...], TN)
        P_ref[j * per:(j + 1) * per, :4 * f, :] = gd.reshape(per, 4 * f, W).astype(BF16)
    leave(0, 0, 4 * f)
    vg_ref[...] = jnp.zeros_like(vg_ref)
    for j in range(p.Z):
        cs = slice(j * block, (j + 1) * block)
        gi = (dot(gl_s[...], G[j].reshape(block, W), NT) * dg_s[:, cs]).astype(BF16)
        gi_s[:, cs] = gi
    for j in range(FF_ // W):
        vg_ref[1 + j:2 + j, :] = jnp.sum(gi_s[:, j * W:(j + 1) * W].astype(F32), 0, keepdims=True)
    for i in range(2):
        parts = [dot(hlt_s[...], gi_s[:, k * W:(k + 1) * W]).reshape(n_dev, f, W) for k in (2 * i, 2 * i + 1)]
        P_ref[:, 4 * f + 2 * f * i:4 * f + 2 * f * (i + 1), :] = jnp.concatenate(parts, 1).astype(BF16)
        leave(1 + i, 4 * f + 2 * f * i, 2 * f)
    r_s[...] += dot(gi_s[...], up_ref[...], NT)

    def back_one(rs):
        gr = r_s[rs, :]
        n = n1_s[rs, :]
        acc_s[3] += fold8(gr * n)
        acc_s[4] += fold8(gr)
        gy = gr * gain_a
        inv = i1_s[rs, :1]
        go = inv * (gy - lane_mean(gy) - n * lane_mean(gy * n))
        g1_ref[rs, :] = go
        gl = go.astype(BF16)
        gl_s[rs, :] = gl
        acc_s[5] += fold8(gl.astype(F32))

    rows_loop(S, RB, back_one)
    for row, i in ((10, 0), (11, 1), (9, 2), (6, 3), (7, 4), (5, 5)):
        vg_ref[row:row + 1, :] = jnp.sum(acc_s[i], 0, keepdims=True)
    go = dot(al_s[...], gl_s[...], TN).reshape(n_dev, f, W)
    P_ref[:, 8 * f:, :] = jnp.concatenate([go, jnp.zeros((n_dev, SLAB - f, W), F32)], 1).astype(BF16)
    leave(3, 8 * f, SLAB)
    r_s[...] = dot(gl_s[...], ow_ref[...], NT)
    of_head = lax.broadcasted_iota(jnp.int32, (W, 128), 0) // (W // heads) == lax.broadcasted_iota(jnp.int32, (W, 128), 1)
    of_head = jnp.where(of_head, 1.0, 0.0).astype(BF16)

    def weighted(rs):
        g = r_s[rs, :] * inv_ref[rs, :]
        gw_ref[rs, :] = g.astype(BF16)
        hi, lo = split2(g * att_ref[rs, :])
        total = -(dot(hi, of_head) + dot(lo, of_head))
        hi = total.astype(BF16).astype(F32)
        gt_ref[rs, :] = (hi + pltpu.roll(total - hi, heads, 1)).astype(BF16)

    loads[4].wait()
    rows_loop(S, RB, weighted)
    g.drain()
    for c in leaving:
        c.wait()


def middle(n_seq, heads, col, x, ct, att, inv, ow, up, vec):
    S, W = x.shape
    FF_ = up.shape[1]
    n_dev = 2 * n_seq
    f = W // n_dev
    Z = n_seq // 4
    V = pltpu.VMEM
    sd = jax.ShapeDtypeStruct
    return pl.pallas_call(
        functools.partial(middle_kernel, n_seq, heads),
        out_shape=(sd((S, W), BF16), sd((S, W), F32), sd((S, W), BF16), sd((S, 128), BF16), sd((24, W), F32), sd((n_dev, 8 * f + SLAB, W), BF16)),
        in_specs=vmem(3) + [pl.BlockSpec(memory_space=pl.ANY)] * 5, out_specs=tuple(vmem(5)) + (pl.BlockSpec(memory_space=pl.ANY),),
        scratch_shapes=[V((S, W), BF16), V((S, W), F32), V((S, W), F32), V((W, W), BF16), V((W, FF_), BF16), V((n_dev, 8 * f + SLAB, W), BF16),
                        V((S, W), BF16), V((S, W), BF16), V((W, S), BF16), V((S, W), F32), V((S, W), F32), V((S, 128), F32),
                        V((S, FF_), BF16), V((S, FF_), F32), V((S, FF_), BF16), V((S, W), F32), V((S, W), BF16), V((6, 8, W), F32),
                        V((Z, 2, 2, 2, 4 * f, W), BF16), dma(DOWN_PARTS, Gather.sems(Z)), dma(DOWN_PARTS, Gather.sems(Z)), dma(5), dma(4)],
        compiler_params=pltpu.CompilerParams(collective_id=2, has_side_effects=True, vmem_limit_bytes=60 << 20),
        name="middle",
    )(col, x, vec, ct, att, inv, ow, up)


BACKWARD = (
    "b0", "b1", "H0", "pre0", "c0", "pr0", "c1", "b2", "pr1", "o0", "c2", "pr2", "b4", "hw0", "o1", "b3", "ri0", "v0", "c3",
    "t0", "o2", "pj0", "c4", "b5", "v1", "t1", "ri1", "o3", "t2", "pj1", "c5", "b6", "o4", "t3", "ri2", "o5", "t4", "c6", "pj2",
    "b7", "t5", "v2", "o6", "v3", "c7", "t6", "f2", "v4", "f1", "o7", "f5", "t7", "f3", "f0", "gx0", "f4", "f6", "v5", "f7",
)
CUT_BACKWARD = (48, 32, 32, 32, 16, 16, 16, 16)


def head_rows(gw, gt, i, heads):
    lane = lax.broadcasted_iota(jnp.int32, gt.shape, 1)
    rows = []
    for h, g in enumerate(halves(gw)):
        mine = jnp.logical_or(lane == 2 * i + h, lane == 2 * i + h + heads)
        rows.append(jnp.concatenate([g, jnp.where(mine, gt, jnp.zeros_like(gt))], 1))
    return jnp.concatenate(rows, 0)


def back_own(S, span, win, heads, i, bias_ref, q_ref, k_ref, v_ref, gw_s, gt_s, mask_s, t_s, w_s, gs_s, p_s, vv_s, gkt_s, gvt_s, gq_s, bsum):
    lanes = pl.ds(pl.multiple_of(i * 128, 128), 128)
    CH = span // 3
    half = win // 2
    coefs(bias_ref, i, t_s, span)
    vv_s[:, :128] = v_ref[:, lanes]
    for a in range(S // SB):
        rs, qs = slice(a * SB, (a + 1) * SB), slice(S + a * SB, S + (a + 1) * SB)
        qq = jnp.concatenate(halves(q_ref[qs, lanes]), 0)
        gg = head_rows(gw_s[qs, lanes], gt_s[qs, :], i, heads)
        for c in range(0, span, CH):
            s = dot(qq, k_ref[a * SB + c:a * SB + c + CH, lanes], NT)
            g = dot(gg, vv_s[a * SB + c:a * SB + c + CH, :], NT)
            m = mask_s[rs, c:c + CH]
            for h in range(2):
                hs = slice(h * SB, (h + 1) * SB)
                cm = t_s[hs, c:c + CH] * m
                w = s[hs] * cm
                w_s[hs, c:c + CH] = w.astype(BF16)
                gs_s[hs, c:c + CH] = (g[hs] * cm).astype(BF16)
                pw = g[hs] * w
                if a == 0:
                    p_s[hs, c:c + CH] = pw
                else:
                    p_s[hs, c:c + CH] += pw
        gq = dot(gs_s[...], k_ref[a * SB:a * SB + span, lanes])
        gq_s[rs, lanes] = pick(gq[:SB], gq[SB:])
        cols = slice(half - a * SB, half - a * SB + S)
        gk, gv = dot(qq, gs_s[:, cols], TN), dot(gg[:, :128], w_s[:, cols], TN)
        if a == 0:
            gkt_s[i], gvt_s[i] = gk, gv
        else:
            gkt_s[i] += gk
            gvt_s[i] += gv
    for h in range(2):
        bsum[pl.ds(2 * i + h, 1), :] = unskew(p_s[h * SB:(h + 1) * SB, :], win)


def back_rim(S, span, heads, i, bias_ref, q_ref, k_ref, v_ref, gw_s, gt_s, maskr_s, t_s, w_s, gs_s, vv_s, gkt_s, gvt_s):
    lanes = pl.ds(pl.multiple_of(i * 128, 128), 128)
    coefs(bias_ref, i, t_s, span)
    vv_s[S:2 * S, :128] = v_ref[S:2 * S, lanes]
    for a in range(S // SB):
        for side, (k0, k1, t0) in enumerate(((0, (a + 1) * SB, span - (a + 1) * SB), (a * SB, S, 0))):
            n = k1 - k0
            qs = slice(2 * S * side + a * SB, 2 * S * side + (a + 1) * SB)
            qq = jnp.concatenate(halves(q_ref[qs, lanes]), 0)
            gg = head_rows(gw_s[qs, lanes], gt_s[qs, :], i, heads)
            s = dot(qq, k_ref[S + k0:S + k1, lanes], NT)
            g = dot(gg, vv_s[S + k0:S + k1, :], NT)
            m = maskr_s[side, a * SB:(a + 1) * SB, k0:k1]
            for h in range(2):
                hs = slice(h * SB, (h + 1) * SB)
                cm = t_s[hs, t0:t0 + n] * m
                w_s[hs, :n] = (s[hs] * cm).astype(BF16)
                gs_s[hs, :n] = (g[hs] * cm).astype(BF16)
            gkt_s[i, :, k0:k1] += dot(qq, gs_s[:, :n], TN)
            gvt_s[i, :, k0:k1] += dot(gg[:, :128], w_s[:, :n], TN)


def phi_back(g, feat, z, dh, dl, on, scale):
    t = g * feat.astype(F32)
    th, tl = split2(t)
    back = dot(th, dh) + dot(tl, dh) + dot(th, dl)
    total = dot(jnp.concatenate([th, tl], 1), on)
    return scale * (back - (z * scale) * total)


def backward_kernel(n_seq, chunks, scale, x_ref, pk_ref, bias_ref, draws_ref, len_ref, vg_ref, gw_ref, gt_ref,
                    w_h, q_h, k_h, v_h, zq_h, zk_h, g1_h, P_h,
                    gx_ref, rel_ref, gqkv_ref, gup_ref, gdown_ref, gout_ref, small_ref,
                    w_ref, q_ref, k_ref, v_ref, zq_ref, zk_ref,
                    U, PQ, R0, R1, R2, R3, mask_s, maskr_s, t_s, w_s, gs_s, p_s, vv_s, gkt_s, gvt_s, gq_s, gw_s, gt_s, gp_s, xt_s, dm_s, ex_s,
                    cur, got, snd, rcv, hsnd, hrcv, vsnd, vrcv, lsem):
    S, W = x_ref.shape
    heads, win = bias_ref.shape
    span = win + SB
    n_pair = W // 128
    n_dev = 2 * n_seq
    f = W // n_dev
    wide = 256
    p = Place(n_seq)
    partner, has = p.partner()
    mine, theirs = 2 * p.c, 2 - 2 * p.c
    far, near = pl.ds(pl.multiple_of(mine * S, S), S), pl.ds(pl.multiple_of(theirs * S, S), S)

    def load(src, dst, i):
        return pltpu.make_async_copy(src, dst, lsem.at[i])

    def own_half(k):
        r0, n = chunks[k][:2]
        return load(P_h.at[:, p.c, :, pl.ds(r0, n)], U.at[k % 2, :, :, pl.ds(0, n)], 1 + k % 2)

    residual = load(g1_h, gx_ref, 0)
    early = [load(h, r, 3 + i) for i, (h, r) in enumerate(((q_h, q_ref), (k_h, k_ref), (v_h, v_ref)))]
    late = [load(h, r, 6 + i) for i, (h, r) in enumerate(((zq_h, zq_ref), (zk_h, zk_ref), (w_h, w_ref)))]
    own_half(0).start()
    for c in early:
        c.start()
    own_half(1).start()
    for c in late:
        c.start()
    residual.start()
    p.greet(True)
    sides = ((gw_ref, gw_s), (gt_ref, gt_s))
    out_far = [remote(a, b.at[near], hsnd.at[i], hrcv.at[i], partner) for i, (a, b) in enumerate(sides)]
    in_far = [remote(a, b.at[far], hsnd.at[i], hrcv.at[i], partner) for i, (a, b) in enumerate(sides)]
    out_near = [remote(a, b.at[far], hsnd.at[2 + i], hrcv.at[2 + i], p.sibling()) for i, (a, b) in enumerate(sides)]
    in_near = [remote(a, b.at[near], hsnd.at[2 + i], hrcv.at[2 + i], p.sibling()) for i, (a, b) in enumerate(sides)]

    def send_halo(_):
        for c in out_near:
            c.start()

        @pl.when(has)
        def _():
            for c in out_far:
                c.start()

    def take_halo(_):
        for c in in_near:
            c.wait_recv()

        @pl.when(has)
        def _():
            for c in in_far:
                c.wait_recv()

    def sib(k, zy):
        return P_h.at[zy, 1 - p.c, :, pl.ds(*chunks[k][:2])] if k < 5 else PQ.at[k - 5, zy, 1 - p.c]

    def own(k, zy, x):
        return U.at[k % 2, zy, x, pl.ds(0, chunks[k][1])] if k < 5 else PQ.at[k - 5, zy, p.c, x]

    sc = Scatter(p, sib, own, R0, R1, R2, R3, snd, rcv, chunks)
    on = ones_per_head()

    def prepare(_):
        start = p.s * S
        fill_band(mask_s, len_ref, pk_ref[...], start, win // 2)
        dk = doc_numbers(len_ref, start + lax.broadcasted_iota(jnp.int32, (1, S), 1))
        real = pk_ref[:, S:2 * S] == 1
        for side in range(2):
            dq = doc_numbers(len_ref, start + (2 * side - 1) * S + lax.broadcasted_iota(jnp.int32, (S, 1), 0))
            maskr_s[side] = jnp.where((dq == dk) & real, 1.0, 0.0)
        fill_features(dm_s, draws_ref)
        vv_s[:, 128:] = jnp.ones((vv_s.shape[0], 128), BF16)
        gw_s[S:2 * S, :] = gw_ref[...]
        gt_s[S:2 * S, :] = gt_ref[...]
        xt_s[...] = x_ref[...].T
        cur[0] = jnp.zeros(cur.shape[1:], F32)

        @pl.when(jnp.logical_not(has))
        def _():
            gw_s[far, :] = jnp.zeros((S, W), BF16)
            gt_s[far, :] = jnp.zeros((S, 128), BF16)
        for c in early:
            c.wait()

    def core(k):
        if k < 5:
            own_half(k).wait()
        sc.core(k)
        if k + 2 < 5:
            own_half(k + 2).start()

    def own_pairs(j):
        def one(i, _):
            back_own(S, span, win, heads, i, bias_ref, q_ref, k_ref, v_ref, gw_s, gt_s, mask_s, t_s, w_s, gs_s, p_s, vv_s, gkt_s, gvt_s, gq_s, cur.at[0])
            return 0

        lax.fori_loop(2 * j, 2 * j + 2, one, 0)

    def rim_pairs(j):
        def one(i, _):
            back_rim(S, span, heads, i, bias_ref, q_ref, k_ref, v_ref, gw_s, gt_s, maskr_s, t_s, w_s, gs_s, vv_s, gkt_s, gvt_s)
            return 0

        lax.fori_loop(2 * j, 2 * j + 2, one, 0)

    def project(l):
        if l == 0:
            for c in late[:2]:
                c.wait()

        def one(i, _):
            def at(t):
                return pl.ds(pl.multiple_of(l * W + t * wide + (i - wide // 128 * l) * 128, 128), 128)

            lanes = pl.ds(pl.multiple_of(i * 128, 128), 128)
            gp_s[:, at(0)] = phi_back(gq_s[:, lanes], q_ref[S:2 * S, lanes], zq_ref[:, lanes], dm_s[0, i], dm_s[1, i], on, scale).astype(BF16)
            gp_s[:, at(1)] = phi_back(gkt_s[i].T, k_ref[S:2 * S, lanes], zk_ref[:, lanes], dm_s[0, i], dm_s[1, i], on, scale).astype(BF16)
            gp_s[:, at(2)] = gvt_s[i].T.astype(BF16)
            return 0

        lax.fori_loop(wide // 128 * l, wide // 128 * (l + 1), one, 0)
        cs = slice(l * W, (l + 1) * W)
        sums = jnp.sum(gp_s[:, cs].astype(F32), 0, keepdims=True)
        extra = jnp.concatenate([sums, vg_ref[8 * l + 1:8 * l + 8, :]], 0)
        part = dot(xt_s[...], gp_s[:, cs]).reshape(n_dev, f, W)
        part = jnp.concatenate([part, jnp.broadcast_to(extra[None], (n_dev,) + extra.shape)], 1)
        PQ[l] = part.astype(BF16).reshape(n_seq // 2, 2, 2, SLAB, W)

    def tokens_back(_):
        residual.wait()
        late[2].wait()
        gx_ref[...] += dot(gp_s[:, :W], w_ref[0], NT) + dot(gp_s[:, W:2 * W], w_ref[1], NT) + dot(gp_s[:, 2 * W:], w_ref[2], NT)

    def done(k):
        total = sc.finish(k)
        if k < 2:
            gdown_ref[2 * f * k:2 * f * (k + 1), :] = total
        elif k < 4:
            for j in range(2):
                gup_ref[:, (2 * (k - 2) + j) * W:(2 * (k - 2) + j + 1) * W] = total[j * f:(j + 1) * f]
        elif k == 4:
            gout_ref[...] = total[:f]
        else:
            l = k - 5
            for t in range(3):
                gqkv_ref[:, t * W + l * wide:t * W + (l + 1) * wide] = total[:f, t * wide:(t + 1) * wide]
            ex_s[8 * l:8 * l + 8, :] = total[f:]

    va = SumAll(p, cur, got, vsnd, vrcv)
    n = SumAll.steps(p.Z)

    def sum_step(i):
        if i:
            va.step(i - 1)
        if i < n:
            va.start(i)

    play(BACKWARD, dict(b=sc.begin, c=core, o=sc.one, t=sc.two, f=done, pre=prepare, pr=own_pairs, ri=rim_pairs, H=send_halo, hw=take_halo, pj=project, gx=tokens_back, v=sum_step))
    rel_ref[...] = cur[n][:rel_ref.shape[0]]

    def mine(row, share):
        width = row.shape[1]
        return pltpu.roll(jnp.broadcast_to(row, (8, width)), lax.rem(width - share * p.me, width), 1)[:1, :128]

    ex = ex_s[...]
    small_ref[0:1, :] = mine(jnp.concatenate([ex[8 * l:8 * l + 1, t * wide:(t + 1) * wide] for t in range(3) for l in range(3)], 1), 3 * f)
    small_ref[1:2, :] = mine(jnp.concatenate([ex[k:k + 1] for k in range(1, 5)], 1), 4 * f)
    singles = jnp.concatenate([ex[5:8], ex[9:12], jnp.zeros((2, W), F32)], 0)
    small_ref[2:8, :] = pltpu.roll(singles, lax.rem(W - f * p.me, W), 1)[:6, :128]
    sc.drain()
    for c in out_near:
        c.wait_send()

    @pl.when(has)
    def _():
        for c in out_far:
            c.wait_send()


def backward(n_seq, x, pk, bias, draws, lens, w, q, k, v, vg, zq, zk, gw, gt, g1, P_):
    S, W = x.shape
    KS = k.shape[0]
    heads, win = bias.shape
    feats, dims = draws.shape[1:]
    span = win + SB
    Z = n_seq // 4
    n_pair = W // 128
    f = W // (2 * n_seq)
    first = 8 * f + SLAB
    R = first + 3 * SLAB
    where = tuple((2 * f * k, 2 * f) for k in range(4)) + ((8 * f, SLAB),) + tuple((first + SLAB * l, SLAB) for l in range(3))
    chunks = tuple(w + (h,) for w, h in zip(where, CUT_BACKWARD))
    V = pltpu.VMEM
    hbm = pl.BlockSpec(memory_space=pl.ANY)
    n = SumAll.steps(Z)
    K = len(chunks)
    sd = jax.ShapeDtypeStruct
    return pl.pallas_call(
        functools.partial(backward_kernel, n_seq, chunks, dims ** -0.25),
        out_shape=(sd((S, W), F32), sd((heads, win), F32), sd((f, 3 * W), F32), sd((f, 4 * W), F32), sd((4 * f, W), F32), sd((f, W), F32), sd((8, 128), F32)),
        in_specs=vmem(4) + [pl.BlockSpec(memory_space=pltpu.SMEM)] + vmem(3) + [hbm] * 8, out_specs=tuple(vmem(7)),
        scratch_shapes=[V(a.shape, a.dtype) for a in (w, q, k, v, zq, zk)] + [
            V((2, 2 * Z, 2, 2 * f, W), BF16), V((3, 2 * Z, 2, 2, SLAB, W), BF16)] + Scatter.buffers(Z, R, W) + [
            V((S, span), F32), V((2, S, S), F32), V((2 * SB, span), F32), V((2 * SB, span), BF16), V((2 * SB, span), BF16), V((2 * SB, span), F32),
            V((KS, 256), BF16), V((n_pair, 128, S), F32), V((n_pair, 128, S), F32), V((S, W), F32), V((KS, W), BF16), V((KS, 128), BF16),
            V((S, 3 * W), BF16), V((W, S), BF16),
            V((2, heads // 2, 2 * feats, 2 * dims), BF16), V((24, W), F32), V((n + 1, 16, win), F32), V((n, 16, win), F32),
            dma(K, Scatter.sems(Z)), dma(K, Scatter.sems(Z)), dma(4), dma(4), dma(n), dma(n), dma(9)],
        compiler_params=pltpu.CompilerParams(collective_id=3, has_side_effects=True, vmem_limit_bytes=64 << 20),
        name="backward",
    )(x, pk, bias, draws, lens, vg, gw, gt, w, q, k, v, zq, zk, g1, P_)


def finish_kernel(n, small_ref, *refs):
    for src, dst in zip(refs[:n], refs[n:2 * n]):
        dst[...] = src[...]
    for i, v in enumerate(refs[2 * n:]):
        v[...] = small_ref[i:i + 1, :v.shape[1]]


def finish(f, small, *large):
    sd = jax.ShapeDtypeStruct
    return pl.pallas_call(
        functools.partial(finish_kernel, len(large)),
        out_shape=tuple(sd(a.shape, a.dtype) for a in large) + tuple(sd((1, n), F32) for n in (3 * f, 4 * f) + (f,) * 6),
        name="finish",
    )(small, *large)

EPS = 1e-06
EXACT_MATMUL = lax.Precision.HIGHEST


def padded_2(cells, sides, width):
    for axis, dim in sides:
        count = lax.axis_size(axis)
        ends = count - 1
        head = lax.slice_in_dim(cells, 0, width, axis=dim)
        tail = lax.slice_in_dim(cells, cells.shape[dim] - width, cells.shape[dim], axis=dim)
        cells = jnp.concatenate(
            [
                lax.ppermute(tail, axis, [(i, (i + 1) % count) for i in range(ends)]),
                cells,
                lax.ppermute(head, axis, [((i + 1) % count, i) for i in range(ends)]),
            ],
            axis=dim,
        )
    return cells


def passed_along(block, axis, distance):
    devices = range(lax.axis_size(axis))
    route = [(i - distance, i) for i in devices if i - distance in devices]
    return lax.ppermute(block, axis, route)


def layer_norm(values, gain, shift):
    center = values - jnp.mean(values, -1, keepdims=True)
    spread = jnp.mean(center * center, -1, keepdims=True)
    return center * lax.rsqrt(spread + EPS) * gain + shift


def feature_map(heads_in, random_features):
    scaled_input = heads_in * heads_in.shape[-1] ** (-0.25)
    projected_rows = jnp.einsum(
        "ykb,kib->yki", scaled_input, random_features, precision=EXACT_MATMUL
    )
    half_square = 0.5 * jnp.sum(scaled_input * scaled_input, -1, keepdims=True)
    return jnp.exp(projected_rows - half_square) * random_features.shape[1] ** (-0.5)


def document_numbers(positions, lengths_row):
    ends = jnp.cumsum(lengths_row)
    counted = jnp.sum((positions[:, None] >= ends[None, :]).astype(jnp.int32), -1)
    return jnp.where(positions < 0, -1, counted)


def fits(n_seq, n_row, f, tokens_here, half_win):
    return n_row == 2 and n_seq == 4 * 4 and f + 8 == SLAB and tokens_here == half_win


def with_kernels(tokens, cotangent, lengths, padding, feature_draws, rel_bias, *weights):
    w_qkv, b_qkv, w_out, b_out, gain_a, shift_a, w_up, b_up, w_down, b_down, gain_f, shift_f = weights
    local = tokens[0]
    W = local.shape[1]
    n_seq = lax.axis_size("seq")
    f = w_out.shape[0]
    vectors = [v[None] for v in (b_qkv, b_up, b_out, gain_a, shift_a, b_down, gain_f, shift_f)]
    (qkv_w, out_w, up_w, zq, zk, q, k, v, att, inv, vec, pk, col) = forward(
        n_seq, w_qkv, w_out, w_up, w_down, vectors, local, padding, rel_bias, feature_draws, lengths)
    out, g1, gw, gt, vg, P_ = middle(n_seq, rel_bias.shape[0], col, local, cotangent[0], att, inv, out_w, up_w, vec)
    P_ = P_.reshape(n_seq // 2, 2, 2, P_.shape[1], W)
    gx, rel, g_qkv, g_up, g_down, g_out, small = backward(
        n_seq, local, pk, rel_bias, feature_draws, lengths, qkv_w, q, k, v, vg, zq, zk, gw, gt, g1, P_)
    out, gx, rel, g_qkv, g_up, g_down, g_out, *vec = finish(f, small, out, gx, rel, g_qkv, g_up, g_down, g_out)
    vec = [v[0] for v in vec]
    return (
        out[None], gx[None], rel, g_qkv, vec[0], g_out, vec[2], vec[3], vec[4], g_up, vec[1], g_down, vec[5], vec[6], vec[7],
    )


def on_device(
    tokens,
    cotangent,
    lengths,
    padding,
    feature_draws,
    rel_bias,
    w_qkv,
    b_qkv,
    w_out,
    b_out,
    gain_attn,
    shift_attn,
    w_up,
    b_up,
    w_down,
    b_down,
    gain_ffn,
    shift_ffn,
):
    if fits(lax.axis_size("seq"), lax.axis_size("row"), w_out.shape[0], tokens.shape[1], rel_bias.shape[1] // 2):
        return with_kernels(
            tokens, cotangent, lengths, padding, feature_draws, rel_bias, w_qkv, b_qkv, w_out, b_out, gain_attn, shift_attn,
            w_up, b_up, w_down, b_down, gain_ffn, shift_ffn,
        )
    local = tokens[0]
    seq_len = local.shape[0]
    model_width = local.shape[1]
    head_count = rel_bias.shape[0]
    window_len = rel_bias.shape[1]
    half_win = window_len // 2
    feat_count = feature_draws.shape[1]
    head_dim = model_width // head_count
    feat_cols = head_count * feat_count
    params = (
        lax.all_gather(w_qkv, ("seq", "row"), axis=0, tiled=True),
        lax.all_gather(b_qkv, ("seq", "row"), axis=0, tiled=True),
        lax.all_gather(w_out, ("seq", "row"), axis=0, tiled=True),
        lax.all_gather(b_out, ("seq", "row"), axis=0, tiled=True),
        lax.all_gather(gain_attn, ("seq", "row"), axis=0, tiled=True),
        lax.all_gather(shift_attn, ("seq", "row"), axis=0, tiled=True),
        lax.all_gather(w_up, ("seq", "row"), axis=0, tiled=True),
        lax.all_gather(b_up, ("seq", "row"), axis=0, tiled=True),
        lax.all_gather(w_down, ("seq", "row"), axis=0, tiled=True),
        lax.all_gather(b_down, ("seq", "row"), axis=0, tiled=True),
        lax.all_gather(gain_ffn, ("seq", "row"), axis=0, tiled=True),
        lax.all_gather(shift_ffn, ("seq", "row"), axis=0, tiled=True),
    )
    (
        qkv_w,
        qkv_b,
        out_w,
        out_b,
        first_norm_gain,
        shift_one,
        up_w,
        up_b,
        down_w,
        down_b,
        gain_two,
        shift_two,
    ) = params
    seq_pos = lax.axis_index("seq")
    start_pos = seq_pos * seq_len
    positions = start_pos + jnp.arange(seq_len, dtype=jnp.int32)
    ext_pos = start_pos - half_win + jnp.arange(seq_len + window_len, dtype=jnp.int32)
    doc_query = document_numbers(positions, lengths[0])
    doc_keys = document_numbers(ext_pos, lengths[0])
    pad_local = padding[0]
    pad_ones = jnp.ones((half_win,), jnp.int32)
    pad_keys = jnp.concatenate([pad_ones, pad_local, pad_ones])
    proj_qkv = jnp.dot(local, qkv_w, preferred_element_type=jnp.float32) + qkv_b
    queries = proj_qkv[:, :model_width].reshape(seq_len, head_count, head_dim)
    keys_in = proj_qkv[:, model_width : 2 * model_width].reshape(seq_len, head_count, head_dim)
    q_full, query_back = jax.vjp(partial(feature_map, random_features=feature_draws), queries)
    k_full, key_back = jax.vjp(partial(feature_map, random_features=feature_draws), keys_in)
    q_feat = q_full.astype(jnp.bfloat16)
    k_flat = k_full.astype(jnp.bfloat16).reshape(seq_len, feat_cols)
    values_low = proj_qkv[:, 2 * model_width :].astype(jnp.bfloat16)
    own_keys = jnp.concatenate([k_flat, values_low], 1)
    masked_keys = jnp.concatenate([k_flat * pad_local.astype(jnp.bfloat16)[:, None], values_low], 1)
    rims = padded_2(masked_keys, (("seq", 0),), half_win)
    key_ext = jnp.concatenate([rims[:half_win], own_keys, rims[half_win + seq_len :]], 0)

    dq, dk, pk = doc_query[:, None], doc_keys[None, :], pad_keys[None, :]
    bias8 = bias_rows(rel_bias)
    q_low = q_feat.reshape(seq_len, feat_cols)
    keys_x, vals_x = key_ext[:, :feat_cols], key_ext[:, feat_cols:]
    attended, inv_tot = attn_fwd(dq, dk, pk, bias8, q_low, keys_x, vals_x)
    att_low = attended.astype(jnp.bfloat16)
    branch = jnp.dot(att_low, out_w, preferred_element_type=jnp.float32) + out_b
    resid_one = local.astype(jnp.float32) + branch
    hidden_one, ln_one_back = jax.vjp(
        layer_norm, resid_one, first_norm_gain.astype(jnp.float32), shift_one.astype(jnp.float32)
    )
    hidden_low = hidden_one.astype(jnp.bfloat16)
    inner = jnp.dot(hidden_low, up_w, preferred_element_type=jnp.float32) + up_b
    active, gelu_back = jax.vjp(partial(jax.nn.gelu, approximate=False), inner)
    active_low = active.astype(jnp.bfloat16)
    ffn_out = jnp.dot(active_low, down_w, preferred_element_type=jnp.float32) + down_b
    result, ln_two_back = jax.vjp(
        layer_norm,
        hidden_one + ffn_out,
        gain_two.astype(jnp.float32),
        shift_two.astype(jnp.float32),
    )
    params = (
        lax.all_gather(w_qkv, ("seq", "row"), axis=0, tiled=True),
        lax.all_gather(b_qkv, ("seq", "row"), axis=0, tiled=True),
        lax.all_gather(w_out, ("seq", "row"), axis=0, tiled=True),
        lax.all_gather(b_out, ("seq", "row"), axis=0, tiled=True),
        lax.all_gather(gain_attn, ("seq", "row"), axis=0, tiled=True),
        lax.all_gather(shift_attn, ("seq", "row"), axis=0, tiled=True),
        lax.all_gather(w_up, ("seq", "row"), axis=0, tiled=True),
        lax.all_gather(b_up, ("seq", "row"), axis=0, tiled=True),
        lax.all_gather(w_down, ("seq", "row"), axis=0, tiled=True),
        lax.all_gather(b_down, ("seq", "row"), axis=0, tiled=True),
        lax.all_gather(gain_ffn, ("seq", "row"), axis=0, tiled=True),
        lax.all_gather(shift_ffn, ("seq", "row"), axis=0, tiled=True),
    )
    (
        qkv_w,
        qkv_b,
        out_w,
        out_b,
        first_norm_gain,
        shift_one,
        up_w,
        up_b,
        down_w,
        down_b,
        gain_two,
        shift_two,
    ) = params
    grad_two, grad_gain_two, grad_shift_two = ln_two_back(cotangent[0].astype(jnp.float32))
    grad_two_low = grad_two.astype(jnp.bfloat16)
    grad_down_w = jnp.einsum(
        "ti,tj->ij", active_low, grad_two_low, preferred_element_type=jnp.float32
    )
    grad_down_b = jnp.sum(grad_two_low, 0, dtype=jnp.float32)
    grad_active = jnp.dot(grad_two_low, down_w.T, preferred_element_type=jnp.float32)
    grad_inner_low = gelu_back(grad_active)[0].astype(jnp.bfloat16)
    grad_up_w = jnp.einsum(
        "ti,tj->ij", hidden_low, grad_inner_low, preferred_element_type=jnp.float32
    )
    grad_up_b = jnp.sum(grad_inner_low, 0, dtype=jnp.float32)
    grad_hidden = grad_two + jnp.dot(grad_inner_low, up_w.T, preferred_element_type=jnp.float32)
    grad_one, grad_gain_one, grad_shift_one = ln_one_back(grad_hidden)
    grad_one_low = grad_one.astype(jnp.bfloat16)
    grad_out_w = jnp.einsum("ti,tj->ij", att_low, grad_one_low, preferred_element_type=jnp.float32)
    grad_out_b = jnp.sum(grad_one_low, 0, dtype=jnp.float32)
    grad_att = jnp.dot(grad_one_low, out_w.T, preferred_element_type=jnp.float32)
    grad_fq_all, grad_kf, grad_vv, grad_b8 = attn_bwd(
        dq, dk, pk, bias8, q_low, keys_x, vals_x, attended, inv_tot, grad_att
    )
    grad_bias = grad_b8.reshape(head_count // 2, 8, window_len)[:, :2].reshape(head_count, window_len)
    lower_rim = jnp.concatenate([grad_kf[:half_win], grad_vv[:half_win]], 1)
    upper_rim = jnp.concatenate([grad_kf[half_win + seq_len :], grad_vv[half_win + seq_len :]], 1)
    from_right = passed_along(lower_rim.astype(jnp.bfloat16), "seq", -1).astype(lower_rim.dtype)
    from_left = passed_along(upper_rim.astype(jnp.bfloat16), "seq", 1).astype(upper_rim.dtype)
    returned = from_left + from_right
    pad_float = pad_local.astype(jnp.float32)[:, None]
    grad_kfeat = grad_kf[half_win : half_win + seq_len] + returned[:, :feat_cols] * pad_float
    value_gradient = grad_vv[half_win : half_win + seq_len] + returned[:, feat_cols:]
    grad_queries = query_back(grad_fq_all.reshape(seq_len, head_count, feat_count))[0]
    grad_keys_in = key_back(grad_kfeat.reshape(seq_len, head_count, feat_count))[0]
    grad_proj_low = jnp.concatenate(
        [
            grad_queries.reshape(seq_len, model_width),
            grad_keys_in.reshape(seq_len, model_width),
            value_gradient,
        ],
        1,
    ).astype(jnp.bfloat16)
    grad_qkv_w = jnp.einsum("ti,tj->ij", local, grad_proj_low, preferred_element_type=jnp.float32)
    grad_qkv_b = jnp.sum(grad_proj_low, 0, dtype=jnp.float32)
    grad_input = grad_one + jnp.dot(grad_proj_low, qkv_w.T, preferred_element_type=jnp.float32)
    grad_rel = lax.psum(grad_bias, ("seq", "row"))
    summed = (
        lax.psum_scatter(grad_qkv_w, ("seq", "row"), scatter_dimension=0, tiled=True),
        lax.psum_scatter(grad_qkv_b, ("seq", "row"), scatter_dimension=0, tiled=True),
        lax.psum_scatter(grad_out_w, ("seq", "row"), scatter_dimension=0, tiled=True),
        lax.psum_scatter(grad_out_b, ("seq", "row"), scatter_dimension=0, tiled=True),
        lax.psum_scatter(grad_gain_one, ("seq", "row"), scatter_dimension=0, tiled=True),
        lax.psum_scatter(grad_shift_one, ("seq", "row"), scatter_dimension=0, tiled=True),
        lax.psum_scatter(grad_up_w, ("seq", "row"), scatter_dimension=0, tiled=True),
        lax.psum_scatter(grad_up_b, ("seq", "row"), scatter_dimension=0, tiled=True),
        lax.psum_scatter(grad_down_w, ("seq", "row"), scatter_dimension=0, tiled=True),
        lax.psum_scatter(grad_down_b, ("seq", "row"), scatter_dimension=0, tiled=True),
        lax.psum_scatter(grad_gain_two, ("seq", "row"), scatter_dimension=0, tiled=True),
        lax.psum_scatter(grad_shift_two, ("seq", "row"), scatter_dimension=0, tiled=True),
    )
    return (
        result[None].astype(jnp.bfloat16),
        grad_input[None],
        grad_rel,
        summed[0],
        summed[1],
        summed[2],
        summed[3],
        summed[4],
        summed[5],
        summed[6],
        summed[7],
        summed[8],
        summed[9],
        summed[10],
        summed[11],
    )


def solution(mesh):
    in_specs = (
        P("row", "seq", None),
        P("row", "seq", None),
        P("row", None),
        P("row", "seq"),
        P(),
        P(),
        P(("seq", "row"), None),
        P(("seq", "row")),
        P(("seq", "row"), None),
        P(("seq", "row")),
        P(("seq", "row")),
        P(("seq", "row")),
        P(("seq", "row"), None),
        P(("seq", "row")),
        P(("seq", "row"), None),
        P(("seq", "row")),
        P(("seq", "row")),
        P(("seq", "row")),
    )
    out_specs = (
        P("row", "seq", None),
        P("row", "seq", None),
        P(),
        P(("seq", "row"), None),
        P(("seq", "row")),
        P(("seq", "row"), None),
        P(("seq", "row")),
        P(("seq", "row")),
        P(("seq", "row")),
        P(("seq", "row"), None),
        P(("seq", "row")),
        P(("seq", "row"), None),
        P(("seq", "row")),
        P(("seq", "row")),
        P(("seq", "row")),
    )
    return jax.shard_map(
        on_device, mesh=mesh, in_specs=in_specs, out_specs=out_specs, check_vma=False
    )
```

```python
from functools import partial

import functools
import jax
import jax.numpy as jnp
from jax import lax
from jax.experimental import pallas as pl
from jax.experimental.pallas import tpu as pltpu
from jax.sharding import PartitionSpec as P

F32, BF16 = jnp.float32, jnp.bfloat16
NT = (((1,), (1,)), ((), ()))
TN = (((0,), (0,)), ((), ()))
SB = 128

def dot(a, b, dims=None):
    if dims is None:
        return jnp.dot(a, b, preferred_element_type=F32)
    return lax.dot_general(a, b, dims, preferred_element_type=F32)

def toep(row, width):
    win = row.shape[1]
    wide = jnp.concatenate([row, jnp.zeros((1, width - win), F32)], 1)
    return pltpu.roll(jnp.broadcast_to(wide, (SB, width)), 0, 1, stride=1, stride_axis=0)

def unskew(p, win):
    rows = p.shape[0]; width = p.shape[1]
    while rows > 8:
        rows //= 2
        p = p[:rows] + pltpu.roll(p[rows:], width - rows, 1)
    r = lax.broadcasted_iota(jnp.int32, (8, 1), 0)
    for s in (1, 2, 4):
        p = jnp.where((r & s) != 0, pltpu.roll(p, width - s, 1), p)
    return jnp.sum(p, 0, keepdims=True)[:, :win]

def fill_mask(mask_s, dq_ref, dk_ref, pk_ref, span, half):
    S = mask_s.shape[0]
    for a in range(S // SB):
        dq = dq_ref[a*SB:(a+1)*SB, :]
        dk = dk_ref[:, a*SB:a*SB+span]
        pk = pk_ref[:, a*SB:a*SB+span]
        r = lax.broadcasted_iota(jnp.int32, (SB, span), 0)
        c = lax.broadcasted_iota(jnp.int32, (SB, span), 1)
        ok = (dq == dk) & ((pk == 1) | (c == r + half))
        mask_s[a*SB:(a+1)*SB, :] = jnp.where(ok, 1.0, 0.0)

def halves(x):
    lane = lax.broadcasted_iota(jnp.int32, x.shape, 1)
    z = jnp.zeros_like(x)
    return jnp.where(lane < 64, x, z), jnp.where(lane >= 64, x, z)

def pick(a, b):
    lane = lax.broadcasted_iota(jnp.int32, a.shape, 1)
    return jnp.where(lane < 64, a, b)

def fwd_kernel(CH, dq_ref, dk_ref, pk_ref, bias_ref, q_ref, k_ref, v_ref, att_ref, inv_ref, mask_s, t_s, w_s, v_s):
    S = q_ref.shape[0]; win = bias_ref.shape[1]; span = win + SB
    p = pl.program_id(0)
    @pl.when(p == 0)
    def _():
        fill_mask(mask_s, dq_ref, dk_ref, pk_ref, span, win // 2)
        v_s[:, 128:] = jnp.ones((v_s.shape[0], 128), BF16)
    rows = jnp.exp(bias_ref[pl.ds(pl.multiple_of(p * 8, 8), 8), :])
    for i in range(2):
        t_s[i*SB:(i+1)*SB, :] = toep(rows[i:i+1], span)
    v_s[:, :128] = v_ref[...]
    for a in range(S // SB):
        qa, qb = halves(q_ref[a*SB:(a+1)*SB, :])
        qq = jnp.concatenate([qa, qb], 0)
        for c in range(0, span, CH):
            s = dot(qq, k_ref[a*SB+c:a*SB+c+CH, :], NT)
            m = mask_s[a*SB:(a+1)*SB, c:c+CH]
            t = t_s[:, c:c+CH]
            w_s[:SB, c:c+CH] = (s[:SB] * (t[:SB] * m)).astype(BF16)
            w_s[SB:, c:c+CH] = (s[SB:] * (t[SB:] * m)).astype(BF16)
        o = dot(w_s[...], v_s[a*SB:a*SB+span, :])
        inv = 1.0 / pick(o[:SB, 128:], o[SB:, 128:])
        att_ref[a*SB:(a+1)*SB, :] = pick(o[:SB, :128], o[SB:, :128]) * inv
        inv_ref[a*SB:(a+1)*SB, :] = inv

def bias_rows(rel_bias):
    h, w = rel_bias.shape
    x = rel_bias.reshape(h // 2, 2, w)
    return jnp.pad(x, ((0, 0), (0, 6), (0, 0))).reshape(h // 2 * 8, w)

def attn_fwd(dq, dk, pk, bias8, q, k, v, CH=384):
    S, D = q.shape; KS = k.shape[0]; win = bias8.shape[1]; span = win + SB
    full = lambda *s: pl.BlockSpec(s, lambda p: (0,) * len(s))
    col = lambda n: pl.BlockSpec((n, 128), lambda p: (0, p))
    return pl.pallas_call(
        functools.partial(fwd_kernel, CH),
        grid=(D // 128,),
        out_shape=(jax.ShapeDtypeStruct((S, D), F32), jax.ShapeDtypeStruct((S, D), F32)),
        in_specs=[full(S, 1), full(1, KS), full(1, KS), full(*bias8.shape), col(S), col(KS), col(KS)],
        out_specs=(col(S), col(S)),
        scratch_shapes=[pltpu.VMEM((S, span), F32), pltpu.VMEM((2*SB, span), F32), pltpu.VMEM((2*SB, span), BF16), pltpu.VMEM((KS, 256), BF16)],
        compiler_params=pltpu.CompilerParams(vmem_limit_bytes=48 << 20),
        name="attn_fwd",
    )(dq, dk, pk, bias8, q, k, v)

def bwd_kernel(CH, dq_ref, dk_ref, pk_ref, bias_ref, q_ref, k_ref, v_ref, att_ref, inv_ref, ga_ref,
               gq_ref, gk_ref, gv_ref, gb_ref, mask_s, t_s, w_s, gs_s, p_s, v_s, gk_s, gv_s):
    S = q_ref.shape[0]; win = bias_ref.shape[1]; span = win + SB
    p = pl.program_id(0)
    @pl.when(p == 0)
    def _():
        fill_mask(mask_s, dq_ref, dk_ref, pk_ref, span, win // 2)
        v_s[:, 128:] = jnp.ones((v_s.shape[0], 128), BF16)
    rows = jnp.exp(bias_ref[pl.ds(pl.multiple_of(p * 8, 8), 8), :])
    for i in range(2):
        t_s[i*SB:(i+1)*SB, :] = toep(rows[i:i+1], span)
    v_s[:, :128] = v_ref[...]
    gk_s[...] = jnp.zeros_like(gk_s)
    gv_s[...] = jnp.zeros_like(gv_s)
    for a in range(S // SB):
        rs = slice(a*SB, (a+1)*SB)
        qa, qb = halves(q_ref[rs, :])
        qq = jnp.concatenate([qa, qb], 0)
        ga = ga_ref[rs, :]
        inv = inv_ref[rs, :]
        gw = (ga * inv).astype(BF16)
        gwa, gwb = halves(gw)
        pr = ga * att_ref[rs, :] * inv
        pa, pb = halves(pr)
        lane = lax.broadcasted_iota(jnp.int32, (SB, 128), 1)
        def ext(x):
            g = -jnp.sum(x, 1, keepdims=True)
            hi = g.astype(BF16)
            lo = (g - hi.astype(F32)).astype(BF16)
            z = jnp.zeros((SB, 128), BF16)
            return jnp.where(lane == 0, hi, jnp.where(lane == 1, lo, z))
        gg = jnp.concatenate([jnp.concatenate([gwa, ext(pa)], 1), jnp.concatenate([gwb, ext(pb)], 1)], 0)
        for c in range(0, span, CH):
            s = dot(qq, k_ref[a*SB+c:a*SB+c+CH, :], NT)
            g = dot(gg, v_s[a*SB+c:a*SB+c+CH, :], NT)
            m = mask_s[rs, c:c+CH]
            for h in range(2):
                hs = slice(h*SB, (h+1)*SB)
                cm = t_s[hs, c:c+CH] * m
                w = s[hs] * cm
                w_s[hs, c:c+CH] = w.astype(BF16)
                gs_s[hs, c:c+CH] = (g[hs] * cm).astype(BF16)
                pw = g[hs] * w
                if a == 0:
                    p_s[hs, c:c+CH] = pw
                else:
                    p_s[hs, c:c+CH] += pw
        gq = dot(gs_s[...], k_ref[a*SB:a*SB+span, :])
        gq_ref[rs, :] = pick(gq[:SB], gq[SB:])
        gk_s[:, a*SB:a*SB+span] += dot(qq, gs_s[...], TN)
        gwq = jnp.concatenate([gwa, gwb], 0)
        gv_s[:, a*SB:a*SB+span] += dot(gwq, w_s[...], TN)
    gk_ref[...] = gk_s[...].T
    gv_ref[...] = gv_s[...].T
    gb_ref[...] = jnp.concatenate([unskew(p_s[:SB, :], win), unskew(p_s[SB:, :], win), jnp.zeros((6, win), F32)], 0)

def attn_bwd(dq, dk, pk, bias8, q, k, v, att, inv, ga, CH=384):
    S, D = q.shape; KS = k.shape[0]; win = bias8.shape[1]; span = win + SB
    full = lambda *s: pl.BlockSpec(s, lambda p: (0,) * len(s))
    col = lambda n: pl.BlockSpec((n, 128), lambda p: (0, p))
    V = pltpu.VMEM
    return pl.pallas_call(
        functools.partial(bwd_kernel, CH),
        grid=(D // 128,),
        out_shape=(jax.ShapeDtypeStruct((S, D), F32), jax.ShapeDtypeStruct((KS, D), F32), jax.ShapeDtypeStruct((KS, D), F32),
                   jax.ShapeDtypeStruct(bias8.shape, F32)),
        in_specs=[full(S, 1), full(1, KS), full(1, KS), full(*bias8.shape), col(S), col(KS), col(KS), col(S), col(S), col(S)],
        out_specs=(col(S), col(KS), col(KS), pl.BlockSpec((8, win), lambda p: (p, 0))),
        scratch_shapes=[V((S, span), F32), V((2*SB, span), F32), V((2*SB, span), BF16), V((2*SB, span), BF16), V((2*SB, span), F32),
                        V((KS, 256), BF16), V((128, KS), F32), V((128, KS), F32)],
        compiler_params=pltpu.CompilerParams(vmem_limit_bytes=56 << 20),
        name="attn_bwd",
    )(dq, dk, pk, bias8, q, k, v, att, inv, ga)


MESH = pl.DeviceIdType.MESH
SLAB = 32


class Place:
    def __init__(self, n_seq):
        self.Z = n_seq // 4
        s, self.x = lax.axis_index("seq"), lax.axis_index("row")
        self.s = s
        self.c, self.y, self.z = lax.rem(s, 2), lax.rem(s // 2, 2), s // 4
        self.me = s * 2 + self.x

    def seq(self, z, y, c):
        return (z * 2 + y) * 2 + c

    def zx(self, k):
        z, d = self.z, 1
        while d <= k:
            if k // d % 2:
                z = z + d - 2 * d * lax.rem(self.z // d, 2)
            d *= 2
        return z

    def sibling(self):
        return (self.seq(self.z, self.y, 1 - self.c), self.x)

    def xpeer(self):
        return (self.s, 1 - self.x)

    def ypeer(self):
        return (self.seq(self.z, 1 - self.y, self.c), self.x)

    def zpeer(self, k):
        return (self.seq(self.zx(k), self.y, self.c), self.x)

    def partner(self):
        t, n = self.s - 1 + 2 * self.c, 4 * self.Z
        return (lax.rem(t + n, n), self.x), jnp.logical_and(t >= 0, t < n)

    def greet(self, partner):
        b = pltpu.get_barrier_semaphore()
        peers = [self.sibling(), self.xpeer(), self.ypeer()] + [self.zpeer(k) for k in range(1, self.Z)]
        if partner:
            peers.append(self.partner()[0])
        for p in peers:
            pl.semaphore_signal(b, inc=1, device_id=p, device_id_type=MESH)
        pl.semaphore_wait(b, len(peers))


def remote(src, dst, snd, rcv, dev):
    return pltpu.make_async_remote_copy(src_ref=src, dst_ref=dst, send_sem=snd, recv_sem=rcv, device_id=dev, device_id_type=MESH)


class Gather:
    def __init__(self, place, own, G, snd, rcv, chunks):
        self.p, self.own, self.G, self.snd, self.rcv, self.chunks = place, own, G, snd, rcv, chunks
        self.sent = []

    @staticmethod
    def sems(Z):
        return 5 * Z + 3

    def _copy(self, k, sem, at, dev, part=None, own=False):
        lo, n = part or self.chunks[k][:2]
        dst = self.G.at[at + (pl.ds(lo, n),)]
        src = self.own.at[pl.ds(lo, n)] if own else dst
        return remote(src, dst, self.snd.at[k, sem], self.rcv.at[k, sem], dev)

    def _send(self, *a, **kw):
        c = self._copy(*a, **kw)
        c.start()
        self.sent.append(c)

    def parts(self, k):
        r0, rows, h = self.chunks[k]
        return (r0, h), (r0 + h, rows - h)

    def at(self, j, fy=0, fx=0):
        p = self.p
        return (p.zx(j), p.y if not fy else 1 - p.y, p.c, p.x if not fx else 1 - p.x)

    def column(self, k, t, other=False):
        p = self.p
        y, x = (1 - p.y if t > 1 else p.y), (1 - p.x if t % 2 else p.x)
        return self._copy(k, 5 * p.Z - 1 + t, (slice(None), y, 1 - p.c if other else p.c, x), p.sibling())

    def give(self, k, t):
        c = self.column(k, t)
        c.start()
        self.sent.append(c)

    def bz(self, k):
        for j in range(1, self.p.Z):
            self._send(k, j - 1, self.at(0), self.p.zpeer(j), own=True)

    def bx(self, k):
        self._send(k, self.p.Z - 1, self.at(0), self.p.xpeer(), own=True)

    def by(self, k):
        self._send(k, 2 * self.p.Z - 1, self.at(0), self.p.ypeer(), own=True)

    def direct(self, k, j):
        p, (lo, n) = self.p, self.chunks[k][:2]
        for sem, dev in ((p.Z - 1 + j, p.xpeer()), (2 * p.Z - 1 + j, p.ypeer())):
            at = self.at(j) + (pl.ds(lo, n),)
            c = remote(self.own.at[p.zx(j), pl.ds(lo, n)], self.G.at[at], self.snd.at[k, sem], self.rcv.at[k, sem], dev)
            c.start()
            self.sent.append(c)

    def pzx(self, k):
        p, Z = self.p, self.p.Z
        for j in range(1, Z):
            self._copy(k, j - 1, self.at(j), p.zpeer(j)).wait_recv()
            self._send(k, Z - 1 + j, self.at(j), p.xpeer())
        self.give(k, 0)

    def pzy(self, k):
        for j in range(1, self.p.Z):
            self._send(k, 2 * self.p.Z - 1 + j, self.at(j), self.p.ypeer())

    def px(self, k):
        p, Z = self.p, self.p.Z
        a, b = self.parts(k)
        for j in range(Z):
            self._copy(k, Z - 1 + j, self.at(j, 0, 1), p.xpeer()).wait_recv()
            if a[1]:
                self._send(k, 3 * Z - 1 + j, self.at(j, 0, 1), p.ypeer(), a)
            self._copy(k, 2 * Z - 1 + j, self.at(j, 1, 0), p.ypeer()).wait_recv()
            if b[1]:
                self._send(k, 4 * Z - 1 + j, self.at(j, 1, 0), p.xpeer(), b)
        self.give(k, 1)
        self.give(k, 2)

    def pd(self, k):
        p, Z = self.p, self.p.Z
        a, b = self.parts(k)
        for j in range(Z):
            if a[1]:
                self._copy(k, 3 * Z - 1 + j, self.at(j, 1, 1), p.ypeer(), a).wait_recv()
            if b[1]:
                self._copy(k, 4 * Z - 1 + j, self.at(j, 1, 1), p.xpeer(), b).wait_recv()
        self.give(k, 3)

    def fin(self, k):
        for t in range(4):
            self.column(k, t, True).wait_recv()

    def drain(self):
        for c in self.sent:
            c.wait_send()
        self.sent = []


def play(steps, table):
    for step in steps:
        name = step.rstrip("0123456789")
        table[name](int(step[len(name):]))


class Scatter:
    def __init__(self, place, sib, own, R0, R1, R2, R3, snd, rcv, chunks):
        self.p, self.sib, self.own, self.R0, self.R1, self.R2, self.R3 = place, sib, own, R0, R1, R2, R3
        self.snd, self.rcv, self.chunks = snd, rcv, chunks
        self.sent = []

    @staticmethod
    def sems(Z):
        return 6 * Z - 1

    @staticmethod
    def buffers(Z, R, W):
        return [pltpu.VMEM((2 * Z, 2, R, W), BF16), pltpu.VMEM((Z, 2, R, W), BF16), pltpu.VMEM((Z, R, W), BF16), pltpu.VMEM((Z - 1, R, W), BF16)]

    def rows(self, k):
        return pl.ds(*self.chunks[k][:2])

    def parts(self, k):
        r0, n, h = self.chunks[k]
        return pl.ds(r0, h) if h else None, pl.ds(r0 + h, n - h) if h < n else None

    def _go(self, src, dst, k, sem, dev, start):
        c = remote(src, dst, self.snd.at[k, sem], self.rcv.at[k, sem], dev)
        if start:
            c.start()
            self.sent.append(c)
        else:
            c.wait_recv()

    def order(self):
        return list(range(self.p.Z - 1, -1, -1))

    def _c0(self, k, j, start):
        zy = pl.ds(2 * self.p.zx(j), 2)
        self._go(self.sib(k, zy), self.R0.at[zy, :, self.rows(k)], k, j, self.p.sibling(), start)

    def _c1(self, k, j, start):
        p = self.p
        z = p.zx(j)
        a, b = self.parts(k)
        if a is not None:
            self._go(self.R0.at[pl.ds(2 * z, 2), 1 - p.x, a], self.R1.at[z, :, a], k, p.Z + j, p.xpeer(), start)
        if b is not None:
            self._go(self.R0.at[2 * z + 1 - p.y, :, b], self.R1.at[z, :, b], k, 2 * p.Z + j, p.ypeer(), start)

    def _c2(self, k, j, start):
        p = self.p
        z = p.zx(j)
        a, b = self.parts(k)
        if a is not None:
            self._go(self.R1.at[z, 1 - p.y, a], self.R2.at[z, a], k, 3 * p.Z + j, p.ypeer(), start)
        if b is not None:
            self._go(self.R1.at[z, 1 - p.x, b], self.R2.at[z, b], k, 4 * p.Z + j, p.xpeer(), start)

    def _c3(self, k, j, start):
        r = self.rows(k)
        self._go(self.R2.at[self.p.zx(j), r], self.R3.at[j - 1, r], k, 5 * self.p.Z + j - 1, self.p.zpeer(j), start)

    def begin(self, k):
        for j in self.order():
            self._c0(k, j, True)

    @staticmethod
    def _add(dst, src):
        dst[...] = (dst[...].astype(F32) + src[...].astype(F32)).astype(BF16)

    def core(self, k, js=None):
        p = self.p
        for j in js or self.order():
            self._c0(k, j, False)
            z = p.zx(j)
            for y in range(2):
                for x in range(2):
                    self._add(self.R0.at[2 * z + y, x, self.rows(k)], self.own(k, 2 * z + y, x))
            self._c1(k, j, True)

    def one(self, k, js=None):
        p = self.p
        a, b = self.parts(k)
        for j in js or self.order():
            self._c1(k, j, False)
            z = p.zx(j)
            for i in range(2):
                if a is not None:
                    self._add(self.R1.at[z, i, a], self.R0.at[2 * z + i, p.x, a])
                if b is not None:
                    self._add(self.R1.at[z, i, b], self.R0.at[2 * z + p.y, i, b])
            self._c2(k, j, True)

    def two(self, k, js=None):
        p = self.p
        a, b = self.parts(k)
        for j in js or self.order():
            self._c2(k, j, False)
            z = p.zx(j)
            if a is not None:
                self._add(self.R2.at[z, a], self.R1.at[z, p.y, a])
            if b is not None:
                self._add(self.R2.at[z, b], self.R1.at[z, p.x, b])
            if j:
                self._c3(k, j, True)

    def finish(self, k):
        p, r = self.p, self.rows(k)
        total = self.R2[p.z, r].astype(F32)
        for j in range(1, p.Z):
            self._c3(k, j, False)
            total = total + self.R3[j - 1, r].astype(F32)
        return total

    def drain(self):
        for c in self.sent:
            c.wait_send()
        self.sent = []


class SumAll:
    def __init__(self, place, cur, got, snd, rcv):
        self.p, self.cur, self.got, self.snd, self.rcv = place, cur, got, snd, rcv
        p = place
        self.peers = [p.sibling(), p.xpeer(), p.ypeer()]
        d = 1
        while d < p.Z:
            self.peers.append(p.zpeer(d))
            d *= 2

    @staticmethod
    def steps(Z):
        return 3 + (Z - 1).bit_length()

    def _copy(self, i):
        return remote(self.cur.at[i], self.got.at[i], self.snd.at[i], self.rcv.at[i], self.peers[i])

    def start(self, i):
        self._copy(i).start()

    def step(self, i):
        self._copy(i).wait()
        self.cur[i + 1] = self.cur[i] + self.got[i]


def dma(*shape):
    return pltpu.SemaphoreType.DMA(shape)


def vmem(*n):
    return [pl.BlockSpec(memory_space=pltpu.VMEM)] * (n[0] if n else 1)


def doc_numbers(len_ref, pos):
    ends, count = jnp.int32(0), jnp.zeros(pos.shape, jnp.int32)
    for i in range(len_ref.shape[1]):
        ends = ends + len_ref[0, i]
        count = count + jnp.where(pos >= ends, 1, 0)
    return jnp.where(pos < 0, -1, count)


def fill_band(mask_s, len_ref, pk, start, half):
    S, span = mask_s.shape
    KS = pk.shape[1]
    dk = doc_numbers(len_ref, start - half + lax.broadcasted_iota(jnp.int32, (1, KS), 1))
    for a in range(S // SB):
        dq = doc_numbers(len_ref, start + a * SB + lax.broadcasted_iota(jnp.int32, (SB, 1), 0))
        r = lax.broadcasted_iota(jnp.int32, (SB, span), 0)
        c = lax.broadcasted_iota(jnp.int32, (SB, span), 1)
        ok = (dq == dk[:, a * SB:a * SB + span]) & ((pk[:, a * SB:a * SB + span] == 1) | (c == r + half))
        mask_s[a * SB:(a + 1) * SB, :] = jnp.where(ok, 1.0, 0.0)


def fill_features(dm_s, draws_ref):
    m, d = draws_ref.shape[1:]
    z = jnp.zeros((m, d), F32)
    for i in range(draws_ref.shape[0] // 2):
        full = jnp.concatenate([jnp.concatenate([draws_ref[2 * i], z], 1), jnp.concatenate([z, draws_ref[2 * i + 1]], 1)], 0)
        dm_s[0, i], dm_s[1, i] = split2(full)


def ones_per_head():
    lane = lax.broadcasted_iota(jnp.int32, (256, 128), 1) // 64
    row = lax.rem(lax.broadcasted_iota(jnp.int32, (256, 128), 0) // 64, 2)
    return jnp.where(lane == row, 1.0, 0.0).astype(BF16)


def split2(x):
    hi = x.astype(BF16)
    return hi, (x - hi.astype(F32)).astype(BF16)


def coefs(bias_ref, i, t_s, span):
    for h in range(2):
        t_s[h * SB:(h + 1) * SB, :] = toep(jnp.exp(bias_ref[pl.ds(2 * i + h, 1), :]), span)


FORWARD = (
    "bx4", "by2", "bz0", "bz1", "pre0", "bx2", "by3", "by0", "bx0", "pzx0", "by1", "bx1", "bz2", "bz3", "pzy0", "by4", "pzx1",
    "pzy1", "pzx2", "bz5", "pzy2", "bz4", "bx5", "H0", "bx3", "px1", "px0", "px2", "pd0", "pzx5", "pd1", "fin0", "fin1", "po0",
    "pd2", "fin2", "pzx4", "po1", "pzx3", "po2", "dz0", "KV0", "pzy3", "pzy4", "hw0", "mask0", "by5", "px3", "kvw0", "rim0",
    "pzy5", "rim1", "px4", "rim2", "pr0", "px5", "pr1", "pd3", "pd4", "pr2", "pd5", "dw0", "fin3", "fin4", "uo0", "uu0", "fin5",
    "uu1",
)
CUT_FORWARD = (0, 0, 0, 0, 0, 0)


def phi(z, dh, dl, on, scale):
    s = z * scale
    sh, sl = split2(s)
    rows = dot(jnp.concatenate([sh, sl], 1), jnp.concatenate([dh, dh], 1), NT) + dot(sh, dl, NT)
    half = dot(jnp.concatenate(split2(s * s * 0.5), 1), on)
    return jnp.exp(rows - half) * (dh.shape[0] // 2) ** -0.5


def fwd_attend(S, span, i, bias_ref, q_s, k_s, v_s, mask_s, t_s, w_s, vv_s, att_ref, inv_ref):
    lanes = pl.ds(pl.multiple_of(i * 128, 128), 128)
    CH = span
    coefs(bias_ref, i, t_s, span)
    vv_s[:, :128] = v_s[:, lanes]
    for a in range(S // SB):
        rs = slice(a * SB, (a + 1) * SB)
        qq = jnp.concatenate(halves(q_s[S + a * SB:S + (a + 1) * SB, lanes]), 0)
        for c in range(0, span, CH):
            s = dot(qq, k_s[a * SB + c:a * SB + c + CH, lanes], NT)
            m = mask_s[rs, c:c + CH]
            for h in range(2):
                hs = slice(h * SB, (h + 1) * SB)
                w_s[a % 2, hs, c:c + CH] = (s[hs] * (t_s[hs, c:c + CH] * m)).astype(BF16)
        o = dot(w_s[a % 2], vv_s[a * SB:a * SB + span, :])
        inv = 1.0 / pick(o[:SB, 128:], o[SB:, 128:])
        att_ref[rs, lanes] = pick(o[:SB, :128], o[SB:, :128]) * inv
        inv_ref[rs, lanes] = inv


def forward_kernel(n_seq, chunks, scale, wq_ref, wo_ref, wu_ref, wd_ref, vq_ref, vu_ref, v1_ref, v2_ref, v3_ref, v4_ref, v5_ref, v6_ref, x_ref, pad_ref, bias_ref, draws_ref, len_ref,
                   qkv_h, out_h, up_h, zq_h, zk_h, q_h, k_h, v_h, att_h, inv_h, vec_ref, pk_ref, col_ref,
                   qkv_ref, out_ref, up_ref, zq_ref, zk_ref, q_ref, k_ref, v_ref, att_ref, inv_ref,
                   own_s, G, XR, P3, pad_s, mask_s, t_s, w_s, vv_s, dm_s, snd, rcv, hsnd, hrcv, dsnd, drcv, osem, vb_s):
    S, W = x_ref.shape
    f = wo_ref.shape[0]
    win = bias_ref.shape[1]
    span = win + SB
    wide = 256
    p = Place(n_seq)
    g = Gather(p, own_s, G, snd, rcv, chunks)

    def placed(v, n):
        return pltpu.roll(jnp.broadcast_to(v, (8, v.shape[1])), p.me * n, 1)[:1]

    def thirds(v, j):
        return jnp.concatenate([v[:, t * W + j * wide:t * W + (j + 1) * wide] for t in range(3)], 1)

    wq = wq_ref[...].astype(F32)
    vb_s[...] = jnp.zeros_like(vb_s)
    for i, r in enumerate((vq_ref, vu_ref, v1_ref, v2_ref, v3_ref, v4_ref, v5_ref, v6_ref)):
        vb_s[i:i + 1, :r.shape[1]] = r[...].astype(F32)
    b3 = placed(vb_s[0:1, :3 * W], 3 * f)
    b4 = placed(vb_s[1:2, :], 4 * f)
    singles = pltpu.roll(vb_s[:, :W], p.me * f, 1)[2:8]
    rest = [[b4[:, j * W:(j + 1) * W] for j in range(4)] + [singles[0:3]], [singles[3:6], jnp.zeros((4, W), F32)], [jnp.zeros((7, W), F32)]]
    for j in range(3):
        own_s[j * SLAB:(j + 1) * SLAB, :] = jnp.concatenate([thirds(wq, j), thirds(b3, j)] + rest[j], 0).astype(BF16)
    wide_up = [wu_ref[:, j * W:(j + 1) * W].astype(F32) for j in range(4)]
    own_s[3 * SLAB:4 * SLAB, :] = jnp.concatenate([wo_ref[...].astype(F32), jnp.zeros((SLAB - f, W), F32)], 0).astype(BF16)
    own_s[4 * SLAB:, :] = jnp.concatenate(wide_up, 0).astype(BF16)
    pad_s[...] = jnp.broadcast_to(pad_ref[...], pad_s.shape)
    p.greet(True)
    partner, has = p.partner()
    mine, theirs = 2 * p.c, 2 - 2 * p.c
    leaving = []

    def leave(src, dst):
        c = pltpu.make_async_copy(src, dst, osem.at[len(leaving)])
        c.start()
        leaving.append(c)

    halo = (remote(x_ref, XR, hsnd.at[0], hrcv.at[0], partner), remote(pad_s, P3.at[theirs], hsnd.at[1], hrcv.at[1], partner))
    halo_in = remote(pad_s, P3.at[mine], hsnd.at[1], hrcv.at[1], partner)
    pads = remote(pad_s, P3.at[mine], hsnd.at[2], hrcv.at[2], p.sibling())
    pads_in = remote(pad_s, P3.at[theirs], hsnd.at[2], hrcv.at[2], p.sibling())
    own_rows, far, near = pl.ds(S, S), pl.ds(pl.multiple_of(mine * S, S), S), pl.ds(pl.multiple_of(theirs * S, S), S)
    given = [remote(r.at[own_rows], r.at[far], hsnd.at[3 + i], hrcv.at[3 + i], p.sibling()) for i, r in enumerate((k_ref, v_ref, q_ref))]
    taken = [remote(r.at[own_rows], r.at[near], hsnd.at[3 + i], hrcv.at[3 + i], p.sibling()) for i, r in enumerate((k_ref, v_ref, q_ref))]
    pads.start()

    def send_halo(_):
        @pl.when(has)
        def _():
            for h in halo:
                h.start()

    def take_halo(_):
        @pl.when(has)
        def _():
            halo[0].wait_recv()
            halo_in.wait_recv()

        @pl.when(jnp.logical_not(has))
        def _():
            XR[...] = jnp.zeros_like(XR)
            P3[mine] = jnp.zeros(pad_s.shape, jnp.int32)

    G[p.z, p.y, p.c, p.x] = own_s[...]
    P3[1] = pad_s[...]

    def down(j):
        return remote(wd_ref, col_ref.at[p.z], dsnd.at[j - 1], drcv.at[j - 1], p.zpeer(j))

    def down_in(j):
        return remote(wd_ref, col_ref.at[p.zx(j)], dsnd.at[j - 1], drcv.at[j - 1], p.zpeer(j))

    def send_down(_):
        for j in range(1, p.Z):
            down(j).start()

    def take_down(_):
        for j in range(1, p.Z):
            down_in(j).wait_recv()

    col_ref[p.z] = wd_ref[...]

    def early(_):
        fill_features(dm_s, draws_ref)
        vv_s[:, 128:] = jnp.ones((vv_s.shape[0], 128), BF16)

    on = ones_per_head()

    def features(z, i):
        return phi(z, dm_s[0, i], dm_s[1, i], on, scale).astype(BF16)

    def project(j):
        cs = slice(j * wide, (j + 1) * wide)
        unpack_qkv(g, j, qkv_ref, vec_ref)
        bias = vec_ref[8 * j:8 * j + 1, :]
        x = x_ref[...]
        zq = dot(x, qkv_ref[j, :, :wide]) + bias[:, :wide]
        zk = dot(x, qkv_ref[j, :, wide:2 * wide]) + bias[:, wide:2 * wide]
        zq_ref[:, cs] = zq
        zk_ref[:, cs] = zk
        for i in range(wide // 128):
            pp, at = wide // 128 * j + i, slice(i * 128, (i + 1) * 128)
            lanes = slice(pp * 128, (pp + 1) * 128)
            q_ref[S:2 * S, lanes] = features(zq[:, at], pp)
            k_ref[S:2 * S, lanes] = features(zk[:, at], pp)
        v_ref[S:2 * S, cs] = (dot(x, qkv_ref[j, :, 2 * wide:]) + bias[:, 2 * wide:]).astype(BF16)
        leave(qkv_ref.at[j], qkv_h.at[j])
        for a, b in ((zq_ref, zq_h), (zk_ref, zk_h)):
            leave(a.at[:, cs], b.at[:, cs])

    def give(_):
        for c in given:
            c.start()

    def band(_):
        pads_in.wait_recv()
        pk_ref[...] = jnp.concatenate([P3[0, :1], P3[1, :1], P3[2, :1]], 1)
        fill_band(mask_s, len_ref, pk_ref[...], p.s * S, win // 2)

    def rim(j):
        cs = slice(j * wide, (j + 1) * wide)
        bias = vec_ref[8 * j:8 * j + 1, :]
        x = XR[...]
        zq = dot(x, qkv_ref[j, :, :wide]) + bias[:, :wide]
        zk = dot(x, qkv_ref[j, :, wide:2 * wide]) + bias[:, wide:2 * wide]
        for i in range(wide // 128):
            pp = wide // 128 * j + i
            q_ref[far, pp * 128:(pp + 1) * 128] = features(zq[:, i * 128:(i + 1) * 128], pp)
            k_ref[far, pp * 128:(pp + 1) * 128] = features(zk[:, i * 128:(i + 1) * 128], pp)
        v_ref[far, cs] = (dot(x, qkv_ref[j, :, 2 * wide:]) + bias[:, 2 * wide:]).astype(BF16)
        if j == 2:
            for a, b in ((q_ref, q_h), (k_ref, k_h), (v_ref, v_h)):
                leave(a, b)

    def take(_):
        for c in taken:
            c.wait_recv()

    def pairs(j):
        def pair(i, _):
            fwd_attend(S, span, i, bias_ref, q_ref, k_ref, v_ref, mask_s, t_s, w_s, vv_s, att_ref, inv_ref)
            return 0

        lax.fori_loop(2 * j, 2 * j + 2, pair, 0)
        cs = slice(j * wide, (j + 1) * wide)
        for a, b in ((att_ref, att_h), (inv_ref, inv_h)):
            leave(a.at[:, cs], b.at[:, cs])

    def unpack_up(i):
        k = 4 + i
        lo, n, _ = chunks[k]
        first = (lo - 4 * SLAB) // f

        def put(at, j, v):
            up_ref[at, (first + j) * W:(first + j + 1) * W] = v

        shard_pairs(G, lo, n, f, put)
        cs = slice(first * W, first * W + n // f * W)
        leave(up_ref.at[:, cs], up_h.at[:, cs])

    def unpack_out(_):
        def put(at, j, v):
            out_ref[at, :] = v

        shard_pairs(G, 3 * SLAB, f, f, put)
        leave(out_ref, out_h)

    play(FORWARD, dict(
        bx=g.bx, by=g.by, bz=g.bz, pzx=g.pzx, pzy=g.pzy, px=g.px, pd=g.pd, fin=g.fin, H=send_halo, hw=take_halo, pre=early, po=project,
        KV=give, kvw=take, mask=band, rim=rim, pr=pairs, uo=unpack_out, uu=unpack_up, dz=send_down, dw=take_down))

    @pl.when(has)
    def _():
        for h in halo:
            h.wait_send()
    for c in given + [pads] + [down(j) for j in range(1, p.Z)]:
        c.wait_send()
    g.drain()
    for c in leaving:
        c.wait()


def shard_pairs(G, lo, n, f, put):
    def one(s, _):
        full = pl.ds(lo, (n + 15) // 16 * 16)
        at = (s // 4, lax.rem(s // 2, 2), lax.rem(s, 2))
        a, b = (G[at + (x, full)].astype(F32) for x in range(2))
        rows = pl.ds(pl.multiple_of(s * 2 * f, 2 * f), 2 * f)
        for j in range(n // f):
            put(rows, j, jnp.concatenate([a[j * f:(j + 1) * f], b[j * f:(j + 1) * f]], 0).astype(BF16))
        return 0

    lax.fori_loop(0, 4 * G.shape[0], one, 0)


def unpack_qkv(g, j, qkv_ref, vec_ref):
    G = g.G
    f = qkv_ref.shape[1] // (8 * G.shape[0])
    lo = j * SLAB

    def one(s, t):
        at = (s // 4, lax.rem(s // 2, 2), lax.rem(s, 2))
        a, b = (G[at + (x, pl.ds(lo, SLAB))].astype(F32) for x in range(2))
        qkv_ref[j, pl.ds(pl.multiple_of(s * 2 * f, 2 * f), 2 * f), :] = jnp.concatenate([a[:f], b[:f]], 0).astype(BF16)
        return t + a[f:] + b[f:]

    vec_ref[8 * j:8 * j + 8, :] = lax.fori_loop(0, 4 * G.shape[0], one, jnp.zeros((SLAB - f, G.shape[-1]), F32))


def forward(n_seq, wq, wo, wu, wd, vectors, x, pad, bias, draws, lens):
    S, W = x.shape
    f = wo.shape[0]
    win = bias.shape[1]
    span = win + SB
    KS = S + win
    Z = n_seq // 4
    R = 4 * SLAB + 4 * f
    chunks = tuple((SLAB * k, SLAB, CUT_FORWARD[k]) for k in range(4)) + tuple((4 * SLAB + 2 * f * k, 2 * f, CUT_FORWARD[4 + k]) for k in range(2))
    V = pltpu.VMEM
    M = Gather.sems(Z)
    D = f * 2 * n_seq
    sd = jax.ShapeDtypeStruct
    heads, feats, dims = draws.shape
    K = len(chunks)
    large = (sd((3, D, W), BF16), sd((D, W), BF16), sd((D, 4 * W), BF16), sd((S, W), F32), sd((S, W), F32),
             sd((KS, W), BF16), sd((KS, W), BF16), sd((KS, W), BF16), sd((S, W), F32), sd((S, W), F32))
    return pl.pallas_call(
        functools.partial(forward_kernel, n_seq, chunks, dims ** -0.25),
        out_shape=large + (sd((24, W), F32), sd((1, KS), jnp.int32), sd((Z, 4 * f, W), BF16)),
        in_specs=vmem(16) + [pl.BlockSpec(memory_space=pltpu.SMEM)], out_specs=(pl.BlockSpec(memory_space=pl.ANY),) * len(large) + tuple(vmem(3)),
        scratch_shapes=[V(s.shape, s.dtype) for s in large] + [
            V((R, W), BF16), V((Z, 2, 2, 2, R, W), BF16), V((S, W), BF16), V((3, 8, S), jnp.int32), V((8, S), jnp.int32),
            V((S, span), F32), V((2 * SB, span), F32), V((2, 2 * SB, span), BF16), V((KS, 256), BF16),
            V((2, heads // 2, 2 * feats, 2 * dims), BF16), dma(K, M), dma(K, M), dma(6), dma(6), dma(Z - 1), dma(Z - 1), dma(24), V((8, 4 * W), F32)],
        compiler_params=pltpu.CompilerParams(collective_id=1, has_side_effects=True, vmem_limit_bytes=60 << 20),
        name="forward",
    )(wq, wo, wu, wd, *vectors, x, pad, bias, draws, lens)


DOWN_PARTS = 3
CUT_DOWN = 16


def lane_mean(v):
    return jnp.mean(v, 1, keepdims=True)


def rows_loop(total, step, body):
    def one(i, c):
        body(pl.ds(pl.multiple_of(i * step, step), step))
        return c

    lax.fori_loop(0, total // step, one, 0)


def fold8(v):
    return jnp.sum(v.reshape(v.shape[0] // 8, 8, v.shape[1]), 0)


def normal_cdf_pdf(x):
    u = jnp.abs(x) * 0.7071067811865476
    t = 1.0 / (1.0 + 0.3275911 * u)
    e = jnp.exp(-0.5 * x * x)
    poly = t * (0.254829592 + t * (-0.284496736 + t * (1.421413741 + t * (-1.453152027 + t * 1.061405429))))
    tail = 0.5 * poly * e
    return jnp.where(x >= 0, 1.0 - tail, tail), e * 0.3989422804014327


def middle_kernel(n_seq, heads, col_ref, x_ref, vec_ref, ct_h, att_h, inv_h, ow_h, up_h, out_ref, g1_ref, gw_ref, gt_ref, vg_ref, P_h,
                  ct_ref, att_ref, inv_ref, ow_ref, up_ref, P_ref,
                  al_s, hl_s, hlt_s, h1_s, n1_s, i1_s, act_s, dg_s, gi_s, r_s, gl_s, acc_s, G, snd, rcv, lsem, osem):
    S, W = x_ref.shape
    FF_ = up_ref.shape[1]
    n_dev = P_ref.shape[0]
    f = W // n_dev
    RB = 256
    p = Place(n_seq)
    loads = [pltpu.make_async_copy(a, b, lsem.at[i]) for i, (a, b) in enumerate(
        ((att_h, att_ref), (ow_h, ow_ref), (up_h, up_ref), (ct_h, ct_ref), (inv_h, inv_ref)))]
    for c in loads:
        c.start()
    part = 4 * f // DOWN_PARTS
    g = Gather(p, col_ref, G, snd, rcv, tuple((part * k, part, CUT_DOWN) for k in range(DOWN_PARTS)))
    p.greet(False)
    G[:, p.y, p.c, p.x] = col_ref[...]
    for k in range(DOWN_PARTS):
        for j in range(p.Z):
            g.direct(k, j)
    for k in range(DOWN_PARTS):
        g.give(k, 0)
    b_out, gain_a, shift_a, b_down, gain_f, shift_f = (vec_ref[i:i + 1] for i in (5, 6, 7, 9, 10, 11))
    acc_s[...] = jnp.zeros_like(acc_s)

    def cast(rs):
        al_s[rs, :] = att_ref[rs, :].astype(BF16)

    loads[0].wait()
    rows_loop(S, RB, cast)
    loads[1].wait()
    r_s[...] = dot(al_s[...], ow_ref[...])

    def norm_one(rs):
        r = r_s[rs, :] + (x_ref[rs, :].astype(F32) + b_out)
        c = r - lane_mean(r)
        inv = lax.rsqrt(lane_mean(c * c) + EPS)
        n = c * inv
        n1_s[rs, :] = n
        i1_s[rs, :] = jnp.broadcast_to(inv, (RB, 128))
        h = n * gain_a + shift_a
        h1_s[rs, :] = h
        hl_s[rs, :] = h.astype(BF16)

    rows_loop(S, RB, norm_one)
    loads[2].wait()
    hlt_s[...] = hl_s[...].T
    CW = W // 2
    between = {1: ((g.px, 0),), 2: ((g.px, 1),), 3: ((g.px, 2),), 5: ((g.pd, 0),), 6: ((g.pd, 1),), 7: ((g.pd, 2),)}
    for j in range(FF_ // CW):
        cs = slice(j * CW, (j + 1) * CW)
        inner = dot(hl_s[...], up_ref[:, cs]) + vec_ref[1 + j // 2:2 + j // 2, j % 2 * CW:(j % 2 + 1) * CW]
        cdf, pdf = normal_cdf_pdf(inner)
        act_s[:, cs] = (inner * cdf).astype(BF16)
        dg_s[:, cs] = cdf + inner * pdf
        for step, k in between.get(j, ()):
            step(k)
    for k in range(DOWN_PARTS):
        g.fin(k)
    r_s[...] = dot(act_s[...], G[...].reshape(FF_, W))

    def norm_two(rs):
        r = r_s[rs, :] + (h1_s[rs, :] + b_down)
        c = r - lane_mean(r)
        inv = lax.rsqrt(lane_mean(c * c) + EPS)
        n = c * inv
        out_ref[rs, :] = (n * gain_f + shift_f).astype(BF16)
        ct = ct_ref[rs, :].astype(F32)
        acc_s[0] += fold8(ct * n)
        acc_s[1] += fold8(ct)
        gy = ct * gain_f
        gr = inv * (gy - lane_mean(gy) - n * lane_mean(gy * n))
        r_s[rs, :] = gr
        gl = gr.astype(BF16)
        gl_s[rs, :] = gl
        acc_s[2] += fold8(gl.astype(F32))

    loads[3].wait()
    rows_loop(S, RB, norm_two)
    block = FF_ // p.Z

    def leave(i, lo, n):
        rows = pl.ds(lo, n)
        c = pltpu.make_async_copy(P_ref.at[:, rows], P_h.at[:, rows], osem.at[i])
        c.start()
        leaving.append(c)

    leaving = []
    per = n_dev // p.Z
    for j in range(p.Z):
        gd = dot(act_s[:, j * block:(j + 1) * block], gl_s[...], TN)
        P_ref[j * per:(j + 1) * per, :4 * f, :] = gd.reshape(per, 4 * f, W).astype(BF16)
    leave(0, 0, 4 * f)
    vg_ref[...] = jnp.zeros_like(vg_ref)
    for j in range(p.Z):
        cs = slice(j * block, (j + 1) * block)
        gi = (dot(gl_s[...], G[j].reshape(block, W), NT) * dg_s[:, cs]).astype(BF16)
        gi_s[:, cs] = gi
    for j in range(FF_ // W):
        vg_ref[1 + j:2 + j, :] = jnp.sum(gi_s[:, j * W:(j + 1) * W].astype(F32), 0, keepdims=True)
    for i in range(2):
        parts = [dot(hlt_s[...], gi_s[:, k * W:(k + 1) * W]).reshape(n_dev, f, W) for k in (2 * i, 2 * i + 1)]
        P_ref[:, 4 * f + 2 * f * i:4 * f + 2 * f * (i + 1), :] = jnp.concatenate(parts, 1).astype(BF16)
        leave(1 + i, 4 * f + 2 * f * i, 2 * f)
    r_s[...] += dot(gi_s[...], up_ref[...], NT)

    def back_one(rs):
        gr = r_s[rs, :]
        n = n1_s[rs, :]
        acc_s[3] += fold8(gr * n)
        acc_s[4] += fold8(gr)
        gy = gr * gain_a
        inv = i1_s[rs, :1]
        go = inv * (gy - lane_mean(gy) - n * lane_mean(gy * n))
        g1_ref[rs, :] = go
        gl = go.astype(BF16)
        gl_s[rs, :] = gl
        acc_s[5] += fold8(gl.astype(F32))

    rows_loop(S, RB, back_one)
    for row, i in ((10, 0), (11, 1), (9, 2), (6, 3), (7, 4), (5, 5)):
        vg_ref[row:row + 1, :] = jnp.sum(acc_s[i], 0, keepdims=True)
    go = dot(al_s[...], gl_s[...], TN).reshape(n_dev, f, W)
    P_ref[:, 8 * f:, :] = jnp.concatenate([go, jnp.zeros((n_dev, SLAB - f, W), F32)], 1).astype(BF16)
    leave(3, 8 * f, SLAB)
    r_s[...] = dot(gl_s[...], ow_ref[...], NT)
    of_head = lax.broadcasted_iota(jnp.int32, (W, 128), 0) // (W // heads) == lax.broadcasted_iota(jnp.int32, (W, 128), 1)
    of_head = jnp.where(of_head, 1.0, 0.0).astype(BF16)

    def weighted(rs):
        g = r_s[rs, :] * inv_ref[rs, :]
        gw_ref[rs, :] = g.astype(BF16)
        hi, lo = split2(g * att_ref[rs, :])
        total = -(dot(hi, of_head) + dot(lo, of_head))
        hi = total.astype(BF16).astype(F32)
        gt_ref[rs, :] = (hi + pltpu.roll(total - hi, heads, 1)).astype(BF16)

    loads[4].wait()
    rows_loop(S, RB, weighted)
    g.drain()
    for c in leaving:
        c.wait()


def middle(n_seq, heads, col, x, ct, att, inv, ow, up, vec):
    S, W = x.shape
    FF_ = up.shape[1]
    n_dev = 2 * n_seq
    f = W // n_dev
    Z = n_seq // 4
    V = pltpu.VMEM
    sd = jax.ShapeDtypeStruct
    return pl.pallas_call(
        functools.partial(middle_kernel, n_seq, heads),
        out_shape=(sd((S, W), BF16), sd((S, W), F32), sd((S, W), BF16), sd((S, 128), BF16), sd((24, W), F32), sd((n_dev, 8 * f + SLAB, W), BF16)),
        in_specs=vmem(3) + [pl.BlockSpec(memory_space=pl.ANY)] * 5, out_specs=tuple(vmem(5)) + (pl.BlockSpec(memory_space=pl.ANY),),
        scratch_shapes=[V((S, W), BF16), V((S, W), F32), V((S, W), F32), V((W, W), BF16), V((W, FF_), BF16), V((n_dev, 8 * f + SLAB, W), BF16),
                        V((S, W), BF16), V((S, W), BF16), V((W, S), BF16), V((S, W), F32), V((S, W), F32), V((S, 128), F32),
                        V((S, FF_), BF16), V((S, FF_), F32), V((S, FF_), BF16), V((S, W), F32), V((S, W), BF16), V((6, 8, W), F32),
                        V((Z, 2, 2, 2, 4 * f, W), BF16), dma(DOWN_PARTS, Gather.sems(Z)), dma(DOWN_PARTS, Gather.sems(Z)), dma(5), dma(4)],
        compiler_params=pltpu.CompilerParams(collective_id=2, has_side_effects=True, vmem_limit_bytes=60 << 20),
        name="middle",
    )(col, x, vec, ct, att, inv, ow, up)


BACKWARD = (
    "b0", "b1", "H0", "pre0", "c0", "pr0", "c1", "b2", "pr1", "o0", "c2", "pr2", "b4", "hw0", "o1", "b3", "ri0", "v0", "c3",
    "t0", "o2", "pj0", "c4", "b5", "v1", "t1", "ri1", "o3", "t2", "pj1", "c5", "b6", "o4", "t3", "ri2", "o5", "t4", "c6", "pj2",
    "b7", "t5", "v2", "o6", "v3", "c7", "t6", "f2", "v4", "f1", "o7", "f5", "t7", "f3", "f0", "gx0", "f4", "f6", "v5", "f7",
)
CUT_BACKWARD = (48, 32, 32, 32, 16, 16, 16, 16)


def head_rows(gw, gt, i, heads):
    lane = lax.broadcasted_iota(jnp.int32, gt.shape, 1)
    rows = []
    for h, g in enumerate(halves(gw)):
        mine = jnp.logical_or(lane == 2 * i + h, lane == 2 * i + h + heads)
        rows.append(jnp.concatenate([g, jnp.where(mine, gt, jnp.zeros_like(gt))], 1))
    return jnp.concatenate(rows, 0)


def back_own(S, span, win, heads, i, bias_ref, q_ref, k_ref, v_ref, gw_s, gt_s, mask_s, t_s, w_s, gs_s, p_s, vv_s, gkt_s, gvt_s, gq_s, bsum):
    lanes = pl.ds(pl.multiple_of(i * 128, 128), 128)
    CH = span // 3
    half = win // 2
    coefs(bias_ref, i, t_s, span)
    vv_s[:, :128] = v_ref[:, lanes]
    for a in range(S // SB):
        rs, qs = slice(a * SB, (a + 1) * SB), slice(S + a * SB, S + (a + 1) * SB)
        qq = jnp.concatenate(halves(q_ref[qs, lanes]), 0)
        gg = head_rows(gw_s[qs, lanes], gt_s[qs, :], i, heads)
        for c in range(0, span, CH):
            s = dot(qq, k_ref[a * SB + c:a * SB + c + CH, lanes], NT)
            g = dot(gg, vv_s[a * SB + c:a * SB + c + CH, :], NT)
            m = mask_s[rs, c:c + CH]
            for h in range(2):
                hs = slice(h * SB, (h + 1) * SB)
                cm = t_s[hs, c:c + CH] * m
                w = s[hs] * cm
                w_s[hs, c:c + CH] = w.astype(BF16)
                gs_s[hs, c:c + CH] = (g[hs] * cm).astype(BF16)
                pw = g[hs] * w
                if a == 0:
                    p_s[hs, c:c + CH] = pw
                else:
                    p_s[hs, c:c + CH] += pw
        gq = dot(gs_s[...], k_ref[a * SB:a * SB + span, lanes])
        gq_s[rs, lanes] = pick(gq[:SB], gq[SB:])
        cols = slice(half - a * SB, half - a * SB + S)
        gk, gv = dot(qq, gs_s[:, cols], TN), dot(gg[:, :128], w_s[:, cols], TN)
        if a == 0:
            gkt_s[i], gvt_s[i] = gk, gv
        else:
            gkt_s[i] += gk
            gvt_s[i] += gv
    for h in range(2):
        bsum[pl.ds(2 * i + h, 1), :] = unskew(p_s[h * SB:(h + 1) * SB, :], win)


def back_rim(S, span, heads, i, bias_ref, q_ref, k_ref, v_ref, gw_s, gt_s, maskr_s, t_s, w_s, gs_s, vv_s, gkt_s, gvt_s):
    lanes = pl.ds(pl.multiple_of(i * 128, 128), 128)
    coefs(bias_ref, i, t_s, span)
    vv_s[S:2 * S, :128] = v_ref[S:2 * S, lanes]
    for a in range(S // SB):
        for side, (k0, k1, t0) in enumerate(((0, (a + 1) * SB, span - (a + 1) * SB), (a * SB, S, 0))):
            n = k1 - k0
            qs = slice(2 * S * side + a * SB, 2 * S * side + (a + 1) * SB)
            qq = jnp.concatenate(halves(q_ref[qs, lanes]), 0)
            gg = head_rows(gw_s[qs, lanes], gt_s[qs, :], i, heads)
            s = dot(qq, k_ref[S + k0:S + k1, lanes], NT)
            g = dot(gg, vv_s[S + k0:S + k1, :], NT)
            m = maskr_s[side, a * SB:(a + 1) * SB, k0:k1]
            for h in range(2):
                hs = slice(h * SB, (h + 1) * SB)
                cm = t_s[hs, t0:t0 + n] * m
                w_s[hs, :n] = (s[hs] * cm).astype(BF16)
                gs_s[hs, :n] = (g[hs] * cm).astype(BF16)
            gkt_s[i, :, k0:k1] += dot(qq, gs_s[:, :n], TN)
            gvt_s[i, :, k0:k1] += dot(gg[:, :128], w_s[:, :n], TN)


def phi_back(g, feat, z, dh, dl, on, scale):
    t = g * feat.astype(F32)
    th, tl = split2(t)
    back = dot(th, dh) + dot(tl, dh) + dot(th, dl)
    total = dot(jnp.concatenate([th, tl], 1), on)
    return scale * (back - (z * scale) * total)


def backward_kernel(n_seq, chunks, scale, x_ref, pk_ref, bias_ref, draws_ref, len_ref, vg_ref, gw_ref, gt_ref,
                    w_h, q_h, k_h, v_h, zq_h, zk_h, g1_h, P_h,
                    gx_ref, rel_ref, gqkv_ref, gup_ref, gdown_ref, gout_ref, small_ref,
                    w_ref, q_ref, k_ref, v_ref, zq_ref, zk_ref,
                    U, PQ, R0, R1, R2, R3, mask_s, maskr_s, t_s, w_s, gs_s, p_s, vv_s, gkt_s, gvt_s, gq_s, gw_s, gt_s, gp_s, xt_s, dm_s, ex_s,
                    cur, got, snd, rcv, hsnd, hrcv, vsnd, vrcv, lsem):
    S, W = x_ref.shape
    heads, win = bias_ref.shape
    span = win + SB
    n_pair = W // 128
    n_dev = 2 * n_seq
    f = W // n_dev
    wide = 256
    p = Place(n_seq)
    partner, has = p.partner()
    mine, theirs = 2 * p.c, 2 - 2 * p.c
    far, near = pl.ds(pl.multiple_of(mine * S, S), S), pl.ds(pl.multiple_of(theirs * S, S), S)

    def load(src, dst, i):
        return pltpu.make_async_copy(src, dst, lsem.at[i])

    def own_half(k):
        r0, n = chunks[k][:2]
        return load(P_h.at[:, p.c, :, pl.ds(r0, n)], U.at[k % 2, :, :, pl.ds(0, n)], 1 + k % 2)

    residual = load(g1_h, gx_ref, 0)
    early = [load(h, r, 3 + i) for i, (h, r) in enumerate(((q_h, q_ref), (k_h, k_ref), (v_h, v_ref)))]
    late = [load(h, r, 6 + i) for i, (h, r) in enumerate(((zq_h, zq_ref), (zk_h, zk_ref), (w_h, w_ref)))]
    own_half(0).start()
    for c in early:
        c.start()
    own_half(1).start()
    for c in late:
        c.start()
    residual.start()
    p.greet(True)
    sides = ((gw_ref, gw_s), (gt_ref, gt_s))
    out_far = [remote(a, b.at[near], hsnd.at[i], hrcv.at[i], partner) for i, (a, b) in enumerate(sides)]
    in_far = [remote(a, b.at[far], hsnd.at[i], hrcv.at[i], partner) for i, (a, b) in enumerate(sides)]
    out_near = [remote(a, b.at[far], hsnd.at[2 + i], hrcv.at[2 + i], p.sibling()) for i, (a, b) in enumerate(sides)]
    in_near = [remote(a, b.at[near], hsnd.at[2 + i], hrcv.at[2 + i], p.sibling()) for i, (a, b) in enumerate(sides)]

    def send_halo(_):
        for c in out_near:
            c.start()

        @pl.when(has)
        def _():
            for c in out_far:
                c.start()

    def take_halo(_):
        for c in in_near:
            c.wait_recv()

        @pl.when(has)
        def _():
            for c in in_far:
                c.wait_recv()

    def sib(k, zy):
        return P_h.at[zy, 1 - p.c, :, pl.ds(*chunks[k][:2])] if k < 5 else PQ.at[k - 5, zy, 1 - p.c]

    def own(k, zy, x):
        return U.at[k % 2, zy, x, pl.ds(0, chunks[k][1])] if k < 5 else PQ.at[k - 5, zy, p.c, x]

    sc = Scatter(p, sib, own, R0, R1, R2, R3, snd, rcv, chunks)
    on = ones_per_head()

    def prepare(_):
        start = p.s * S
        fill_band(mask_s, len_ref, pk_ref[...], start, win // 2)
        dk = doc_numbers(len_ref, start + lax.broadcasted_iota(jnp.int32, (1, S), 1))
        real = pk_ref[:, S:2 * S] == 1
        for side in range(2):
            dq = doc_numbers(len_ref, start + (2 * side - 1) * S + lax.broadcasted_iota(jnp.int32, (S, 1), 0))
            maskr_s[side] = jnp.where((dq == dk) & real, 1.0, 0.0)
        fill_features(dm_s, draws_ref)
        vv_s[:, 128:] = jnp.ones((vv_s.shape[0], 128), BF16)
        gw_s[S:2 * S, :] = gw_ref[...]
        gt_s[S:2 * S, :] = gt_ref[...]
        xt_s[...] = x_ref[...].T
        cur[0] = jnp.zeros(cur.shape[1:], F32)

        @pl.when(jnp.logical_not(has))
        def _():
            gw_s[far, :] = jnp.zeros((S, W), BF16)
            gt_s[far, :] = jnp.zeros((S, 128), BF16)
        for c in early:
            c.wait()

    def core(k):
        if k < 5:
            own_half(k).wait()
        sc.core(k)
        if k + 2 < 5:
            own_half(k + 2).start()

    def own_pairs(j):
        def one(i, _):
            back_own(S, span, win, heads, i, bias_ref, q_ref, k_ref, v_ref, gw_s, gt_s, mask_s, t_s, w_s, gs_s, p_s, vv_s, gkt_s, gvt_s, gq_s, cur.at[0])
            return 0

        lax.fori_loop(2 * j, 2 * j + 2, one, 0)

    def rim_pairs(j):
        def one(i, _):
            back_rim(S, span, heads, i, bias_ref, q_ref, k_ref, v_ref, gw_s, gt_s, maskr_s, t_s, w_s, gs_s, vv_s, gkt_s, gvt_s)
            return 0

        lax.fori_loop(2 * j, 2 * j + 2, one, 0)

    def project(l):
        if l == 0:
            for c in late[:2]:
                c.wait()

        def one(i, _):
            def at(t):
                return pl.ds(pl.multiple_of(l * W + t * wide + (i - wide // 128 * l) * 128, 128), 128)

            lanes = pl.ds(pl.multiple_of(i * 128, 128), 128)
            gp_s[:, at(0)] = phi_back(gq_s[:, lanes], q_ref[S:2 * S, lanes], zq_ref[:, lanes], dm_s[0, i], dm_s[1, i], on, scale).astype(BF16)
            gp_s[:, at(1)] = phi_back(gkt_s[i].T, k_ref[S:2 * S, lanes], zk_ref[:, lanes], dm_s[0, i], dm_s[1, i], on, scale).astype(BF16)
            gp_s[:, at(2)] = gvt_s[i].T.astype(BF16)
            return 0

        lax.fori_loop(wide // 128 * l, wide // 128 * (l + 1), one, 0)
        cs = slice(l * W, (l + 1) * W)
        sums = jnp.sum(gp_s[:, cs].astype(F32), 0, keepdims=True)
        extra = jnp.concatenate([sums, vg_ref[8 * l + 1:8 * l + 8, :]], 0)
        part = dot(xt_s[...], gp_s[:, cs]).reshape(n_dev, f, W)
        part = jnp.concatenate([part, jnp.broadcast_to(extra[None], (n_dev,) + extra.shape)], 1)
        PQ[l] = part.astype(BF16).reshape(n_seq // 2, 2, 2, SLAB, W)

    def tokens_back(_):
        residual.wait()
        late[2].wait()
        gx_ref[...] += dot(gp_s[:, :W], w_ref[0], NT) + dot(gp_s[:, W:2 * W], w_ref[1], NT) + dot(gp_s[:, 2 * W:], w_ref[2], NT)

    def done(k):
        total = sc.finish(k)
        if k < 2:
            gdown_ref[2 * f * k:2 * f * (k + 1), :] = total
        elif k < 4:
            for j in range(2):
                gup_ref[:, (2 * (k - 2) + j) * W:(2 * (k - 2) + j + 1) * W] = total[j * f:(j + 1) * f]
        elif k == 4:
            gout_ref[...] = total[:f]
        else:
            l = k - 5
            for t in range(3):
                gqkv_ref[:, t * W + l * wide:t * W + (l + 1) * wide] = total[:f, t * wide:(t + 1) * wide]
            ex_s[8 * l:8 * l + 8, :] = total[f:]

    va = SumAll(p, cur, got, vsnd, vrcv)
    n = SumAll.steps(p.Z)

    def sum_step(i):
        if i:
            va.step(i - 1)
        if i < n:
            va.start(i)

    play(BACKWARD, dict(b=sc.begin, c=core, o=sc.one, t=sc.two, f=done, pre=prepare, pr=own_pairs, ri=rim_pairs, H=send_halo, hw=take_halo, pj=project, gx=tokens_back, v=sum_step))
    rel_ref[...] = cur[n][:rel_ref.shape[0]]

    def mine(row, share):
        width = row.shape[1]
        return pltpu.roll(jnp.broadcast_to(row, (8, width)), lax.rem(width - share * p.me, width), 1)[:1, :128]

    ex = ex_s[...]
    small_ref[0:1, :] = mine(jnp.concatenate([ex[8 * l:8 * l + 1, t * wide:(t + 1) * wide] for t in range(3) for l in range(3)], 1), 3 * f)
    small_ref[1:2, :] = mine(jnp.concatenate([ex[k:k + 1] for k in range(1, 5)], 1), 4 * f)
    singles = jnp.concatenate([ex[5:8], ex[9:12], jnp.zeros((2, W), F32)], 0)
    small_ref[2:8, :] = pltpu.roll(singles, lax.rem(W - f * p.me, W), 1)[:6, :128]
    sc.drain()
    for c in out_near:
        c.wait_send()

    @pl.when(has)
    def _():
        for c in out_far:
            c.wait_send()


def backward(n_seq, x, pk, bias, draws, lens, w, q, k, v, vg, zq, zk, gw, gt, g1, P_):
    S, W = x.shape
    KS = k.shape[0]
    heads, win = bias.shape
    feats, dims = draws.shape[1:]
    span = win + SB
    Z = n_seq // 4
    n_pair = W // 128
    f = W // (2 * n_seq)
    first = 8 * f + SLAB
    R = first + 3 * SLAB
    where = tuple((2 * f * k, 2 * f) for k in range(4)) + ((8 * f, SLAB),) + tuple((first + SLAB * l, SLAB) for l in range(3))
    chunks = tuple(w + (h,) for w, h in zip(where, CUT_BACKWARD))
    V = pltpu.VMEM
    hbm = pl.BlockSpec(memory_space=pl.ANY)
    n = SumAll.steps(Z)
    K = len(chunks)
    sd = jax.ShapeDtypeStruct
    return pl.pallas_call(
        functools.partial(backward_kernel, n_seq, chunks, dims ** -0.25),
        out_shape=(sd((S, W), F32), sd((heads, win), F32), sd((f, 3 * W), F32), sd((f, 4 * W), F32), sd((4 * f, W), F32), sd((f, W), F32), sd((8, 128), F32)),
        in_specs=vmem(4) + [pl.BlockSpec(memory_space=pltpu.SMEM)] + vmem(3) + [hbm] * 8, out_specs=tuple(vmem(7)),
        scratch_shapes=[V(a.shape, a.dtype) for a in (w, q, k, v, zq, zk)] + [
            V((2, 2 * Z, 2, 2 * f, W), BF16), V((3, 2 * Z, 2, 2, SLAB, W), BF16)] + Scatter.buffers(Z, R, W) + [
            V((S, span), F32), V((2, S, S), F32), V((2 * SB, span), F32), V((2 * SB, span), BF16), V((2 * SB, span), BF16), V((2 * SB, span), F32),
            V((KS, 256), BF16), V((n_pair, 128, S), F32), V((n_pair, 128, S), F32), V((S, W), F32), V((KS, W), BF16), V((KS, 128), BF16),
            V((S, 3 * W), BF16), V((W, S), BF16),
            V((2, heads // 2, 2 * feats, 2 * dims), BF16), V((24, W), F32), V((n + 1, 16, win), F32), V((n, 16, win), F32),
            dma(K, Scatter.sems(Z)), dma(K, Scatter.sems(Z)), dma(4), dma(4), dma(n), dma(n), dma(9)],
        compiler_params=pltpu.CompilerParams(collective_id=3, has_side_effects=True, vmem_limit_bytes=64 << 20),
        name="backward",
    )(x, pk, bias, draws, lens, vg, gw, gt, w, q, k, v, zq, zk, g1, P_)


def finish_kernel(n, small_ref, *refs):
    for src, dst in zip(refs[:2], refs[n:n + 2]):
        dst[...] = src[...]

    @pl.when(pl.program_id(0) == 0)
    def _():
        for src, dst in zip(refs[2:n], refs[n + 2:2 * n]):
            dst[...] = src[...]
        for i, v in enumerate(refs[2 * n:]):
            v[...] = small_ref[i:i + 1, :v.shape[1]]


def finish(f, small, *large):
    sd = jax.ShapeDtypeStruct
    steps = 4

    def whole(shape):
        return pl.BlockSpec(shape, lambda i: (0, 0))

    specs = [pl.BlockSpec((a.shape[0] // steps, a.shape[1]), lambda i: (i, 0)) for a in large[:2]] + [whole(a.shape) for a in large[2:]]
    vectors = [(1, n) for n in (3 * f, 4 * f) + (f,) * 6]
    return pl.pallas_call(
        functools.partial(finish_kernel, len(large)),
        grid=(steps,),
        out_shape=tuple(sd(a.shape, a.dtype) for a in large) + tuple(sd(v, F32) for v in vectors),
        in_specs=[whole(small.shape)] + specs,
        out_specs=tuple(specs) + tuple(whole(v) for v in vectors),
        name="finish",
    )(small, *large)


EPS = 1e-06
EXACT_MATMUL = lax.Precision.HIGHEST


def padded_2(cells, sides, width):
    for axis, dim in sides:
        count = lax.axis_size(axis)
        ends = count - 1
        head = lax.slice_in_dim(cells, 0, width, axis=dim)
        tail = lax.slice_in_dim(cells, cells.shape[dim] - width, cells.shape[dim], axis=dim)
        cells = jnp.concatenate(
            [
                lax.ppermute(tail, axis, [(i, (i + 1) % count) for i in range(ends)]),
                cells,
                lax.ppermute(head, axis, [((i + 1) % count, i) for i in range(ends)]),
            ],
            axis=dim,
        )
    return cells


def passed_along(block, axis, distance):
    devices = range(lax.axis_size(axis))
    route = [(i - distance, i) for i in devices if i - distance in devices]
    return lax.ppermute(block, axis, route)


def layer_norm(values, gain, shift):
    center = values - jnp.mean(values, -1, keepdims=True)
    spread = jnp.mean(center * center, -1, keepdims=True)
    return center * lax.rsqrt(spread + EPS) * gain + shift


def feature_map(heads_in, random_features):
    scaled_input = heads_in * heads_in.shape[-1] ** (-0.25)
    projected_rows = jnp.einsum(
        "ykb,kib->yki", scaled_input, random_features, precision=EXACT_MATMUL
    )
    half_square = 0.5 * jnp.sum(scaled_input * scaled_input, -1, keepdims=True)
    return jnp.exp(projected_rows - half_square) * random_features.shape[1] ** (-0.5)


def document_numbers(positions, lengths_row):
    ends = jnp.cumsum(lengths_row)
    counted = jnp.sum((positions[:, None] >= ends[None, :]).astype(jnp.int32), -1)
    return jnp.where(positions < 0, -1, counted)


def fits(n_seq, n_row, f, tokens_here, half_win):
    return n_row == 2 and n_seq == 4 * 4 and f + 8 == SLAB and tokens_here == half_win


def with_kernels(tokens, cotangent, lengths, padding, feature_draws, rel_bias, *weights):
    w_qkv, b_qkv, w_out, b_out, gain_a, shift_a, w_up, b_up, w_down, b_down, gain_f, shift_f = weights
    local = tokens[0]
    W = local.shape[1]
    n_seq = lax.axis_size("seq")
    f = w_out.shape[0]
    vectors = [v[None] for v in (b_qkv, b_up, b_out, gain_a, shift_a, b_down, gain_f, shift_f)]
    (qkv_w, out_w, up_w, zq, zk, q, k, v, att, inv, vec, pk, col) = forward(
        n_seq, w_qkv, w_out, w_up, w_down, vectors, local, padding, rel_bias, feature_draws, lengths)
    out, g1, gw, gt, vg, P_ = middle(n_seq, rel_bias.shape[0], col, local, cotangent[0], att, inv, out_w, up_w, vec)
    P_ = P_.reshape(n_seq // 2, 2, 2, P_.shape[1], W)
    gx, rel, g_qkv, g_up, g_down, g_out, small = backward(
        n_seq, local, pk, rel_bias, feature_draws, lengths, qkv_w, q, k, v, vg, zq, zk, gw, gt, g1, P_)
    out, gx, rel, g_qkv, g_up, g_down, g_out, *vec = finish(f, small, out, gx, rel, g_qkv, g_up, g_down, g_out)
    vec = [v[0] for v in vec]
    return (
        out[None], gx[None], rel, g_qkv, vec[0], g_out, vec[2], vec[3], vec[4], g_up, vec[1], g_down, vec[5], vec[6], vec[7],
    )


def on_device(
    tokens,
    cotangent,
    lengths,
    padding,
    feature_draws,
    rel_bias,
    w_qkv,
    b_qkv,
    w_out,
    b_out,
    gain_attn,
    shift_attn,
    w_up,
    b_up,
    w_down,
    b_down,
    gain_ffn,
    shift_ffn,
):
    if fits(lax.axis_size("seq"), lax.axis_size("row"), w_out.shape[0], tokens.shape[1], rel_bias.shape[1] // 2):
        return with_kernels(
            tokens, cotangent, lengths, padding, feature_draws, rel_bias, w_qkv, b_qkv, w_out, b_out, gain_attn, shift_attn,
            w_up, b_up, w_down, b_down, gain_ffn, shift_ffn,
        )
    local = tokens[0]
    seq_len = local.shape[0]
    model_width = local.shape[1]
    head_count = rel_bias.shape[0]
    window_len = rel_bias.shape[1]
    half_win = window_len // 2
    feat_count = feature_draws.shape[1]
    head_dim = model_width // head_count
    feat_cols = head_count * feat_count
    params = (
        lax.all_gather(w_qkv, ("seq", "row"), axis=0, tiled=True),
        lax.all_gather(b_qkv, ("seq", "row"), axis=0, tiled=True),
        lax.all_gather(w_out, ("seq", "row"), axis=0, tiled=True),
        lax.all_gather(b_out, ("seq", "row"), axis=0, tiled=True),
        lax.all_gather(gain_attn, ("seq", "row"), axis=0, tiled=True),
        lax.all_gather(shift_attn, ("seq", "row"), axis=0, tiled=True),
        lax.all_gather(w_up, ("seq", "row"), axis=0, tiled=True),
        lax.all_gather(b_up, ("seq", "row"), axis=0, tiled=True),
        lax.all_gather(w_down, ("seq", "row"), axis=0, tiled=True),
        lax.all_gather(b_down, ("seq", "row"), axis=0, tiled=True),
        lax.all_gather(gain_ffn, ("seq", "row"), axis=0, tiled=True),
        lax.all_gather(shift_ffn, ("seq", "row"), axis=0, tiled=True),
    )
    (
        qkv_w,
        qkv_b,
        out_w,
        out_b,
        first_norm_gain,
        shift_one,
        up_w,
        up_b,
        down_w,
        down_b,
        gain_two,
        shift_two,
    ) = params
    seq_pos = lax.axis_index("seq")
    start_pos = seq_pos * seq_len
    positions = start_pos + jnp.arange(seq_len, dtype=jnp.int32)
    ext_pos = start_pos - half_win + jnp.arange(seq_len + window_len, dtype=jnp.int32)
    doc_query = document_numbers(positions, lengths[0])
    doc_keys = document_numbers(ext_pos, lengths[0])
    pad_local = padding[0]
    pad_ones = jnp.ones((half_win,), jnp.int32)
    pad_keys = jnp.concatenate([pad_ones, pad_local, pad_ones])
    proj_qkv = jnp.dot(local, qkv_w, preferred_element_type=jnp.float32) + qkv_b
    queries = proj_qkv[:, :model_width].reshape(seq_len, head_count, head_dim)
    keys_in = proj_qkv[:, model_width : 2 * model_width].reshape(seq_len, head_count, head_dim)
    q_full, query_back = jax.vjp(partial(feature_map, random_features=feature_draws), queries)
    k_full, key_back = jax.vjp(partial(feature_map, random_features=feature_draws), keys_in)
    q_feat = q_full.astype(jnp.bfloat16)
    k_flat = k_full.astype(jnp.bfloat16).reshape(seq_len, feat_cols)
    values_low = proj_qkv[:, 2 * model_width :].astype(jnp.bfloat16)
    own_keys = jnp.concatenate([k_flat, values_low], 1)
    masked_keys = jnp.concatenate([k_flat * pad_local.astype(jnp.bfloat16)[:, None], values_low], 1)
    rims = padded_2(masked_keys, (("seq", 0),), half_win)
    key_ext = jnp.concatenate([rims[:half_win], own_keys, rims[half_win + seq_len :]], 0)

    dq, dk, pk = doc_query[:, None], doc_keys[None, :], pad_keys[None, :]
    bias8 = bias_rows(rel_bias)
    q_low = q_feat.reshape(seq_len, feat_cols)
    keys_x, vals_x = key_ext[:, :feat_cols], key_ext[:, feat_cols:]
    attended, inv_tot = attn_fwd(dq, dk, pk, bias8, q_low, keys_x, vals_x)
    att_low = attended.astype(jnp.bfloat16)
    branch = jnp.dot(att_low, out_w, preferred_element_type=jnp.float32) + out_b
    resid_one = local.astype(jnp.float32) + branch
    hidden_one, ln_one_back = jax.vjp(
        layer_norm, resid_one, first_norm_gain.astype(jnp.float32), shift_one.astype(jnp.float32)
    )
    hidden_low = hidden_one.astype(jnp.bfloat16)
    inner = jnp.dot(hidden_low, up_w, preferred_element_type=jnp.float32) + up_b
    active, gelu_back = jax.vjp(partial(jax.nn.gelu, approximate=False), inner)
    active_low = active.astype(jnp.bfloat16)
    ffn_out = jnp.dot(active_low, down_w, preferred_element_type=jnp.float32) + down_b
    result, ln_two_back = jax.vjp(
        layer_norm,
        hidden_one + ffn_out,
        gain_two.astype(jnp.float32),
        shift_two.astype(jnp.float32),
    )
    params = (
        lax.all_gather(w_qkv, ("seq", "row"), axis=0, tiled=True),
        lax.all_gather(b_qkv, ("seq", "row"), axis=0, tiled=True),
        lax.all_gather(w_out, ("seq", "row"), axis=0, tiled=True),
        lax.all_gather(b_out, ("seq", "row"), axis=0, tiled=True),
        lax.all_gather(gain_attn, ("seq", "row"), axis=0, tiled=True),
        lax.all_gather(shift_attn, ("seq", "row"), axis=0, tiled=True),
        lax.all_gather(w_up, ("seq", "row"), axis=0, tiled=True),
        lax.all_gather(b_up, ("seq", "row"), axis=0, tiled=True),
        lax.all_gather(w_down, ("seq", "row"), axis=0, tiled=True),
        lax.all_gather(b_down, ("seq", "row"), axis=0, tiled=True),
        lax.all_gather(gain_ffn, ("seq", "row"), axis=0, tiled=True),
        lax.all_gather(shift_ffn, ("seq", "row"), axis=0, tiled=True),
    )
    (
        qkv_w,
        qkv_b,
        out_w,
        out_b,
        first_norm_gain,
        shift_one,
        up_w,
        up_b,
        down_w,
        down_b,
        gain_two,
        shift_two,
    ) = params
    grad_two, grad_gain_two, grad_shift_two = ln_two_back(cotangent[0].astype(jnp.float32))
    grad_two_low = grad_two.astype(jnp.bfloat16)
    grad_down_w = jnp.einsum(
        "ti,tj->ij", active_low, grad_two_low, preferred_element_type=jnp.float32
    )
    grad_down_b = jnp.sum(grad_two_low, 0, dtype=jnp.float32)
    grad_active = jnp.dot(grad_two_low, down_w.T, preferred_element_type=jnp.float32)
    grad_inner_low = gelu_back(grad_active)[0].astype(jnp.bfloat16)
    grad_up_w = jnp.einsum(
        "ti,tj->ij", hidden_low, grad_inner_low, preferred_element_type=jnp.float32
    )
    grad_up_b = jnp.sum(grad_inner_low, 0, dtype=jnp.float32)
    grad_hidden = grad_two + jnp.dot(grad_inner_low, up_w.T, preferred_element_type=jnp.float32)
    grad_one, grad_gain_one, grad_shift_one = ln_one_back(grad_hidden)
    grad_one_low = grad_one.astype(jnp.bfloat16)
    grad_out_w = jnp.einsum("ti,tj->ij", att_low, grad_one_low, preferred_element_type=jnp.float32)
    grad_out_b = jnp.sum(grad_one_low, 0, dtype=jnp.float32)
    grad_att = jnp.dot(grad_one_low, out_w.T, preferred_element_type=jnp.float32)
    grad_fq_all, grad_kf, grad_vv, grad_b8 = attn_bwd(
        dq, dk, pk, bias8, q_low, keys_x, vals_x, attended, inv_tot, grad_att
    )
    grad_bias = grad_b8.reshape(head_count // 2, 8, window_len)[:, :2].reshape(head_count, window_len)
    lower_rim = jnp.concatenate([grad_kf[:half_win], grad_vv[:half_win]], 1)
    upper_rim = jnp.concatenate([grad_kf[half_win + seq_len :], grad_vv[half_win + seq_len :]], 1)
    from_right = passed_along(lower_rim.astype(jnp.bfloat16), "seq", -1).astype(lower_rim.dtype)
    from_left = passed_along(upper_rim.astype(jnp.bfloat16), "seq", 1).astype(upper_rim.dtype)
    returned = from_left + from_right
    pad_float = pad_local.astype(jnp.float32)[:, None]
    grad_kfeat = grad_kf[half_win : half_win + seq_len] + returned[:, :feat_cols] * pad_float
    value_gradient = grad_vv[half_win : half_win + seq_len] + returned[:, feat_cols:]
    grad_queries = query_back(grad_fq_all.reshape(seq_len, head_count, feat_count))[0]
    grad_keys_in = key_back(grad_kfeat.reshape(seq_len, head_count, feat_count))[0]
    grad_proj_low = jnp.concatenate(
        [
            grad_queries.reshape(seq_len, model_width),
            grad_keys_in.reshape(seq_len, model_width),
            value_gradient,
        ],
        1,
    ).astype(jnp.bfloat16)
    grad_qkv_w = jnp.einsum("ti,tj->ij", local, grad_proj_low, preferred_element_type=jnp.float32)
    grad_qkv_b = jnp.sum(grad_proj_low, 0, dtype=jnp.float32)
    grad_input = grad_one + jnp.dot(grad_proj_low, qkv_w.T, preferred_element_type=jnp.float32)
    grad_rel = lax.psum(grad_bias, ("seq", "row"))
    summed = (
        lax.psum_scatter(grad_qkv_w, ("seq", "row"), scatter_dimension=0, tiled=True),
        lax.psum_scatter(grad_qkv_b, ("seq", "row"), scatter_dimension=0, tiled=True),
        lax.psum_scatter(grad_out_w, ("seq", "row"), scatter_dimension=0, tiled=True),
        lax.psum_scatter(grad_out_b, ("seq", "row"), scatter_dimension=0, tiled=True),
        lax.psum_scatter(grad_gain_one, ("seq", "row"), scatter_dimension=0, tiled=True),
        lax.psum_scatter(grad_shift_one, ("seq", "row"), scatter_dimension=0, tiled=True),
        lax.psum_scatter(grad_up_w, ("seq", "row"), scatter_dimension=0, tiled=True),
        lax.psum_scatter(grad_up_b, ("seq", "row"), scatter_dimension=0, tiled=True),
        lax.psum_scatter(grad_down_w, ("seq", "row"), scatter_dimension=0, tiled=True),
        lax.psum_scatter(grad_down_b, ("seq", "row"), scatter_dimension=0, tiled=True),
        lax.psum_scatter(grad_gain_two, ("seq", "row"), scatter_dimension=0, tiled=True),
        lax.psum_scatter(grad_shift_two, ("seq", "row"), scatter_dimension=0, tiled=True),
    )
    return (
        result[None].astype(jnp.bfloat16),
        grad_input[None],
        grad_rel,
        summed[0],
        summed[1],
        summed[2],
        summed[3],
        summed[4],
        summed[5],
        summed[6],
        summed[7],
        summed[8],
        summed[9],
        summed[10],
        summed[11],
    )


def solution(mesh):
    in_specs = (
        P("row", "seq", None),
        P("row", "seq", None),
        P("row", None),
        P("row", "seq"),
        P(),
        P(),
        P(("seq", "row"), None),
        P(("seq", "row")),
        P(("seq", "row"), None),
        P(("seq", "row")),
        P(("seq", "row")),
        P(("seq", "row")),
        P(("seq", "row"), None),
        P(("seq", "row")),
        P(("seq", "row"), None),
        P(("seq", "row")),
        P(("seq", "row")),
        P(("seq", "row")),
    )
    out_specs = (
        P("row", "seq", None),
        P("row", "seq", None),
        P(),
        P(("seq", "row"), None),
        P(("seq", "row")),
        P(("seq", "row"), None),
        P(("seq", "row")),
        P(("seq", "row")),
        P(("seq", "row")),
        P(("seq", "row"), None),
        P(("seq", "row")),
        P(("seq", "row"), None),
        P(("seq", "row")),
        P(("seq", "row")),
        P(("seq", "row")),
    )
    return jax.shard_map(
        on_device, mesh=mesh, in_specs=in_specs, out_specs=out_specs, check_vma=False
    )
```
